128 devices in a mesh: grp: 8 (over x, core), mem: 16 (over z, y).
Axes of the slice: x: 4, y: 4, z: 4, core: 2. Of those that a mesh axis runs over, the one named last changes fastest.
Arguments:
- embeddings: bfloat16 [65536, 768], P(('grp', 'mem')), may hold values from -6 to 6
- initial_centroids: bfloat16 [104, 100, 768], P('grp'), may hold values from -6 to 6
- row_owner: int32 [65536, 1], P(('grp', 'mem')), may hold values from 0 to 127; in each aligned block of 512 rows (0 to 511, 512 to 1023, ...) at most 12 rows name the same one
- prefix_offset: int32 [65536], P(('grp', 'mem')), may hold values from 0 to 12
- first_assign: int32 [65536], P(('grp', 'mem')), may hold values from 0 to 99
- second_assign: int32 [65536], P(('grp', 'mem')), may hold values from 0 to 99
Outputs:
- distances: float32 [100, 65536], P(None, ('grp', 'mem'))
- first_distance: float32 [65536], P(('grp', 'mem'))
The draws below stay inside these ranges and needn't reach their ends.
Inputs may be any that keep to these rules, and one draw needn't show every extreme that they name: `row_owner`: owners are numbered grp index times 16 plus mem index. At most 12 passages of one device have the same owner, and in every draw some owner has exactly 12 passages of some device.
All inputs are finite; a program needn't handle non-finite values.
Results may differ from the reference program's by a relative error of at most 0.00035.
Values may be sent and summed in bfloat16 or wider, within the bound.
No kernel may reach another device: no remote copies, remote signals or barrier semaphores. Data moves between devices by JAX's collectives and lax.ppermute only.
A program may use at most 128 MiB of HBM per device.

```python
import math
import jax
import jax.numpy as jnp
import numpy as np
from jax import lax

D = 768
K2 = 100
CODES_GRP = 13
PRIOR = 16
ROWS_DEV = 512
K1 = 104
ROWS = 65536
CAP = 12
N_MEM = 16
DEVICES = 128


def with_ends(values, own_key, smallest, largest):
    shape = values.shape
    place = [jax.random.randint(jax.random.fold_in(own_key, axis), (), 0, shape[axis]) for axis in range(len(shape))]
    values = values.at[tuple(place)].set(smallest)
    longest = shape.index(max(shape))
    place[longest] = (place[longest] + 1) % shape[longest]
    return values.at[tuple(place)].set(largest)


def levels(rng, dims, cuts, low, largest):
    loudness = 1.0
    for dim, shards_of in cuts:
        draws = jax.random.uniform(jax.random.fold_in(jax.random.fold_in(rng, 6), dim), (shards_of,), jnp.float32, low / len(cuts), largest / len(cuts))
        loudness = loudness * jnp.repeat(jnp.exp(draws), dims[dim] // shards_of).reshape((-1,) + (1,) * (len(dims) - 1 - dim))
    return loudness


def deal_out(key, own, number, rows, amount, top, most, skew):
    sequence = jax.random.permutation(key, amount)
    crowded, ordinary = load_shares(amount, rows * top, most, skew, True), load_shares(amount, rows * top, most, skew, False)
    places = jnp.arange(amount)

    def named(lengths, rotation):
        used = int((lengths > 0).sum())
        fixed = max(1, used // 4)
        moved = fixed + (places - fixed + rotation * (used - fixed)) % max(1, amount - fixed)
        return jnp.zeros((amount,), jnp.int32).at[sequence[jnp.where(places < fixed, places, moved)]].set(jnp.asarray(lengths, jnp.int32))

    lengths = jnp.where(number % 4 == 0, named(crowded, number // 4), named(ordinary, number - number // 4 - 1))
    mixed = jax.random.permutation(jax.random.fold_in(own, 3), amount)
    giver, sink = mixed[0:amount // 2 * 2:2], mixed[1:amount // 2 * 2:2]
    slack = jnp.minimum(lengths[giver] - 1, most - lengths[sink]) // 2
    slack = jnp.where((giver == sequence[0]) | (sink == sequence[0]) | (lengths[sink] == 0), 0, jnp.maximum(slack, 0))
    moved = jax.random.randint(jax.random.fold_in(own, 4), (amount // 2,), 0, 1 << 20) % (slack + 1)
    lengths = lengths.at[giver].add(-moved).at[sink].add(moved)
    members = jnp.searchsorted(jnp.cumsum(lengths), jnp.arange(rows * top), side="right").astype(jnp.int32)
    grid = members.reshape(top, rows).T
    grid = grid[jax.random.permutation(jax.random.fold_in(own, 1), rows)]
    rotation = jax.random.randint(jax.random.fold_in(own, 2), (rows, 1), 0, top)
    return jnp.take_along_axis(grid, (jnp.arange(top)[None, :] + rotation) % top, axis=1)


def load_shares(number_of, total, bound, lean, full):
    portions = [(1 << 20) // math.isqrt(rank ** lean) + 1 for rank in range(1, number_of + 1)]
    largest = bound if full else min(bound, max(-(-total // number_of), total * portions[0] // sum(portions)))
    least = 1 if total - largest >= number_of - 1 else 0
    holding, rest = [largest] + [least] * (number_of - 1), total - largest - least * (number_of - 1)
    while rest > 0:
        candidates = [i for i in range(1, number_of) if holding[i] < largest] or [i for i in range(1, number_of) if holding[i] < bound]
        whole, budget = sum([portions[i] for i in candidates]), rest
        for i in candidates:
            addition = min(bound - holding[i], max(1, budget * portions[i] // whole), rest)
            holding[i] = holding[i] + addition
            rest = rest - addition
    return np.array(holding)


def bell_draw(key, dims, spread, limit, shards=(), dtype=jnp.bfloat16):
    gain = levels(key, dims, shards, -0.22, 0.18) if shards else 1.0
    drawn = jax.random.normal(key, dims, jnp.float32) * spread * gain
    return jnp.minimum(jnp.maximum(drawn, -limit), limit).astype(dtype)


def setup_inputs(seed: int = 0) -> dict:
    splits = jax.random.split(jax.random.key(seed), 7)
    embeddings = bell_draw(splits[0], (ROWS, D), 1.0, 6.0, ((0, 128),))
    initial_centroids = bell_draw(splits[1], (K1, K2, D), 1.0, 6.0, ((0, 8),))
    row_owner_keys = jax.random.split(jax.random.fold_in(splits[2], 1), ROWS // ROWS_DEV)
    row_owner_turns = jax.random.permutation(jax.random.fold_in(splits[2], 3), ROWS // ROWS_DEV)
    row_owner = jax.vmap(lambda own, number: deal_out(jax.random.fold_in(splits[2], 2), own, number, ROWS_DEV, DEVICES, 1, CAP, 2))(row_owner_keys, row_owner_turns).reshape((ROWS, 1))
    prefix_offset = with_ends(jax.random.randint(splits[3], (ROWS,), 0, CODES_GRP), jax.random.fold_in(splits[3], 1), 0, CODES_GRP - 1).astype(jnp.int32)
    first_assign = with_ends(jax.random.randint(splits[4], (ROWS,), 0, K2), jax.random.fold_in(splits[4], 1), 0, K2 - 1).astype(jnp.int32)
    second_assign = with_ends(jax.random.randint(splits[5], (ROWS,), 0, K2), jax.random.fold_in(splits[5], 1), 0, K2 - 1).astype(jnp.int32)
    return dict(embeddings=embeddings, initial_centroids=initial_centroids, row_owner=row_owner, prefix_offset=prefix_offset, first_assign=first_assign, second_assign=second_assign)


def cluster_update(features, cluster_ids, previous, total_clusters):
    sums = jax.ops.segment_sum(features, cluster_ids, num_segments=total_clusters)
    counts = jax.ops.segment_sum(jnp.ones(cluster_ids.shape, jnp.float32), cluster_ids, num_segments=total_clusters)
    return (sums + PRIOR * previous) / (counts[:, None] + PRIOR)


def reference(embeddings, initial_centroids, row_owner, prefix_offset, first_assign, second_assign):
    total_clusters = K1 * K2
    target = row_owner[:, 0]
    first_code = ((target // N_MEM) * CODES_GRP + prefix_offset).astype(jnp.int32)
    features = embeddings.astype(jnp.float32)
    squares = jnp.sum(features * features, axis=1)
    previous = initial_centroids.astype(jnp.float32).reshape(total_clusters, D)
    ids_one = (first_code * K2 + first_assign).astype(jnp.int32)
    centre_one = cluster_update(features, ids_one, previous, total_clusters)
    rounded_one = lax.optimization_barrier(centre_one.astype(jnp.bfloat16)).astype(jnp.float32)
    assigned = jnp.take(rounded_one, ids_one, axis=0)
    first_distance = (squares - 2.0 * jnp.sum(features * assigned, axis=1) + jnp.sum(assigned * assigned, axis=1)) / D
    ids_two = (first_code * K2 + second_assign).astype(jnp.int32)
    centre_two = cluster_update(features, ids_two, centre_one, total_clusters)
    rounded_two = lax.optimization_barrier(centre_two.astype(jnp.bfloat16)).astype(jnp.float32).reshape(K1, K2, D)
    centre_squares = jnp.sum(rounded_two * rounded_two, axis=2)
    block_rows = 256 if ROWS % 256 == 0 else ROWS

    def one_block(pieces):
        block_x, block_code, block_sq = pieces
        nearby = jnp.take(rounded_two, block_code, axis=0)
        inner = jnp.einsum("rd,rkd->rk", block_x, nearby)
        return (block_sq[:, None] - 2.0 * inner + jnp.take(centre_squares, block_code, axis=0)) / D

    scored = lax.map(one_block, (features.reshape(-1, block_rows, D), first_code.reshape(-1, block_rows), squares.reshape(-1, block_rows)))
    distances = scored.reshape(ROWS, K2).T
    return distances, first_distance
```

```python
import jax
import jax.numpy as jnp
from jax import lax
from jax.experimental import pallas as pl
from jax.experimental.pallas import tpu as pltpu
from jax.sharding import PartitionSpec as P

PRIOR = 16
SLOTS_GROUP = 128
SLOTS_CODE = 96
LANES = 128
OFFSET, FIRST, SECOND, LIVE, FULL = 0, 1, 2, 3, 4
NT = (((1,), (1,)), ((), ()))
VMEM_LIMIT = 48 * 1024 * 1024


def iota(shape, dim):
    return lax.broadcasted_iota(jnp.int32, shape, dim)


def hot(condition):
    return jnp.where(condition, 1.0, 0.0).astype(jnp.bfloat16)


def dot(a, b):
    return jnp.dot(a, b, preferred_element_type=jnp.float32)


def dot_nt(a, b):
    return lax.dot_general(a, b, NT, preferred_element_type=jnp.float32)


def three_terms(values):
    high = values.astype(jnp.bfloat16)
    rest = values - high.astype(jnp.float32)
    middle = rest.astype(jnp.bfloat16)
    low = (rest - middle.astype(jnp.float32)).astype(jnp.bfloat16)
    return high, middle, low


def call(kernel, out_shape, args, out_memory=None):
    count = len(args)
    in_specs = [pl.BlockSpec(memory_space=pltpu.VMEM)] * count
    out_specs = out_memory or [pl.BlockSpec(memory_space=pltpu.VMEM)] * len(out_shape)
    return pl.pallas_call(
        kernel,
        out_shape=out_shape,
        in_specs=in_specs,
        out_specs=out_specs,
        compiler_params=pltpu.CompilerParams(vmem_limit_bytes=VMEM_LIMIT),
    )(*args)


def pack_kernel(member_count, owner_ref, offset_ref, first_ref, second_ref, x_ref, send_ref, slot_ref):
    rows, feat = x_ref.shape
    groups = send_ref.shape[0] // SLOTS_GROUP
    group = owner_ref[...] // member_count
    member = iota((16, rows), 0) == group
    hot_group = hot(member)
    before = hot(iota((rows, rows), 0) < iota((rows, rows), 1))
    rank = jnp.sum(jnp.where(member, dot(hot_group, before), 0.0), axis=0, keepdims=True)
    rank = rank.astype(jnp.int32)
    fits = rank < SLOTS_GROUP
    full = jnp.max(jnp.where(fits, 0.0, 1.0))
    slot = jnp.where(fits, group * SLOTS_GROUP + rank, -1)
    slot_ref[...] = slot
    kind = iota((LANES, rows), 0)
    labels = jnp.where(kind == OFFSET, offset_ref[...], 0)
    labels = jnp.where(kind == FIRST, first_ref[...], labels)
    labels = jnp.where(kind == SECOND, second_ref[...], labels)
    labels = jnp.where(kind == LIVE, 1, labels)
    labels = labels.astype(jnp.float32).astype(jnp.bfloat16)
    full_column = jnp.where(iota((SLOTS_GROUP, LANES), 1) == FULL, full, 0.0)
    x = x_ref[...]
    for block in range(groups):
        begin = block * SLOTS_GROUP
        place = hot(iota((SLOTS_GROUP, rows), 0) + begin == slot)
        send_ref[begin : begin + SLOTS_GROUP, :feat] = dot(place, x).astype(jnp.bfloat16)
        send_ref[begin : begin + SLOTS_GROUP, feat:] = (dot_nt(place, labels) + full_column).astype(
            jnp.bfloat16
        )


def relay_kernel(got_ref, send_ref, place_ref):
    total, width = got_ref.shape
    feat = width - LANES
    labels = got_ref[:, feat:]
    columns = labels.astype(jnp.float32)
    full = jnp.max(jnp.where(iota((total, LANES), 1) == FULL, columns, 0.0))
    turn = hot(iota((16, LANES), 0) == iota((16, LANES), 1))
    across = dot_nt(turn, labels)
    lane_code = across[OFFSET : OFFSET + 1]
    lane_live = across[LIVE : LIVE + 1] > 0.5
    member = (iota((16, total), 0).astype(jnp.float32) == lane_code) & lane_live
    hot_code = hot(member)
    before = hot(iota((LANES, LANES), 0) < iota((LANES, LANES), 1))
    base = jnp.zeros((16, 1), jnp.float32)
    ranks = []
    for begin in range(0, total, LANES):
        piece = hot_code[:, begin : begin + LANES]
        ranks.append(dot(piece, before) + base)
        base = base + jnp.sum(piece.astype(jnp.float32), axis=1, keepdims=True)
    rank = jnp.concatenate(ranks, axis=1)
    rank = jnp.sum(jnp.where(member, rank, 0.0), axis=0, keepdims=True)
    fits = rank < SLOTS_CODE
    full = jnp.maximum(full, jnp.max(jnp.where(lane_live & ~fits, 1.0, 0.0)))
    place = jnp.where(lane_live & fits, lane_code * SLOTS_CODE + rank, -1.0).astype(jnp.int32)
    column_member = (iota((total, LANES), 1).astype(jnp.float32) == columns[:, OFFSET : OFFSET + 1]) & (
        columns[:, LIVE : LIVE + 1] > 0.5
    )
    column_hot = hot(column_member)
    after = hot(iota((LANES, LANES), 0) > iota((LANES, LANES), 1))
    base = jnp.zeros((1, LANES), jnp.float32)
    for begin in range(0, total, LANES):
        piece = column_hot[begin : begin + LANES]
        counted = dot(after, piece) + base
        base = base + jnp.sum(piece.astype(jnp.float32), axis=0, keepdims=True)
        chosen = column_member[begin : begin + LANES]
        own = jnp.sum(jnp.where(chosen, counted, 0.0), axis=1, keepdims=True)
        live = columns[begin : begin + LANES, LIVE : LIVE + 1] > 0.5
        code = columns[begin : begin + LANES, OFFSET : OFFSET + 1]
        own = jnp.where(live & (own < SLOTS_CODE), code * SLOTS_CODE + own, -1.0)
        place_ref[begin : begin + LANES, :] = own.astype(jnp.int32)
    got = got_ref[...]
    is_full = iota((SLOTS_CODE, LANES), 1) == FULL
    blocks = send_ref.shape[0] // SLOTS_CODE
    for block in range(blocks):
        begin = block * SLOTS_CODE
        chosen = hot(iota((SLOTS_CODE, total), 0) + begin == place)
        moved = dot(chosen, got)
        send_ref[begin : begin + SLOTS_CODE, :feat] = moved[:, :feat].astype(jnp.bfloat16)
        send_ref[begin : begin + SLOTS_CODE, feat:] = jnp.where(is_full, full, moved[:, feat:]).astype(
            jnp.bfloat16
        )


def code_kernel(got_ref, start_ref, out_ref, start):
    total, width = got_ref.shape
    feat = width - LANES
    codes_two = start_ref.shape[0]
    start[...] = jnp.zeros_like(start)
    start[0:codes_two, :] = start_ref[...].astype(jnp.float32)
    x = got_ref[:, :feat]
    labels = got_ref[:, feat:]
    columns = labels.astype(jnp.float32)
    lane = iota((total, LANES), 1)
    full = jnp.max(jnp.where(lane == FULL, columns, 0.0))
    turn = hot(iota((16, LANES), 0) == iota((16, LANES), 1))
    across = dot_nt(turn, labels)
    live = across[LIVE : LIVE + 1] > 0.5
    cluster = iota((LANES, total), 0).astype(jnp.float32)

    def update(earlier, assigned):
        member = hot((cluster == assigned) & live)
        totals = dot(member, x)
        counts = jnp.sum(member.astype(jnp.float32), axis=1, keepdims=True)
        return (totals + PRIOR * earlier) / (counts + PRIOR)

    diagonal = iota((LANES, LANES), 0) == iota((LANES, LANES), 1)

    def squares_of(rounded):
        wide = rounded.astype(jnp.float32)
        down = jnp.sum(wide * wide, axis=1, keepdims=True)
        return jnp.sum(jnp.where(diagonal, down, 0.0), axis=0, keepdims=True)

    centre_one = update(start[...], across[FIRST : FIRST + 1])
    rounded_one = centre_one.astype(jnp.bfloat16)
    centre_two = update(centre_one, across[SECOND : SECOND + 1])
    rounded_two = centre_two.astype(jnp.bfloat16)
    squares_one = squares_of(rounded_one)
    squares_two = squares_of(rounded_two)
    wide_x = x.astype(jnp.float32)
    squares = jnp.sum(wide_x * wide_x, axis=1, keepdims=True)
    near = (squares - 2.0 * dot_nt(x, rounded_one) + squares_one) / feat
    near = jnp.sum(
        jnp.where(lane.astype(jnp.float32) == columns[:, FIRST : FIRST + 1], near, 0.0),
        axis=1,
        keepdims=True,
    )
    score = (squares - 2.0 * dot_nt(x, rounded_two) + squares_two) / feat
    score = jnp.where(lane == codes_two, near, score)
    out_ref[...] = jnp.where(lane > codes_two, full, score)


def unrelay_kernel(got_ref, place_ref, out_ref):
    total = got_ref.shape[0]
    got = got_ref[...]
    full = jnp.max(got[:, LANES - 1 :])
    terms = jnp.concatenate(three_terms(got), axis=1)
    for begin in range(0, out_ref.shape[0], LANES):
        chosen = hot(iota((LANES, total), 1) == place_ref[begin : begin + LANES, :])
        moved = dot(chosen, terms)
        moved = moved[:, :LANES] + (moved[:, LANES : 2 * LANES] + moved[:, 2 * LANES :])
        out_ref[begin : begin + LANES, :] = jnp.where(iota((LANES, LANES), 1) == LANES - 1, full, moved)


def unpack_kernel(got_ref, slot_ref, all_ref, one_ref, full_ref):
    total = got_ref.shape[0]
    rows = slot_ref.shape[1]
    codes_two = all_ref.shape[0]
    got = got_ref[...]
    full_ref[0, 0] = (jnp.max(got[:, LANES - 1 :]) > 0.5).astype(jnp.int32)
    high, middle, low = three_terms(got.T)
    chosen = hot(iota((total, rows), 0) == slot_ref[...])
    moved = dot(high, chosen) + (dot(middle, chosen) + dot(low, chosen))
    all_ref[...] = moved[:codes_two]
    one_ref[...] = moved[codes_two : codes_two + 1]


def pick_block(total):
    for candidate in range(1024, 0, -1):
        if total % candidate == 0:
            return candidate
    return total


def general(embeddings, initial_centroids, row_owner, prefix_offset, first_assign, second_assign):
    row_count, feat_width = embeddings.shape
    group_codes = initial_centroids.shape[0]
    codes_two = initial_centroids.shape[1]
    clusters = group_codes * codes_two
    group_count = lax.axis_size("grp")
    member_count = lax.axis_size("mem")
    devices_all = group_count * member_count
    capacity = 2 * row_count // devices_all + 4
    slot_total = devices_all * capacity
    target = row_owner[:, 0]
    dest_table = (target[:, None] == jnp.arange(devices_all, dtype=jnp.int32)[None, :]).astype(
        jnp.int32
    )
    slot_rank = jnp.sum(jnp.cumsum(dest_table, axis=0) * dest_table, axis=1) - 1
    slot_index = target * capacity + slot_rank
    send_rows = jnp.zeros((slot_total, feat_width), jnp.bfloat16).at[slot_index].set(embeddings)
    labels = jnp.stack([prefix_offset, first_assign, second_assign], axis=1)
    send_labels = jnp.full((slot_total, 3), -1, jnp.int32).at[slot_index].set(labels)
    got_rows, got_labels = (
        lax.all_to_all(send_rows, ("grp", "mem"), split_axis=0, concat_axis=0, tiled=True),
        lax.all_to_all(send_labels, ("grp", "mem"), split_axis=0, concat_axis=0, tiled=True),
    )
    offsets = got_labels[:, 0]
    live = offsets >= 0
    ids_one = jnp.where(live, offsets * codes_two + got_labels[:, 1], -1)
    ids_two = jnp.where(live, offsets * codes_two + got_labels[:, 2], -1)
    squares = jnp.sum(jnp.square(got_rows.astype(jnp.float32)), axis=1)
    block_rows = pick_block(slot_total)
    block_count = slot_total // block_rows
    row_blocks = got_rows.reshape(block_count, block_rows, feat_width)
    cluster_range = jnp.arange(clusters, dtype=jnp.int32)

    def local_totals(cluster_ids):

        def add_block(carry, pieces):
            totals, counts = carry
            block_x, block_ids = pieces
            hot_table = (block_ids[:, None] == cluster_range[None, :]).astype(jnp.bfloat16)
            totals = totals + lax.dot_general(
                hot_table, block_x, (((0,), (0,)), ((), ())), preferred_element_type=jnp.float32
            )
            counts = counts + jnp.sum(hot_table, axis=0, dtype=jnp.float32)
            return ((totals, counts), None)

        start = (
            jnp.zeros((clusters, feat_width), jnp.float32),
            jnp.zeros((clusters,), jnp.float32),
        )
        result, unused = lax.scan(
            add_block, start, (row_blocks, cluster_ids.reshape(block_count, block_rows))
        )
        return result

    start_table = initial_centroids.reshape(clusters, feat_width).astype(jnp.float32)

    def update(earlier, cluster_ids):
        totals, counts = local_totals(cluster_ids)
        totals, counts = (
            lax.psum(totals.astype(jnp.bfloat16), "mem").astype(jnp.float32),
            lax.psum(counts.astype(jnp.bfloat16), "mem").astype(jnp.float32),
        )
        centre = (totals + PRIOR * earlier) / (counts[:, None] + PRIOR)
        return (centre, centre.astype(jnp.bfloat16))

    centre_one, rounded_one = update(start_table, ids_one)
    assigned = jnp.take(rounded_one, jnp.maximum(ids_one, 0), axis=0).astype(jnp.float32)
    first_local = (
        squares
        - 2.0 * jnp.sum(got_rows.astype(jnp.float32) * assigned, axis=1)
        + jnp.sum(assigned * assigned, axis=1)
    ) / feat_width
    centre_two, rounded_two = update(centre_one, ids_two)
    centre_squares = jnp.sum(jnp.square(rounded_two.astype(jnp.float32)), axis=1).reshape(
        group_codes, codes_two
    )
    code_range = jnp.arange(group_codes, dtype=jnp.int32)

    def score_block(pieces):
        block_x, block_offsets, block_sq = pieces
        raw = lax.dot_general(
            rounded_two, block_x, (((1,), (1,)), ((), ())), preferred_element_type=jnp.float32
        )
        raw = raw.reshape(group_codes, codes_two, block_rows)
        select = (block_offsets[None, :] == code_range[:, None]).astype(jnp.float32)
        inner = jnp.sum(raw * select[:, None, :], axis=0)
        norms = jnp.sum(centre_squares[:, :, None] * select[:, None, :], axis=0)
        return (block_sq[None, :] - 2.0 * inner + norms) / feat_width

    scored = lax.map(
        score_block,
        (
            row_blocks,
            offsets.reshape(block_count, block_rows),
            squares.reshape(block_count, block_rows),
        ),
    )
    all_local = jnp.transpose(scored, (1, 0, 2)).reshape(codes_two, slot_total)
    one_local = first_local[None, :]
    back_all, back_one = (
        lax.all_to_all(all_local, ("grp", "mem"), split_axis=1, concat_axis=1, tiled=True),
        lax.all_to_all(one_local, ("grp", "mem"), split_axis=1, concat_axis=1, tiled=True),
    )
    distances = jnp.take(back_all, slot_index, axis=1)
    first_distance = jnp.take(back_one[0], slot_index, axis=0)
    return (distances, first_distance)


def quick(embeddings, initial_centroids, row_owner, prefix_offset, first_assign, second_assign):
    rows, feat = embeddings.shape
    group_codes, codes_two = initial_centroids.shape[:2]
    groups = lax.axis_size("grp")
    members = lax.axis_size("mem")
    width = feat + LANES
    relay_total = groups * SLOTS_GROUP
    code_total = members * SLOTS_CODE
    shape = jax.ShapeDtypeStruct
    send, slot = call(
        lambda *refs: pack_kernel(members, *refs),
        [shape((relay_total, width), jnp.bfloat16), shape((1, rows), jnp.int32)],
        [
            row_owner.reshape(1, rows),
            prefix_offset.reshape(1, rows),
            first_assign.reshape(1, rows),
            second_assign.reshape(1, rows),
            embeddings,
        ],
    )
    got = lax.all_to_all(
        send.reshape(groups, SLOTS_GROUP, width), "grp", split_axis=0, concat_axis=0, tiled=True
    )
    send, place = call(
        relay_kernel,
        [shape((code_total, width), jnp.bfloat16), shape((relay_total, 1), jnp.int32)],
        [got.reshape(relay_total, width)],
    )
    got = lax.all_to_all(
        send.reshape(members, SLOTS_CODE, width), "mem", split_axis=0, concat_axis=0, tiled=True
    )
    code = jnp.minimum(lax.axis_index("mem"), group_codes - 1)
    start = lax.dynamic_index_in_dim(initial_centroids, code, 0, keepdims=False)
    scored = pl.pallas_call(
        code_kernel,
        out_shape=shape((code_total, LANES), jnp.float32),
        in_specs=[pl.BlockSpec(memory_space=pltpu.VMEM)] * 2,
        out_specs=pl.BlockSpec(memory_space=pltpu.VMEM),
        scratch_shapes=[pltpu.VMEM((LANES, feat), jnp.float32)],
        compiler_params=pltpu.CompilerParams(vmem_limit_bytes=VMEM_LIMIT),
    )(got.reshape(code_total, width), start)
    back = lax.all_to_all(
        scored.reshape(members, SLOTS_CODE, LANES), "mem", split_axis=0, concat_axis=0, tiled=True
    )
    (back,) = call(
        unrelay_kernel,
        [shape((relay_total, LANES), jnp.float32)],
        [back.reshape(code_total, LANES), place],
    )
    back = lax.all_to_all(
        back.reshape(groups, SLOTS_GROUP, LANES), "grp", split_axis=0, concat_axis=0, tiled=True
    )
    return call(
        unpack_kernel,
        [shape((codes_two, rows), jnp.float32), shape((1, rows), jnp.float32), shape((1, 1), jnp.int32)],
        [back.reshape(relay_total, LANES), slot],
        out_memory=[
            pl.BlockSpec(memory_space=pltpu.VMEM),
            pl.BlockSpec(memory_space=pltpu.VMEM),
            pl.BlockSpec(memory_space=pltpu.SMEM),
        ],
    )


def body(*inputs):
    distances, first_distance, full = quick(*inputs)
    return lax.cond(
        full[0, 0] > 0,
        lambda kept, given: general(*given),
        lambda kept, given: kept,
        (distances, first_distance[0]),
        inputs,
    )


def solution(mesh):
    placed = (
        P(("grp", "mem"), None),
        P("grp", None, None),
        P(("grp", "mem"), None),
        P(("grp", "mem")),
        P(("grp", "mem")),
        P(("grp", "mem")),
    )
    return jax.shard_map(
        body,
        mesh=mesh,
        in_specs=placed,
        out_specs=(P(None, ("grp", "mem")), P(("grp", "mem"))),
        check_vma=False,
    )
```

```python
import jax
import jax.numpy as jnp
from jax import lax
from jax.experimental import pallas as pl
from jax.experimental.pallas import tpu as pltpu
from jax.sharding import PartitionSpec as P

PRIOR = 16
BLOCK_RELAY = 72
BLOCK_CODE = 160
LANES = 128
FIRST, SECOND, GROUP = 0, 1, 2
NT = (((1,), (1,)), ((), ()))
VMEM_LIMIT = 48 * 1024 * 1024


def iota(shape, dim):
    return lax.broadcasted_iota(jnp.int32, shape, dim)


def hot(condition):
    return jnp.where(condition, 1.0, 0.0).astype(jnp.bfloat16)


def dot(a, b):
    return jnp.dot(a, b, preferred_element_type=jnp.float32)


def dot_nt(a, b):
    return lax.dot_general(a, b, NT, preferred_element_type=jnp.float32)


def three_terms(values):
    high = values.astype(jnp.bfloat16)
    rest = values - high.astype(jnp.float32)
    middle = rest.astype(jnp.bfloat16)
    low = (rest - middle.astype(jnp.float32)).astype(jnp.bfloat16)
    return high, middle, low


def call(kernel, out_shape, args, out_memory=None, in_memory=None, scratch=()):
    vmem = pl.BlockSpec(memory_space=pltpu.VMEM)
    return pl.pallas_call(
        kernel,
        out_shape=out_shape,
        in_specs=in_memory or [vmem] * len(args),
        out_specs=out_memory or [vmem] * len(out_shape),
        scratch_shapes=scratch,
        compiler_params=pltpu.CompilerParams(vmem_limit_bytes=VMEM_LIMIT),
    )(*args)


def rank_in_bin(member):
    bins = hot(member)
    before = hot(iota((LANES, LANES), 0) < iota((LANES, LANES), 1))
    base = jnp.zeros((member.shape[0], 1), jnp.float32)
    ranks = []
    for begin in range(0, member.shape[1], LANES):
        piece = bins[:, begin : begin + LANES]
        ranks.append(dot(piece, before) + base)
        base = base + jnp.sum(piece.astype(jnp.float32), axis=1, keepdims=True)
    rank = jnp.concatenate(ranks, axis=1)
    return jnp.sum(jnp.where(member, rank, 0.0), axis=0, keepdims=True)


def column_of(row):
    diagonal = iota((LANES, LANES), 0) == iota((LANES, LANES), 1)
    pieces = []
    for begin in range(0, row.shape[1], LANES):
        piece = jnp.where(diagonal, row[:, begin : begin + LANES], 0.0)
        pieces.append(jnp.sum(piece, axis=1, keepdims=True))
    return jnp.concatenate(pieces, axis=0)


def last_row(ref, block, size):
    begin = block * size + size - 8
    return ref[begin : begin + 8, :].astype(jnp.float32)[7:8, :]


def pack_kernel(members, group_codes, owner_ref, offset_ref, first_ref, second_ref, x_ref, send_ref, slot_ref):
    rows, feat = x_ref.shape
    group = owner_ref[...] // members
    relay = (group * group_codes + offset_ref[...]) % members
    rank = rank_in_bin(iota((members, rows), 0) == relay).astype(jnp.int32)
    fits = rank < BLOCK_RELAY - 1
    full = jnp.max(jnp.where(fits, 0.0, 1.0))
    slot_ref[...] = jnp.where(fits, relay * BLOCK_RELAY + rank, -1)
    rank = jnp.where(fits, rank, -1)
    kind = iota((16, rows), 0)
    labels = jnp.where(kind == FIRST, first_ref[...] + 1, 0)
    labels = jnp.where(kind == SECOND, second_ref[...], labels)
    labels = jnp.where(kind == GROUP, group, labels)
    labels = labels.astype(jnp.float32).astype(jnp.bfloat16)
    x = x_ref[...]
    full_row = jnp.full((1, feat - 3 * LANES), full, jnp.float32)
    is_last = iota((BLOCK_RELAY, feat), 0) == BLOCK_RELAY - 1
    for block in range(members):
        begin = block * BLOCK_RELAY
        chosen = hot((iota((LANES, rows), 0) == rank) & (relay == block))
        kinds = dot_nt(labels, chosen)
        last = [kinds[kind : kind + 1] for kind in (FIRST, SECOND, GROUP)] + [full_row]
        last = jnp.concatenate(last, axis=1)
        moved = dot(chosen[:BLOCK_RELAY], x)
        send_ref[begin : begin + BLOCK_RELAY, :] = jnp.where(is_last, last, moved).astype(jnp.bfloat16)


def relay_kernel(got_ref, send_ref, place_ref):
    total, feat = got_ref.shape
    sources = total // BLOCK_RELAY
    groups = send_ref.shape[0] // BLOCK_CODE
    labels = []
    full = jnp.zeros((1, 1), jnp.float32)
    for block in range(sources):
        row = last_row(got_ref, block, BLOCK_RELAY)
        full = jnp.maximum(full, row[:, 3 * LANES : 3 * LANES + 1])
        kinds = [row[:, kind * LANES : kind * LANES + BLOCK_RELAY] for kind in (FIRST, SECOND, GROUP)]
        kinds.append(jnp.zeros((13, BLOCK_RELAY), jnp.float32))
        labels.append(jnp.concatenate(kinds, axis=0))
    labels = jnp.concatenate(labels, axis=1)
    live = labels[FIRST : FIRST + 1] > 0.5
    group = labels[GROUP : GROUP + 1]
    member = (iota((16, total), 0).astype(jnp.float32) == group) & live
    rank = rank_in_bin(member)
    fits = rank < BLOCK_CODE - 1
    full = jnp.maximum(full, jnp.max(jnp.where(live & ~fits, 1.0, 0.0)))
    place = jnp.where(live & fits, group * BLOCK_CODE + rank, -1.0)
    place_ref[...] = column_of(place).astype(jnp.int32)
    place = place.astype(jnp.int32)
    labels = labels.astype(jnp.bfloat16)
    got = got_ref[...]
    empty = jnp.zeros((1, 2 * LANES - BLOCK_CODE), jnp.float32)
    full_row = jnp.broadcast_to(full, (1, feat - 4 * LANES))
    is_last = iota((BLOCK_CODE, feat), 0) == BLOCK_CODE - 1
    for block in range(groups):
        begin = block * BLOCK_CODE
        chosen = hot(iota((BLOCK_CODE, total), 0) + begin == place)
        kinds = dot_nt(labels, chosen)
        last = [kinds[FIRST : FIRST + 1], empty, kinds[SECOND : SECOND + 1], empty, full_row]
        last = jnp.concatenate(last, axis=1)
        send_ref[begin : begin + BLOCK_CODE, :] = jnp.where(is_last, last, dot(chosen, got)).astype(
            jnp.bfloat16
        )


def code_kernel(got_ref, start_ref, out_ref, mine, start, sem):
    total, feat = got_ref.shape
    group_codes, codes_two = start_ref.shape[:2]
    sources = total // BLOCK_CODE
    offset = (lax.axis_index("mem") + 16 * group_codes - group_codes * lax.axis_index("grp")) % 16
    fetch = pltpu.make_async_copy(start_ref.at[jnp.minimum(offset, group_codes - 1)], mine, sem)
    fetch.start()
    labels = []
    full = jnp.zeros((1, 1), jnp.float32)
    for block in range(sources):
        row = last_row(got_ref, block, BLOCK_CODE)
        full = jnp.maximum(full, row[:, 4 * LANES : 4 * LANES + 1])
        kinds = [row[:, 2 * kind * LANES : 2 * kind * LANES + BLOCK_CODE] for kind in (FIRST, SECOND)]
        kinds.append(jnp.zeros((6, BLOCK_CODE), jnp.float32))
        labels.append(jnp.concatenate(kinds, axis=0))
    labels = jnp.concatenate(labels, axis=1)
    first = labels[FIRST : FIRST + 1] - 1.0
    second = jnp.where(first >= 0.0, labels[SECOND : SECOND + 1], -1.0)
    x = got_ref[...]
    cluster = iota((LANES, total), 0).astype(jnp.float32)
    fetch.wait()
    start[...] = jnp.zeros_like(start)
    start[0:codes_two, :] = mine[...].astype(jnp.float32)

    def update(earlier, assigned):
        member = hot(cluster == assigned)
        totals = dot(member, x)
        counts = jnp.sum(member.astype(jnp.float32), axis=1, keepdims=True)
        return (totals + PRIOR * earlier) / (counts + PRIOR)

    diagonal = iota((LANES, LANES), 0) == iota((LANES, LANES), 1)

    def squares_of(rounded):
        wide = rounded.astype(jnp.float32)
        down = jnp.sum(wide * wide, axis=1, keepdims=True)
        return jnp.sum(jnp.where(diagonal, down, 0.0), axis=0, keepdims=True)

    centre_one = update(start[...], first)
    rounded_one = centre_one.astype(jnp.bfloat16)
    centre_two = update(centre_one, second)
    rounded_two = centre_two.astype(jnp.bfloat16)
    squares_one = squares_of(rounded_one)
    squares_two = squares_of(rounded_two)
    wide_x = x.astype(jnp.float32)
    squares = jnp.sum(wide_x * wide_x, axis=1, keepdims=True)
    lane = iota((total, LANES), 1)
    near = (squares - 2.0 * dot_nt(x, rounded_one) + squares_one) / feat
    near = jnp.where(lane.astype(jnp.float32) == column_of(first), near, 0.0)
    near = jnp.sum(near, axis=1, keepdims=True)
    score = (squares - 2.0 * dot_nt(x, rounded_two) + squares_two) / feat
    score = jnp.where(lane == codes_two, near, score)
    out_ref[...] = jnp.where(lane > codes_two, full, score)


def unrelay_kernel(got_ref, place_ref, out_ref):
    total = got_ref.shape[0]
    got = got_ref[...]
    full = jnp.max(got[:, LANES - 1 :])
    terms = jnp.concatenate(three_terms(got), axis=1)
    for begin in range(0, out_ref.shape[0], LANES):
        chosen = hot(iota((LANES, total), 1) == place_ref[begin : begin + LANES, :])
        moved = dot(chosen, terms)
        moved = moved[:, :LANES] + (moved[:, LANES : 2 * LANES] + moved[:, 2 * LANES :])
        out_ref[begin : begin + LANES, :] = jnp.where(iota((LANES, LANES), 1) == LANES - 1, full, moved)


def unpack_kernel(got_ref, slot_ref, all_ref, one_ref, full_ref):
    total = got_ref.shape[0]
    rows = slot_ref.shape[1]
    codes_two = all_ref.shape[0]
    got = got_ref[...]
    full_ref[0, 0] = (jnp.max(got[:, LANES - 1 :]) > 0.5).astype(jnp.int32)
    high, middle, low = three_terms(got.T)
    chosen = hot(iota((total, rows), 0) == slot_ref[...])
    moved = dot(high, chosen) + (dot(middle, chosen) + dot(low, chosen))
    all_ref[...] = moved[:codes_two]
    one_ref[...] = moved[codes_two : codes_two + 1]


def over_members(totals, counts):
    members = lax.axis_size("mem")
    clusters, feat = totals.shape
    share = -(-clusters // members)

    def swap(blocks):
        return lax.all_to_all(blocks, "mem", split_axis=0, concat_axis=0, tiled=True)

    padded = jnp.pad(totals.astype(jnp.bfloat16), ((0, members * share - clusters), (0, 0)))
    own = jnp.sum(swap(padded.reshape(members, share, feat)).astype(jnp.float32), axis=0)
    own = jnp.broadcast_to(own.astype(jnp.bfloat16)[None], (members, share, feat))
    summed = swap(own).reshape(members * share, feat)[:clusters].astype(jnp.float32)
    counted = jnp.sum(swap(jnp.broadcast_to(counts[None], (members, clusters))), axis=0)
    return summed, counted


def pick_block(total):
    for candidate in range(1024, 0, -1):
        if total % candidate == 0:
            return candidate
    return total


def general(embeddings, initial_centroids, row_owner, prefix_offset, first_assign, second_assign):
    row_count, feat_width = embeddings.shape
    group_codes = initial_centroids.shape[0]
    codes_two = initial_centroids.shape[1]
    clusters = group_codes * codes_two
    group_count = lax.axis_size("grp")
    member_count = lax.axis_size("mem")
    devices_all = group_count * member_count
    capacity = 2 * row_count // devices_all + 4
    slot_total = devices_all * capacity
    target = row_owner[:, 0]
    dest_table = (target[:, None] == jnp.arange(devices_all, dtype=jnp.int32)[None, :]).astype(
        jnp.int32
    )
    slot_rank = jnp.sum(jnp.cumsum(dest_table, axis=0) * dest_table, axis=1) - 1
    slot_index = target * capacity + slot_rank
    send_rows = jnp.zeros((slot_total, feat_width), jnp.bfloat16).at[slot_index].set(embeddings)
    labels = jnp.stack([prefix_offset, first_assign, second_assign], axis=1)
    send_labels = jnp.full((slot_total, 3), -1, jnp.int32).at[slot_index].set(labels)
    got_rows, got_labels = (
        lax.all_to_all(send_rows, ("grp", "mem"), split_axis=0, concat_axis=0, tiled=True),
        lax.all_to_all(send_labels, ("grp", "mem"), split_axis=0, concat_axis=0, tiled=True),
    )
    offsets = got_labels[:, 0]
    live = offsets >= 0
    ids_one = jnp.where(live, offsets * codes_two + got_labels[:, 1], -1)
    ids_two = jnp.where(live, offsets * codes_two + got_labels[:, 2], -1)
    squares = jnp.sum(jnp.square(got_rows.astype(jnp.float32)), axis=1)
    block_rows = pick_block(slot_total)
    block_count = slot_total // block_rows
    row_blocks = got_rows.reshape(block_count, block_rows, feat_width)
    cluster_range = jnp.arange(clusters, dtype=jnp.int32)

    def local_totals(cluster_ids):

        def add_block(carry, pieces):
            totals, counts = carry
            block_x, block_ids = pieces
            hot_table = (block_ids[:, None] == cluster_range[None, :]).astype(jnp.bfloat16)
            totals = totals + lax.dot_general(
                hot_table, block_x, (((0,), (0,)), ((), ())), preferred_element_type=jnp.float32
            )
            counts = counts + jnp.sum(hot_table, axis=0, dtype=jnp.float32)
            return ((totals, counts), None)

        start = (
            jnp.zeros((clusters, feat_width), jnp.float32),
            jnp.zeros((clusters,), jnp.float32),
        )
        result, unused = lax.scan(
            add_block, start, (row_blocks, cluster_ids.reshape(block_count, block_rows))
        )
        return result

    start_table = initial_centroids.reshape(clusters, feat_width).astype(jnp.float32)

    def update(earlier, cluster_ids):
        totals, counts = local_totals(cluster_ids)
        totals, counts = over_members(totals, counts)
        centre = (totals + PRIOR * earlier) / (counts[:, None] + PRIOR)
        return (centre, centre.astype(jnp.bfloat16))

    centre_one, rounded_one = update(start_table, ids_one)
    assigned = jnp.take(rounded_one, jnp.maximum(ids_one, 0), axis=0).astype(jnp.float32)
    first_local = (
        squares
        - 2.0 * jnp.sum(got_rows.astype(jnp.float32) * assigned, axis=1)
        + jnp.sum(assigned * assigned, axis=1)
    ) / feat_width
    centre_two, rounded_two = update(centre_one, ids_two)
    centre_squares = jnp.sum(jnp.square(rounded_two.astype(jnp.float32)), axis=1).reshape(
        group_codes, codes_two
    )
    code_range = jnp.arange(group_codes, dtype=jnp.int32)

    def score_block(pieces):
        block_x, block_offsets, block_sq = pieces
        raw = lax.dot_general(
            rounded_two, block_x, (((1,), (1,)), ((), ())), preferred_element_type=jnp.float32
        )
        raw = raw.reshape(group_codes, codes_two, block_rows)
        select = (block_offsets[None, :] == code_range[:, None]).astype(jnp.float32)
        inner = jnp.sum(raw * select[:, None, :], axis=0)
        norms = jnp.sum(centre_squares[:, :, None] * select[:, None, :], axis=0)
        return (block_sq[None, :] - 2.0 * inner + norms) / feat_width

    scored = lax.map(
        score_block,
        (
            row_blocks,
            offsets.reshape(block_count, block_rows),
            squares.reshape(block_count, block_rows),
        ),
    )
    all_local = jnp.transpose(scored, (1, 0, 2)).reshape(codes_two, slot_total)
    one_local = first_local[None, :]
    back_all, back_one = (
        lax.all_to_all(all_local, ("grp", "mem"), split_axis=1, concat_axis=1, tiled=True),
        lax.all_to_all(one_local, ("grp", "mem"), split_axis=1, concat_axis=1, tiled=True),
    )
    distances = jnp.take(back_all, slot_index, axis=1)
    first_distance = jnp.take(back_one[0], slot_index, axis=0)
    return (distances, first_distance)


def quick(embeddings, initial_centroids, row_owner, prefix_offset, first_assign, second_assign):
    rows, feat = embeddings.shape
    group_codes, codes_two = initial_centroids.shape[:2]
    groups = lax.axis_size("grp")
    members = lax.axis_size("mem")
    relay_total = members * BLOCK_RELAY
    code_total = groups * BLOCK_CODE
    shape = jax.ShapeDtypeStruct
    vmem = pl.BlockSpec(memory_space=pltpu.VMEM)

    def swap(array, axis, count):
        blocks = array.reshape(count, array.shape[0] // count, array.shape[1])
        return lax.all_to_all(blocks, axis, split_axis=0, concat_axis=0, tiled=True).reshape(array.shape)

    send, slot = call(
        lambda *refs: pack_kernel(members, group_codes, *refs),
        [shape((relay_total, feat), jnp.bfloat16), shape((1, rows), jnp.int32)],
        [
            row_owner.reshape(1, rows),
            prefix_offset.reshape(1, rows),
            first_assign.reshape(1, rows),
            second_assign.reshape(1, rows),
            embeddings,
        ],
    )
    got = swap(send, "mem", members)
    send, place = call(
        relay_kernel,
        [shape((code_total, feat), jnp.bfloat16), shape((relay_total, 1), jnp.int32)],
        [got],
    )
    got = swap(send, "grp", groups)
    (scored,) = call(
        code_kernel,
        [shape((code_total, LANES), jnp.float32)],
        [got, initial_centroids],
        in_memory=[vmem, pl.BlockSpec(memory_space=pl.ANY)],
        scratch=[
            pltpu.VMEM((codes_two, feat), jnp.bfloat16),
            pltpu.VMEM((LANES, feat), jnp.float32),
            pltpu.SemaphoreType.DMA,
        ],
    )
    back = swap(scored, "grp", groups)
    (back,) = call(unrelay_kernel, [shape((relay_total, LANES), jnp.float32)], [back, place])
    back = swap(back, "mem", members)
    return call(
        unpack_kernel,
        [shape((codes_two, rows), jnp.float32), shape((1, rows), jnp.float32), shape((1, 1), jnp.int32)],
        [back, slot],
        out_memory=[vmem, vmem, pl.BlockSpec(memory_space=pltpu.SMEM)],
    )


def body(*inputs):
    distances, first_distance, full = quick(*inputs)
    return lax.cond(
        full[0, 0] > 0,
        lambda kept, given: general(*given),
        lambda kept, given: kept,
        (distances, first_distance[0]),
        inputs,
    )


def solution(mesh):
    placed = (
        P(("grp", "mem"), None),
        P("grp", None, None),
        P(("grp", "mem"), None),
        P(("grp", "mem")),
        P(("grp", "mem")),
        P(("grp", "mem")),
    )
    return jax.shard_map(
        body,
        mesh=mesh,
        in_specs=placed,
        out_specs=(P(None, ("grp", "mem")), P(("grp", "mem"))),
        check_vma=False,
    )
```

```python
import jax
import jax.numpy as jnp
from jax import lax
from jax.experimental import pallas as pl
from jax.experimental.pallas import tpu as pltpu
from jax.sharding import PartitionSpec as P

PRIOR = 16
BLOCK_RELAY = 72
BLOCK_CODE = 160
BLOCK_BACK = 24
LANES = 128
FIRST, SECOND, RANK, GROUP, MEMBER = 0, 1, 2, 3, 3
ROUNDING = 1.5e-4
NT = (((1,), (1,)), ((), ()))
VMEM_LIMIT = 48 * 1024 * 1024


def iota(shape, dim):
    return lax.broadcasted_iota(jnp.int32, shape, dim)


def hot(condition):
    return jnp.where(condition, 1.0, 0.0).astype(jnp.bfloat16)


def dot(a, b):
    return jnp.dot(a, b, preferred_element_type=jnp.float32)


def dot_nt(a, b):
    return lax.dot_general(a, b, NT, preferred_element_type=jnp.float32)


def three_terms(values):
    high = values.astype(jnp.bfloat16)
    rest = values - high.astype(jnp.float32)
    middle = rest.astype(jnp.bfloat16)
    low = (rest - middle.astype(jnp.float32)).astype(jnp.bfloat16)
    return high, middle, low


def call(kernel, out_shape, args, out_memory=None, in_memory=None, scratch=()):
    vmem = pl.BlockSpec(memory_space=pltpu.VMEM)
    return pl.pallas_call(
        kernel,
        out_shape=out_shape,
        in_specs=in_memory or [vmem] * len(args),
        out_specs=out_memory or [vmem] * len(out_shape),
        scratch_shapes=scratch,
        compiler_params=pltpu.CompilerParams(vmem_limit_bytes=VMEM_LIMIT),
    )(*args)


def rank_in_bin(member):
    bins = hot(member)
    before = hot(iota((LANES, LANES), 0) < iota((LANES, LANES), 1))
    base = jnp.zeros((member.shape[0], 1), jnp.float32)
    ranks = []
    for begin in range(0, member.shape[1], LANES):
        piece = bins[:, begin : begin + LANES]
        ranks.append(dot(piece, before) + base)
        base = base + jnp.sum(piece.astype(jnp.float32), axis=1, keepdims=True)
    rank = jnp.concatenate(ranks, axis=1)
    return jnp.sum(jnp.where(member, rank, 0.0), axis=0, keepdims=True)


def column_of(row):
    diagonal = iota((LANES, LANES), 0) == iota((LANES, LANES), 1)
    pieces = []
    for begin in range(0, row.shape[1], LANES):
        piece = jnp.where(diagonal, row[:, begin : begin + LANES], 0.0)
        pieces.append(jnp.sum(piece, axis=1, keepdims=True))
    return jnp.concatenate(pieces, axis=0)


def last_rows(ref, block, size):
    begin = block * size + size - 8
    return ref[begin : begin + 8, :].astype(jnp.float32)


def pack_kernel(members, group_codes, owner_ref, offset_ref, first_ref, second_ref, x_ref, send_ref, slot_ref):
    rows, feat = x_ref.shape
    group = owner_ref[...] // members
    code = group * group_codes + offset_ref[...]
    relay = code % members
    rank = rank_in_bin(iota((members, rows), 0) == relay).astype(jnp.int32)
    back_rank = rank_in_bin(iota((LANES, rows), 0) == code).astype(jnp.int32)
    fits = rank < BLOCK_RELAY - 1
    full = jnp.max(jnp.where(fits & (back_rank < BLOCK_BACK), 0.0, 1.0))
    slot_ref[...] = (group * members + relay) * BLOCK_BACK + jnp.minimum(back_rank, BLOCK_BACK - 1)
    rank = jnp.where(fits, rank, -1)
    kind = iota((16, rows), 0)
    labels = jnp.where(kind == FIRST, first_ref[...] + 1, 0)
    labels = jnp.where(kind == SECOND, second_ref[...], labels)
    labels = jnp.where(kind == RANK, jnp.minimum(back_rank, BLOCK_BACK - 1), labels)
    labels = jnp.where(kind == GROUP, group, labels)
    labels = labels.astype(jnp.float32).astype(jnp.bfloat16)
    x = x_ref[...]
    full_row = jnp.full((1, feat - 4 * LANES), full, jnp.float32)
    is_last = iota((BLOCK_RELAY, feat), 0) == BLOCK_RELAY - 1
    for block in range(members):
        begin = block * BLOCK_RELAY
        chosen = hot((iota((LANES, rows), 0) == rank) & (relay == block))
        kinds = dot_nt(labels, chosen)
        last = [kinds[kind : kind + 1] for kind in (FIRST, SECOND, RANK, GROUP)] + [full_row]
        last = jnp.concatenate(last, axis=1)
        moved = dot(chosen[:BLOCK_RELAY], x)
        send_ref[begin : begin + BLOCK_RELAY, :] = jnp.where(is_last, last, moved).astype(jnp.bfloat16)


def relay_kernel(got_ref, send_ref):
    total, feat = got_ref.shape
    sources = total // BLOCK_RELAY
    groups = send_ref.shape[0] // BLOCK_CODE
    labels = []
    full = jnp.zeros((1, 1), jnp.float32)
    for block in range(sources):
        row = last_rows(got_ref, block, BLOCK_RELAY)[7:8]
        full = jnp.maximum(full, row[:, 4 * LANES : 4 * LANES + 1])
        kinds = [row[:, kind * LANES : kind * LANES + BLOCK_RELAY] for kind in (FIRST, SECOND, RANK, GROUP)]
        kinds.append(jnp.full((1, BLOCK_RELAY), block, jnp.float32))
        kinds.append(jnp.zeros((11, BLOCK_RELAY), jnp.float32))
        labels.append(jnp.concatenate(kinds, axis=0))
    labels = jnp.concatenate(labels, axis=1)
    live = labels[FIRST : FIRST + 1] > 0.5
    group = labels[GROUP : GROUP + 1]
    member = (iota((16, total), 0).astype(jnp.float32) == group) & live
    rank = rank_in_bin(member)
    fits = rank < BLOCK_CODE - 2
    full = jnp.maximum(full, jnp.max(jnp.where(live & ~fits, 1.0, 0.0)))
    place = jnp.where(live & fits, group * BLOCK_CODE + rank, -1.0).astype(jnp.int32)
    labels = labels.astype(jnp.bfloat16)
    got = got_ref[...]
    empty = jnp.zeros((1, 2 * LANES - BLOCK_CODE), jnp.float32)
    full_row = jnp.broadcast_to(full, (1, feat - 4 * LANES))
    row_id = iota((BLOCK_CODE, feat), 0)
    for block in range(groups):
        begin = block * BLOCK_CODE
        chosen = hot(iota((BLOCK_CODE, total), 0) + begin == place)
        kinds = dot_nt(labels, chosen)
        codes = [kinds[FIRST : FIRST + 1], empty, kinds[SECOND : SECOND + 1], empty, full_row]
        source = [kinds[RANK : RANK + 1], empty, kinds[GROUP + 1 : GROUP + 2], empty, full_row]
        moved = jnp.where(row_id == BLOCK_CODE - 2, jnp.concatenate(codes, axis=1), dot(chosen, got))
        moved = jnp.where(row_id == BLOCK_CODE - 1, jnp.concatenate(source, axis=1), moved)
        send_ref[begin : begin + BLOCK_CODE, :] = moved.astype(jnp.bfloat16)


def code_kernel(members, got_ref, start_ref, out_ref, mine, start, sem):
    total, feat = got_ref.shape
    group_codes, codes_two = start_ref.shape[:2]
    sources = total // BLOCK_CODE
    offset = (lax.axis_index("mem") + members * group_codes - group_codes * lax.axis_index("grp")) % members
    fetch = pltpu.make_async_copy(start_ref.at[jnp.minimum(offset, group_codes - 1)], mine, sem)
    fetch.start()
    labels = []
    full = jnp.zeros((1, 1), jnp.float32)
    for block in range(sources):
        both = last_rows(got_ref, block, BLOCK_CODE)
        codes, source = both[6:7], both[7:8]
        full = jnp.maximum(full, codes[:, 4 * LANES : 4 * LANES + 1])
        kinds = [row[:, begin : begin + BLOCK_CODE] for row in (codes, source) for begin in (0, 2 * LANES)]
        kinds.append(jnp.zeros((4, BLOCK_CODE), jnp.float32))
        labels.append(jnp.concatenate(kinds, axis=0))
    back = [kinds[MEMBER : MEMBER + 1] * BLOCK_BACK + kinds[RANK : RANK + 1] for kinds in labels]
    back = [jnp.where(kinds[FIRST : FIRST + 1] > 0.5, row, -1.0) for kinds, row in zip(labels, back)]
    labels = jnp.concatenate(labels, axis=1)
    first = labels[FIRST : FIRST + 1] - 1.0
    second = jnp.where(first >= 0.0, labels[SECOND : SECOND + 1], -1.0)
    x = got_ref[...]
    cluster = iota((LANES, total), 0).astype(jnp.float32)
    fetch.wait()
    start[...] = jnp.zeros_like(start)
    start[0:codes_two, :] = mine[...].astype(jnp.float32)

    def update(earlier, assigned):
        member = hot(cluster == assigned)
        totals = dot(member, x)
        counts = jnp.sum(member.astype(jnp.float32), axis=1, keepdims=True)
        return (totals + PRIOR * earlier) / (counts + PRIOR)

    diagonal = iota((LANES, LANES), 0) == iota((LANES, LANES), 1)

    def squares_of(rounded):
        wide = rounded.astype(jnp.float32)
        down = jnp.sum(wide * wide, axis=1, keepdims=True)
        return jnp.sum(jnp.where(diagonal, down, 0.0), axis=0, keepdims=True)

    centre_one = update(start[...], first)
    rounded_one = centre_one.astype(jnp.bfloat16)
    centre_two = update(centre_one, second)
    rounded_two = centre_two.astype(jnp.bfloat16)
    squares_one = squares_of(rounded_one)
    squares_two = squares_of(rounded_two)
    wide_x = x.astype(jnp.float32)
    squares = jnp.sum(wide_x * wide_x, axis=1, keepdims=True)
    lane = iota((total, LANES), 1)
    first_column = column_of(first)
    near = (squares - 2.0 * dot_nt(x, rounded_one) + squares_one) / feat
    near = jnp.where(lane.astype(jnp.float32) == first_column, near, 0.0)
    near = jnp.sum(near, axis=1, keepdims=True)
    score = (squares - 2.0 * dot_nt(x, rounded_two) + squares_two) / feat
    score = jnp.where(lane < codes_two, score, 0.0)
    mean = jnp.sum(score, axis=1, keepdims=True) / codes_two
    rest = jnp.where(lane < codes_two, score - mean, 0.0)
    record = rest.astype(jnp.bfloat16)
    lost = rest - record.astype(jnp.float32)
    lost = jnp.sum(lost * lost - (ROUNDING * ROUNDING) * (score * score), axis=1, keepdims=True)
    full = jnp.maximum(full, jnp.max(jnp.where((first_column >= 0.0) & (lost > 0.0), 1.0, 0.0)))
    for place, term in enumerate(three_terms(mean) + three_terms(near)):
        record = jnp.where(lane == codes_two + place, term, record)
    for block in range(sources):
        size = members * BLOCK_BACK
        chosen = hot(iota((size, BLOCK_CODE), 0).astype(jnp.float32) == back[block])
        moved = dot(chosen, record[block * BLOCK_CODE : (block + 1) * BLOCK_CODE])
        moved = jnp.where(iota((size, LANES), 1) == LANES - 1, full, moved)
        out_ref[block * size : (block + 1) * size, :] = moved.astype(jnp.bfloat16)


def unpack_kernel(got_ref, slot_ref, all_ref, one_ref, full_ref):
    total = got_ref.shape[0]
    rows = slot_ref.shape[1]
    codes_two = all_ref.shape[0]
    got = got_ref[...]
    full_ref[0, 0] = (jnp.max(got[:, LANES - 1 :].astype(jnp.float32)) > 0.5).astype(jnp.int32)
    chosen = hot(iota((total, rows), 0) == slot_ref[...])
    moved = dot(got.T, chosen)
    mean, near = [
        moved[begin : begin + 1] + (moved[begin + 1 : begin + 2] + moved[begin + 2 : begin + 3])
        for begin in (codes_two, codes_two + 3)
    ]
    all_ref[...] = moved[:codes_two] + mean
    one_ref[...] = near


def over_members(totals, counts):
    members = lax.axis_size("mem")
    clusters, feat = totals.shape
    share = -(-clusters // members)

    def swap(blocks):
        return lax.all_to_all(blocks, "mem", split_axis=0, concat_axis=0, tiled=True)

    padded = jnp.pad(totals.astype(jnp.bfloat16), ((0, members * share - clusters), (0, 0)))
    own = jnp.sum(swap(padded.reshape(members, share, feat)).astype(jnp.float32), axis=0)
    own = jnp.broadcast_to(own.astype(jnp.bfloat16)[None], (members, share, feat))
    summed = swap(own).reshape(members * share, feat)[:clusters].astype(jnp.float32)
    counted = jnp.sum(swap(jnp.broadcast_to(counts[None], (members, clusters))), axis=0)
    return summed, counted


def pick_block(total):
    for candidate in range(1024, 0, -1):
        if total % candidate == 0:
            return candidate
    return total


def general(embeddings, initial_centroids, row_owner, prefix_offset, first_assign, second_assign):
    row_count, feat_width = embeddings.shape
    group_codes = initial_centroids.shape[0]
    codes_two = initial_centroids.shape[1]
    clusters = group_codes * codes_two
    group_count = lax.axis_size("grp")
    member_count = lax.axis_size("mem")
    devices_all = group_count * member_count
    capacity = 2 * row_count // devices_all + 4
    slot_total = devices_all * capacity
    target = row_owner[:, 0]
    dest_table = (target[:, None] == jnp.arange(devices_all, dtype=jnp.int32)[None, :]).astype(
        jnp.int32
    )
    slot_rank = jnp.sum(jnp.cumsum(dest_table, axis=0) * dest_table, axis=1) - 1
    slot_index = target * capacity + slot_rank
    send_rows = jnp.zeros((slot_total, feat_width), jnp.bfloat16).at[slot_index].set(embeddings)
    labels = jnp.stack([prefix_offset, first_assign, second_assign], axis=1)
    send_labels = jnp.full((slot_total, 3), -1, jnp.int32).at[slot_index].set(labels)
    got_rows, got_labels = (
        lax.all_to_all(send_rows, ("grp", "mem"), split_axis=0, concat_axis=0, tiled=True),
        lax.all_to_all(send_labels, ("grp", "mem"), split_axis=0, concat_axis=0, tiled=True),
    )
    offsets = got_labels[:, 0]
    live = offsets >= 0
    ids_one = jnp.where(live, offsets * codes_two + got_labels[:, 1], -1)
    ids_two = jnp.where(live, offsets * codes_two + got_labels[:, 2], -1)
    squares = jnp.sum(jnp.square(got_rows.astype(jnp.float32)), axis=1)
    block_rows = pick_block(slot_total)
    block_count = slot_total // block_rows
    row_blocks = got_rows.reshape(block_count, block_rows, feat_width)
    cluster_range = jnp.arange(clusters, dtype=jnp.int32)

    def local_totals(cluster_ids):

        def add_block(carry, pieces):
            totals, counts = carry
            block_x, block_ids = pieces
            hot_table = (block_ids[:, None] == cluster_range[None, :]).astype(jnp.bfloat16)
            totals = totals + lax.dot_general(
                hot_table, block_x, (((0,), (0,)), ((), ())), preferred_element_type=jnp.float32
            )
            counts = counts + jnp.sum(hot_table, axis=0, dtype=jnp.float32)
            return ((totals, counts), None)

        start = (
            jnp.zeros((clusters, feat_width), jnp.float32),
            jnp.zeros((clusters,), jnp.float32),
        )
        result, unused = lax.scan(
            add_block, start, (row_blocks, cluster_ids.reshape(block_count, block_rows))
        )
        return result

    start_table = initial_centroids.reshape(clusters, feat_width).astype(jnp.float32)

    def update(earlier, cluster_ids):
        totals, counts = local_totals(cluster_ids)
        totals, counts = over_members(totals, counts)
        centre = (totals + PRIOR * earlier) / (counts[:, None] + PRIOR)
        return (centre, centre.astype(jnp.bfloat16))

    centre_one, rounded_one = update(start_table, ids_one)
    assigned = jnp.take(rounded_one, jnp.maximum(ids_one, 0), axis=0).astype(jnp.float32)
    first_local = (
        squares
        - 2.0 * jnp.sum(got_rows.astype(jnp.float32) * assigned, axis=1)
        + jnp.sum(assigned * assigned, axis=1)
    ) / feat_width
    centre_two, rounded_two = update(centre_one, ids_two)
    centre_squares = jnp.sum(jnp.square(rounded_two.astype(jnp.float32)), axis=1).reshape(
        group_codes, codes_two
    )
    code_range = jnp.arange(group_codes, dtype=jnp.int32)

    def score_block(pieces):
        block_x, block_offsets, block_sq = pieces
        raw = lax.dot_general(
            rounded_two, block_x, (((1,), (1,)), ((), ())), preferred_element_type=jnp.float32
        )
        raw = raw.reshape(group_codes, codes_two, block_rows)
        select = (block_offsets[None, :] == code_range[:, None]).astype(jnp.float32)
        inner = jnp.sum(raw * select[:, None, :], axis=0)
        norms = jnp.sum(centre_squares[:, :, None] * select[:, None, :], axis=0)
        return (block_sq[None, :] - 2.0 * inner + norms) / feat_width

    scored = lax.map(
        score_block,
        (
            row_blocks,
            offsets.reshape(block_count, block_rows),
            squares.reshape(block_count, block_rows),
        ),
    )
    all_local = jnp.transpose(scored, (1, 0, 2)).reshape(codes_two, slot_total)
    one_local = first_local[None, :]
    back_all, back_one = (
        lax.all_to_all(all_local, ("grp", "mem"), split_axis=1, concat_axis=1, tiled=True),
        lax.all_to_all(one_local, ("grp", "mem"), split_axis=1, concat_axis=1, tiled=True),
    )
    distances = jnp.take(back_all, slot_index, axis=1)
    first_distance = jnp.take(back_one[0], slot_index, axis=0)
    return (distances, first_distance)


def quick(embeddings, initial_centroids, row_owner, prefix_offset, first_assign, second_assign):
    rows, feat = embeddings.shape
    group_codes, codes_two = initial_centroids.shape[:2]
    groups = lax.axis_size("grp")
    members = lax.axis_size("mem")
    relay_total = members * BLOCK_RELAY
    code_total = groups * BLOCK_CODE
    shape = jax.ShapeDtypeStruct
    vmem = pl.BlockSpec(memory_space=pltpu.VMEM)

    def swap(array, axis, count):
        blocks = array.reshape(count, array.shape[0] // count, array.shape[1])
        return lax.all_to_all(blocks, axis, split_axis=0, concat_axis=0, tiled=True).reshape(array.shape)

    send, slot = call(
        lambda *refs: pack_kernel(members, group_codes, *refs),
        [shape((relay_total, feat), jnp.bfloat16), shape((1, rows), jnp.int32)],
        [
            row_owner.reshape(1, rows),
            prefix_offset.reshape(1, rows),
            first_assign.reshape(1, rows),
            second_assign.reshape(1, rows),
            embeddings,
        ],
    )
    got = swap(send, "mem", members)
    (send,) = call(relay_kernel, [shape((code_total, feat), jnp.bfloat16)], [got])
    got = swap(send, "grp", groups)
    (record,) = call(
        lambda *refs: code_kernel(members, *refs),
        [shape((groups * members * BLOCK_BACK, LANES), jnp.bfloat16)],
        [got, initial_centroids],
        in_memory=[vmem, pl.BlockSpec(memory_space=pl.ANY)],
        scratch=[
            pltpu.VMEM((codes_two, feat), jnp.bfloat16),
            pltpu.VMEM((LANES, feat), jnp.float32),
            pltpu.SemaphoreType.DMA,
        ],
    )
    back = swap(record, ("grp", "mem"), groups * members)
    return call(
        unpack_kernel,
        [shape((codes_two, rows), jnp.float32), shape((1, rows), jnp.float32), shape((1, 1), jnp.int32)],
        [back, slot],
        out_memory=[vmem, vmem, pl.BlockSpec(memory_space=pltpu.SMEM)],
    )


def body(*inputs):
    distances, first_distance, full = quick(*inputs)
    return lax.cond(
        full[0, 0] > 0,
        lambda kept, given: general(*given),
        lambda kept, given: kept,
        (distances, first_distance[0]),
        inputs,
    )


def solution(mesh):
    placed = (
        P(("grp", "mem"), None),
        P("grp", None, None),
        P(("grp", "mem"), None),
        P(("grp", "mem")),
        P(("grp", "mem")),
        P(("grp", "mem")),
    )
    return jax.shard_map(
        body,
        mesh=mesh,
        in_specs=placed,
        out_specs=(P(None, ("grp", "mem")), P(("grp", "mem"))),
        check_vma=False,
    )
```

```python
import jax
import jax.numpy as jnp
from jax import lax
from jax.experimental import pallas as pl
from jax.experimental.pallas import tpu as pltpu
from jax.sharding import PartitionSpec as P

PRIOR = 16
BLOCK_RELAY = 72
BLOCK_CODE = 160
BLOCK_BACK = 24
LANES = 128
FIRST, SECOND, RANK, GROUP, MEMBER = 0, 1, 2, 3, 3
ROUNDING_ROW = 4.5e-4
ROUNDING_ALL = 2.5e-4
NT = (((1,), (1,)), ((), ()))
VMEM_LIMIT = 48 * 1024 * 1024


def iota(shape, dim):
    return lax.broadcasted_iota(jnp.int32, shape, dim)


def hot(condition):
    return jnp.where(condition, 1.0, 0.0).astype(jnp.bfloat16)


def dot(a, b):
    return jnp.dot(a, b, preferred_element_type=jnp.float32)


def dot_nt(a, b):
    return lax.dot_general(a, b, NT, preferred_element_type=jnp.float32)


def three_terms(values):
    high = values.astype(jnp.bfloat16)
    rest = values - high.astype(jnp.float32)
    middle = rest.astype(jnp.bfloat16)
    low = (rest - middle.astype(jnp.float32)).astype(jnp.bfloat16)
    return high, middle, low


def call(kernel, out_shape, args, out_memory=None, in_memory=None, scratch=()):
    vmem = pl.BlockSpec(memory_space=pltpu.VMEM)
    return pl.pallas_call(
        kernel,
        out_shape=out_shape,
        in_specs=in_memory or [vmem] * len(args),
        out_specs=out_memory or [vmem] * len(out_shape),
        scratch_shapes=scratch,
        compiler_params=pltpu.CompilerParams(vmem_limit_bytes=VMEM_LIMIT),
    )(*args)


def rank_in_bin(member):
    bins = hot(member)
    before = hot(iota((LANES, LANES), 0) < iota((LANES, LANES), 1))
    base = jnp.zeros((member.shape[0], 1), jnp.float32)
    ranks = []
    for begin in range(0, member.shape[1], LANES):
        piece = bins[:, begin : begin + LANES]
        ranks.append(dot(piece, before) + base)
        base = base + jnp.sum(piece.astype(jnp.float32), axis=1, keepdims=True)
    rank = jnp.concatenate(ranks, axis=1)
    return jnp.sum(jnp.where(member, rank, 0.0), axis=0, keepdims=True)


def column_of(row):
    diagonal = iota((LANES, LANES), 0) == iota((LANES, LANES), 1)
    pieces = []
    for begin in range(0, row.shape[1], LANES):
        piece = jnp.where(diagonal, row[:, begin : begin + LANES], 0.0)
        pieces.append(jnp.sum(piece, axis=1, keepdims=True))
    return jnp.concatenate(pieces, axis=0)


def last_rows(ref, block, size):
    begin = block * size + size - 8
    return ref[begin : begin + 8, :].astype(jnp.float32)


def pack_kernel(members, group_codes, owner_ref, offset_ref, first_ref, second_ref, x_ref, send_ref, slot_ref):
    rows, feat = x_ref.shape
    group = owner_ref[...] // members
    code = group * group_codes + offset_ref[...]
    relay = code % members
    rank = rank_in_bin(iota((members, rows), 0) == relay).astype(jnp.int32)
    back_rank = rank_in_bin(iota((LANES, rows), 0) == code).astype(jnp.int32)
    fits = rank < BLOCK_RELAY - 1
    full = jnp.max(jnp.where(fits & (back_rank < BLOCK_BACK), 0.0, 1.0))
    slot_ref[...] = (group * members + relay) * BLOCK_BACK + jnp.minimum(back_rank, BLOCK_BACK - 1)
    rank = jnp.where(fits, rank, -1)
    kind = iota((16, rows), 0)
    labels = jnp.where(kind == FIRST, first_ref[...] + 1, 0)
    labels = jnp.where(kind == SECOND, second_ref[...], labels)
    labels = jnp.where(kind == RANK, jnp.minimum(back_rank, BLOCK_BACK - 1), labels)
    labels = jnp.where(kind == GROUP, group, labels)
    labels = labels.astype(jnp.float32).astype(jnp.bfloat16)
    x = x_ref[...]
    full_row = jnp.full((1, feat - 4 * LANES), full, jnp.float32)
    is_last = iota((BLOCK_RELAY, feat), 0) == BLOCK_RELAY - 1
    for block in range(members):
        begin = block * BLOCK_RELAY
        chosen = hot((iota((LANES, rows), 0) == rank) & (relay == block))
        kinds = dot_nt(labels, chosen)
        last = [kinds[kind : kind + 1] for kind in (FIRST, SECOND, RANK, GROUP)] + [full_row]
        last = jnp.concatenate(last, axis=1)
        moved = dot(chosen[:BLOCK_RELAY], x)
        send_ref[begin : begin + BLOCK_RELAY, :] = jnp.where(is_last, last, moved).astype(jnp.bfloat16)


def relay_kernel(got_ref, send_ref):
    total, feat = got_ref.shape
    sources = total // BLOCK_RELAY
    groups = send_ref.shape[0] // BLOCK_CODE
    labels = []
    full = jnp.zeros((1, 1), jnp.float32)
    for block in range(sources):
        row = last_rows(got_ref, block, BLOCK_RELAY)[7:8]
        full = jnp.maximum(full, row[:, 4 * LANES : 4 * LANES + 1])
        kinds = [row[:, kind * LANES : kind * LANES + BLOCK_RELAY] for kind in (FIRST, SECOND, RANK, GROUP)]
        kinds.append(jnp.full((1, BLOCK_RELAY), block, jnp.float32))
        kinds.append(jnp.zeros((11, BLOCK_RELAY), jnp.float32))
        labels.append(jnp.concatenate(kinds, axis=0))
    labels = jnp.concatenate(labels, axis=1)
    live = labels[FIRST : FIRST + 1] > 0.5
    group = labels[GROUP : GROUP + 1]
    member = (iota((16, total), 0).astype(jnp.float32) == group) & live
    rank = rank_in_bin(member)
    fits = rank < BLOCK_CODE - 2
    full = jnp.maximum(full, jnp.max(jnp.where(live & ~fits, 1.0, 0.0)))
    place = jnp.where(live & fits, group * BLOCK_CODE + rank, -1.0).astype(jnp.int32)
    labels = labels.astype(jnp.bfloat16)
    got = got_ref[...]
    empty = jnp.zeros((1, 2 * LANES - BLOCK_CODE), jnp.float32)
    full_row = jnp.broadcast_to(full, (1, feat - 4 * LANES))
    row_id = iota((BLOCK_CODE, feat), 0)
    for block in range(groups):
        begin = block * BLOCK_CODE
        chosen = hot(iota((BLOCK_CODE, total), 0) + begin == place)
        kinds = dot_nt(labels, chosen)
        codes = [kinds[FIRST : FIRST + 1], empty, kinds[SECOND : SECOND + 1], empty, full_row]
        source = [kinds[RANK : RANK + 1], empty, kinds[GROUP + 1 : GROUP + 2], empty, full_row]
        moved = jnp.where(row_id == BLOCK_CODE - 2, jnp.concatenate(codes, axis=1), dot(chosen, got))
        moved = jnp.where(row_id == BLOCK_CODE - 1, jnp.concatenate(source, axis=1), moved)
        send_ref[begin : begin + BLOCK_CODE, :] = moved.astype(jnp.bfloat16)


def code_kernel(members, got_ref, start_ref, out_ref, mine, start, sem):
    total, feat = got_ref.shape
    group_codes, codes_two = start_ref.shape[:2]
    sources = total // BLOCK_CODE
    offset = (lax.axis_index("mem") + members * group_codes - group_codes * lax.axis_index("grp")) % members
    fetch = pltpu.make_async_copy(start_ref.at[jnp.minimum(offset, group_codes - 1)], mine, sem)
    fetch.start()
    labels = []
    full = jnp.zeros((1, 1), jnp.float32)
    for block in range(sources):
        both = last_rows(got_ref, block, BLOCK_CODE)
        codes, source = both[6:7], both[7:8]
        full = jnp.maximum(full, codes[:, 4 * LANES : 4 * LANES + 1])
        kinds = [row[:, begin : begin + BLOCK_CODE] for row in (codes, source) for begin in (0, 2 * LANES)]
        kinds.append(jnp.zeros((4, BLOCK_CODE), jnp.float32))
        labels.append(jnp.concatenate(kinds, axis=0))
    back = [kinds[MEMBER : MEMBER + 1] * BLOCK_BACK + kinds[RANK : RANK + 1] for kinds in labels]
    back = [jnp.where(kinds[FIRST : FIRST + 1] > 0.5, row, -1.0) for kinds, row in zip(labels, back)]
    labels = jnp.concatenate(labels, axis=1)
    first = labels[FIRST : FIRST + 1] - 1.0
    second = jnp.where(first >= 0.0, labels[SECOND : SECOND + 1], -1.0)
    x = got_ref[...]
    cluster = iota((LANES, total), 0).astype(jnp.float32)
    fetch.wait()
    start[...] = jnp.zeros_like(start)
    start[0:codes_two, :] = mine[...].astype(jnp.float32)

    def update(earlier, assigned):
        member = hot(cluster == assigned)
        totals = dot(member, x)
        counts = jnp.sum(member.astype(jnp.float32), axis=1, keepdims=True)
        return (totals + PRIOR * earlier) / (counts + PRIOR)

    diagonal = iota((LANES, LANES), 0) == iota((LANES, LANES), 1)

    def squares_of(rounded):
        wide = rounded.astype(jnp.float32)
        down = jnp.sum(wide * wide, axis=1, keepdims=True)
        return jnp.sum(jnp.where(diagonal, down, 0.0), axis=0, keepdims=True)

    centre_one = update(start[...], first)
    rounded_one = centre_one.astype(jnp.bfloat16)
    centre_two = update(centre_one, second)
    rounded_two = centre_two.astype(jnp.bfloat16)
    squares_one = squares_of(rounded_one)
    squares_two = squares_of(rounded_two)
    wide_x = x.astype(jnp.float32)
    squares = jnp.sum(wide_x * wide_x, axis=1, keepdims=True)
    lane = iota((total, LANES), 1)
    first_column = column_of(first)
    near = (squares - 2.0 * dot_nt(x, rounded_one) + squares_one) / feat
    near = jnp.where(lane.astype(jnp.float32) == first_column, near, 0.0)
    near = jnp.sum(near, axis=1, keepdims=True)
    score = (squares - 2.0 * dot_nt(x, rounded_two) + squares_two) / feat
    score = jnp.where(lane < codes_two, score, 0.0)
    mean = jnp.sum(score, axis=1, keepdims=True) / codes_two
    rest = jnp.where(lane < codes_two, score - mean, 0.0)
    record = rest.astype(jnp.bfloat16)
    lost = rest - record.astype(jnp.float32)
    is_live = first_column >= 0.0
    lost = jnp.where(is_live, jnp.sum(lost * lost, axis=1, keepdims=True), 0.0)
    sent = jnp.where(is_live, jnp.sum(score * score, axis=1, keepdims=True), 0.0)
    over = jnp.max(jnp.where(lost > (ROUNDING_ROW * ROUNDING_ROW) * sent, 1.0, 0.0))
    over_all = jnp.sum(lost) > (ROUNDING_ALL * ROUNDING_ALL) * jnp.sum(sent)
    full = jnp.maximum(full, jnp.maximum(over, jnp.where(over_all, 1.0, 0.0)))
    for place, term in enumerate(three_terms(mean) + three_terms(near)):
        record = jnp.where(lane == codes_two + place, term, record)
    for block in range(sources):
        size = members * BLOCK_BACK
        chosen = hot(iota((size, BLOCK_CODE), 0).astype(jnp.float32) == back[block])
        moved = dot(chosen, record[block * BLOCK_CODE : (block + 1) * BLOCK_CODE])
        moved = jnp.where(iota((size, LANES), 1) == LANES - 1, full, moved)
        out_ref[block * size : (block + 1) * size, :] = moved.astype(jnp.bfloat16)


def unpack_kernel(got_ref, slot_ref, all_ref, one_ref, full_ref):
    total = got_ref.shape[0]
    rows = slot_ref.shape[1]
    codes_two = all_ref.shape[0]
    got = got_ref[...]
    full_ref[0, 0] = (jnp.max(got[:, LANES - 1 :].astype(jnp.float32)) > 0.5).astype(jnp.int32)
    chosen = hot(iota((total, rows), 0) == slot_ref[...])
    moved = dot(got.T, chosen)
    mean, near = [
        moved[begin : begin + 1] + (moved[begin + 1 : begin + 2] + moved[begin + 2 : begin + 3])
        for begin in (codes_two, codes_two + 3)
    ]
    all_ref[...] = moved[:codes_two] + mean
    one_ref[...] = near


def over_members(totals, counts):
    members = lax.axis_size("mem")
    clusters, feat = totals.shape
    share = -(-clusters // members)

    def swap(blocks):
        return lax.all_to_all(blocks, "mem", split_axis=0, concat_axis=0, tiled=True)

    padded = jnp.pad(totals.astype(jnp.bfloat16), ((0, members * share - clusters), (0, 0)))
    own = jnp.sum(swap(padded.reshape(members, share, feat)).astype(jnp.float32), axis=0)
    own = jnp.broadcast_to(own.astype(jnp.bfloat16)[None], (members, share, feat))
    summed = swap(own).reshape(members * share, feat)[:clusters].astype(jnp.float32)
    counted = jnp.sum(swap(jnp.broadcast_to(counts[None], (members, clusters))), axis=0)
    return summed, counted


def pick_block(total):
    for candidate in range(1024, 0, -1):
        if total % candidate == 0:
            return candidate
    return total


def general(embeddings, initial_centroids, row_owner, prefix_offset, first_assign, second_assign):
    row_count, feat_width = embeddings.shape
    group_codes = initial_centroids.shape[0]
    codes_two = initial_centroids.shape[1]
    clusters = group_codes * codes_two
    group_count = lax.axis_size("grp")
    member_count = lax.axis_size("mem")
    devices_all = group_count * member_count
    capacity = 2 * row_count // devices_all + 4
    slot_total = devices_all * capacity
    target = row_owner[:, 0]
    dest_table = (target[:, None] == jnp.arange(devices_all, dtype=jnp.int32)[None, :]).astype(
        jnp.int32
    )
    slot_rank = jnp.sum(jnp.cumsum(dest_table, axis=0) * dest_table, axis=1) - 1
    slot_index = target * capacity + slot_rank
    send_rows = jnp.zeros((slot_total, feat_width), jnp.bfloat16).at[slot_index].set(embeddings)
    labels = jnp.stack([prefix_offset, first_assign, second_assign], axis=1)
    send_labels = jnp.full((slot_total, 3), -1, jnp.int32).at[slot_index].set(labels)
    got_rows, got_labels = (
        lax.all_to_all(send_rows, ("grp", "mem"), split_axis=0, concat_axis=0, tiled=True),
        lax.all_to_all(send_labels, ("grp", "mem"), split_axis=0, concat_axis=0, tiled=True),
    )
    offsets = got_labels[:, 0]
    live = offsets >= 0
    ids_one = jnp.where(live, offsets * codes_two + got_labels[:, 1], -1)
    ids_two = jnp.where(live, offsets * codes_two + got_labels[:, 2], -1)
    squares = jnp.sum(jnp.square(got_rows.astype(jnp.float32)), axis=1)
    block_rows = pick_block(slot_total)
    block_count = slot_total // block_rows
    row_blocks = got_rows.reshape(block_count, block_rows, feat_width)
    cluster_range = jnp.arange(clusters, dtype=jnp.int32)

    def local_totals(cluster_ids):

        def add_block(carry, pieces):
            totals, counts = carry
            block_x, block_ids = pieces
            hot_table = (block_ids[:, None] == cluster_range[None, :]).astype(jnp.bfloat16)
            totals = totals + lax.dot_general(
                hot_table, block_x, (((0,), (0,)), ((), ())), preferred_element_type=jnp.float32
            )
            counts = counts + jnp.sum(hot_table, axis=0, dtype=jnp.float32)
            return ((totals, counts), None)

        start = (
            jnp.zeros((clusters, feat_width), jnp.float32),
            jnp.zeros((clusters,), jnp.float32),
        )
        result, unused = lax.scan(
            add_block, start, (row_blocks, cluster_ids.reshape(block_count, block_rows))
        )
        return result

    start_table = initial_centroids.reshape(clusters, feat_width).astype(jnp.float32)

    def update(earlier, cluster_ids):
        totals, counts = local_totals(cluster_ids)
        totals, counts = over_members(totals, counts)
        centre = (totals + PRIOR * earlier) / (counts[:, None] + PRIOR)
        return (centre, centre.astype(jnp.bfloat16))

    centre_one, rounded_one = update(start_table, ids_one)
    assigned = jnp.take(rounded_one, jnp.maximum(ids_one, 0), axis=0).astype(jnp.float32)
    first_local = (
        squares
        - 2.0 * jnp.sum(got_rows.astype(jnp.float32) * assigned, axis=1)
        + jnp.sum(assigned * assigned, axis=1)
    ) / feat_width
    centre_two, rounded_two = update(centre_one, ids_two)
    centre_squares = jnp.sum(jnp.square(rounded_two.astype(jnp.float32)), axis=1).reshape(
        group_codes, codes_two
    )
    code_range = jnp.arange(group_codes, dtype=jnp.int32)

    def score_block(pieces):
        block_x, block_offsets, block_sq = pieces
        raw = lax.dot_general(
            rounded_two, block_x, (((1,), (1,)), ((), ())), preferred_element_type=jnp.float32
        )
        raw = raw.reshape(group_codes, codes_two, block_rows)
        select = (block_offsets[None, :] == code_range[:, None]).astype(jnp.float32)
        inner = jnp.sum(raw * select[:, None, :], axis=0)
        norms = jnp.sum(centre_squares[:, :, None] * select[:, None, :], axis=0)
        return (block_sq[None, :] - 2.0 * inner + norms) / feat_width

    scored = lax.map(
        score_block,
        (
            row_blocks,
            offsets.reshape(block_count, block_rows),
            squares.reshape(block_count, block_rows),
        ),
    )
    all_local = jnp.transpose(scored, (1, 0, 2)).reshape(codes_two, slot_total)
    one_local = first_local[None, :]
    back_all, back_one = (
        lax.all_to_all(all_local, ("grp", "mem"), split_axis=1, concat_axis=1, tiled=True),
        lax.all_to_all(one_local, ("grp", "mem"), split_axis=1, concat_axis=1, tiled=True),
    )
    distances = jnp.take(back_all, slot_index, axis=1)
    first_distance = jnp.take(back_one[0], slot_index, axis=0)
    return (distances, first_distance)


def quick(embeddings, initial_centroids, row_owner, prefix_offset, first_assign, second_assign):
    rows, feat = embeddings.shape
    group_codes, codes_two = initial_centroids.shape[:2]
    groups = lax.axis_size("grp")
    members = lax.axis_size("mem")
    relay_total = members * BLOCK_RELAY
    code_total = groups * BLOCK_CODE
    shape = jax.ShapeDtypeStruct
    vmem = pl.BlockSpec(memory_space=pltpu.VMEM)

    def swap(array, axis, count):
        blocks = array.reshape(count, array.shape[0] // count, array.shape[1])
        return lax.all_to_all(blocks, axis, split_axis=0, concat_axis=0, tiled=True).reshape(array.shape)

    send, slot = call(
        lambda *refs: pack_kernel(members, group_codes, *refs),
        [shape((relay_total, feat), jnp.bfloat16), shape((1, rows), jnp.int32)],
        [
            row_owner.reshape(1, rows),
            prefix_offset.reshape(1, rows),
            first_assign.reshape(1, rows),
            second_assign.reshape(1, rows),
            embeddings,
        ],
    )
    got = swap(send, "mem", members)
    (send,) = call(relay_kernel, [shape((code_total, feat), jnp.bfloat16)], [got])
    got = swap(send, "grp", groups)
    (record,) = call(
        lambda *refs: code_kernel(members, *refs),
        [shape((groups * members * BLOCK_BACK, LANES), jnp.bfloat16)],
        [got, initial_centroids],
        in_memory=[vmem, pl.BlockSpec(memory_space=pl.ANY)],
        scratch=[
            pltpu.VMEM((codes_two, feat), jnp.bfloat16),
            pltpu.VMEM((LANES, feat), jnp.float32),
            pltpu.SemaphoreType.DMA,
        ],
    )
    back = swap(record, ("grp", "mem"), groups * members)
    return call(
        unpack_kernel,
        [shape((codes_two, rows), jnp.float32), shape((1, rows), jnp.float32), shape((1, 1), jnp.int32)],
        [back, slot],
        out_memory=[vmem, vmem, pl.BlockSpec(memory_space=pltpu.SMEM)],
    )


def body(*inputs):
    distances, first_distance, full = quick(*inputs)
    return lax.cond(
        full[0, 0] > 0,
        lambda kept, given: general(*given),
        lambda kept, given: kept,
        (distances, first_distance[0]),
        inputs,
    )


def solution(mesh):
    placed = (
        P(("grp", "mem"), None),
        P("grp", None, None),
        P(("grp", "mem"), None),
        P(("grp", "mem")),
        P(("grp", "mem")),
        P(("grp", "mem")),
    )
    return jax.shard_map(
        body,
        mesh=mesh,
        in_specs=placed,
        out_specs=(P(None, ("grp", "mem")), P(("grp", "mem"))),
        check_vma=False,
    )
```

```python
import jax
import jax.numpy as jnp
from jax import lax
from jax.experimental import pallas as pl
from jax.experimental.pallas import tpu as pltpu
from jax.sharding import PartitionSpec as P

PRIOR = 16
BLOCK = 32
LANES = 128
SHARE = LANES // BLOCK
CORES = 2
SECTION = 112
FIRST, SECOND, SIDE = 0, 1, 2
ROUNDING_ROW = 4.5e-4
ROUNDING_ALL = 2.5e-4
NT = (((1,), (1,)), ((), ()))
VMEM_LIMIT = 48 * 1024 * 1024


def iota(shape, dim):
    return lax.broadcasted_iota(jnp.int32, shape, dim)


def hot(condition):
    return jnp.where(condition, 1.0, 0.0).astype(jnp.bfloat16)


def dot(a, b):
    return jnp.dot(a, b, preferred_element_type=jnp.float32)


def dot_nt(a, b):
    return lax.dot_general(a, b, NT, preferred_element_type=jnp.float32)


def three_terms(values):
    high = values.astype(jnp.bfloat16)
    rest = values - high.astype(jnp.float32)
    middle = rest.astype(jnp.bfloat16)
    low = (rest - middle.astype(jnp.float32)).astype(jnp.bfloat16)
    return high, middle, low


def call(kernel, out_shape, args, out_memory=None, in_memory=None, scratch=()):
    vmem = pl.BlockSpec(memory_space=pltpu.VMEM)
    return pl.pallas_call(
        kernel,
        out_shape=out_shape,
        in_specs=in_memory or [vmem] * len(args),
        out_specs=out_memory or [vmem] * len(out_shape),
        scratch_shapes=scratch,
        compiler_params=pltpu.CompilerParams(vmem_limit_bytes=VMEM_LIMIT),
    )(*args)


def rank_in_bin(member):
    bins = hot(member)
    before = hot(iota((LANES, LANES), 0) < iota((LANES, LANES), 1))
    base = jnp.zeros((member.shape[0], 1), jnp.float32)
    ranks = []
    for begin in range(0, member.shape[1], LANES):
        piece = bins[:, begin : begin + LANES]
        ranks.append(dot(piece, before) + base)
        base = base + jnp.sum(piece.astype(jnp.float32), axis=1, keepdims=True)
    rank = jnp.concatenate(ranks, axis=1)
    return jnp.sum(jnp.where(member, rank, 0.0), axis=0, keepdims=True)


def column_of(row):
    diagonal = iota((LANES, LANES), 0) == iota((LANES, LANES), 1)
    pieces = []
    for begin in range(0, row.shape[1], LANES):
        piece = jnp.where(diagonal, row[:, begin : begin + LANES], 0.0)
        pieces.append(jnp.sum(piece, axis=1, keepdims=True))
    return jnp.concatenate(pieces, axis=0)


def pack_kernel(members, group_codes, owner_ref, offset_ref, first_ref, second_ref, x_ref, send_ref, slot_ref):
    rows, feat = x_ref.shape
    chips = send_ref.shape[0] // BLOCK
    group = owner_ref[...] // members
    code = group * group_codes + offset_ref[...]
    chip = (group // CORES) * members + code % members
    rank = rank_in_bin(iota((chips, rows), 0) == chip).astype(jnp.int32)
    fits = rank < BLOCK - 1
    full = jnp.max(jnp.where(fits, 0.0, 1.0))
    slot = jnp.where(fits, chip * BLOCK + rank, -1)
    slot_ref[...] = slot
    kind = iota((16, rows), 0)
    labels = jnp.where(kind == FIRST, first_ref[...] + 1, 0)
    labels = jnp.where(kind == SECOND, second_ref[...], labels)
    labels = jnp.where(kind == SIDE, group % CORES, labels)
    labels = labels.astype(jnp.float32).astype(jnp.bfloat16)
    turn = lax.axis_index("mem") % SHARE
    old, new = iota((LANES, SHARE * LANES), 0), iota((LANES, SHARE * LANES), 1)
    move = hot((old // BLOCK == new // LANES) & (new % LANES == turn * BLOCK + old % BLOCK))
    x = x_ref[...]
    full_row = jnp.full((1, feat - 3 * LANES), full, jnp.float32)
    is_last = iota((BLOCK, feat), 0) == BLOCK - 1
    for begin in range(0, chips * BLOCK, LANES):
        chosen = hot(iota((LANES, rows), 0) + begin == slot)
        moved = dot(chosen, x)
        kinds = dot(dot_nt(labels, chosen).astype(jnp.bfloat16), move)
        for part in range(SHARE):
            own = kinds[:, part * LANES : (part + 1) * LANES]
            last = [own[kind : kind + 1] for kind in (FIRST, SECOND, SIDE)] + [full_row]
            last = jnp.concatenate(last, axis=1)
            block = jnp.where(is_last, last, moved[part * BLOCK : (part + 1) * BLOCK])
            at = begin + part * BLOCK
            send_ref[at : at + BLOCK, :] = block.astype(jnp.bfloat16)


def row_of(column):
    diagonal = iota((LANES, LANES), 0) == iota((LANES, LANES), 1)
    return jnp.sum(jnp.where(diagonal, column, 0.0), axis=0, keepdims=True)


def sums_kernel(members, got_ref, start_ref, part_ref, label_ref, mine, sem):
    total, feat = got_ref.shape
    group_codes, codes_two = start_ref.shape[:2]
    offset = (lax.axis_index("mem") + members * group_codes - group_codes * lax.axis_index("grp")) % members
    fetch = pltpu.make_async_copy(start_ref.at[jnp.minimum(offset, group_codes - 1)], mine, sem)
    fetch.start()
    chunks = []
    for begin in range(0, total, LANES):
        row = jnp.zeros((1, feat), jnp.float32)
        for at in range(begin, begin + LANES, BLOCK):
            row = row + got_ref[at + BLOCK - 8 : at + BLOCK, :].astype(jnp.float32)[7:8, :]
        chunks.append(row)

    def along(kind):
        return jnp.concatenate([row[:, kind * LANES : (kind + 1) * LANES] for row in chunks], axis=1)

    side = along(SIDE)
    first = along(FIRST) - 1.0
    second = jnp.where(first >= 0.0, along(SECOND) + side * LANES, -1.0)
    full = jnp.maximum(jnp.max(sum(row[:, 3 * LANES : 3 * LANES + 1] for row in chunks)), 0.0)
    label_ref[...] = jnp.concatenate([first, side, jnp.zeros((6, total), jnp.float32)], axis=0)
    first = jnp.where(first >= 0.0, first + side * LANES, -1.0)
    x = got_ref[...]
    cluster = iota((CORES * LANES, total), 0).astype(jnp.float32)
    is_count = iota((SECTION, feat), 0) == SECTION - 1
    for update, assigned in enumerate((first, second)):
        member = hot(cluster == assigned)
        totals = dot(member, x)
        counts = jnp.sum(member.astype(jnp.float32), axis=1, keepdims=True)
        for core in range(CORES):
            count = row_of(counts[core * LANES : (core + 1) * LANES])
            large = jnp.floor(count * (1.0 / LANES))
            count = [large, count - large * LANES, jnp.full((1, feat - 2 * LANES), full, jnp.float32)]
            section = jnp.where(
                is_count,
                jnp.concatenate(count, axis=1),
                totals[core * LANES : core * LANES + SECTION],
            )
            at = (update * CORES + core) * SECTION
            part_ref[at : at + SECTION, :] = section.astype(jnp.bfloat16)
    fetch.wait()
    at = 2 * CORES * SECTION
    part_ref[at : at + SECTION, :] = jnp.zeros((SECTION, feat), jnp.bfloat16)
    part_ref[at : at + codes_two, :] = mine[...]


def score_kernel(codes_two, got_ref, own_ref, other_ref, label_ref, out_ref):
    total, feat = got_ref.shape
    my_core = lax.axis_index("grp") % CORES
    count_row = SECTION - 1

    def both(at):
        own = own_ref[at : at + SECTION, :].astype(jnp.float32)
        return own + other_ref[at : at + SECTION, :].astype(jnp.float32)

    full = jnp.zeros((1, 1), jnp.float32)
    rounded, squares_of = [], []
    at = 2 * CORES * SECTION
    starts = [ref[at : at + SECTION, :].astype(jnp.float32) for ref in (own_ref, other_ref)]
    for core in range(CORES):
        centre = jnp.where(my_core == core, starts[0], starts[1])
        for update in range(2):
            sums = both((update * CORES + core) * SECTION)
            counts = sums[count_row : count_row + 1]
            full = jnp.maximum(full, counts[:, 2 * LANES : 2 * LANES + 1])
            counts = column_of(counts[:, :LANES] * LANES + counts[:, LANES : 2 * LANES])
            centre = (sums + PRIOR * centre) / (counts[:SECTION] + PRIOR)
            narrow = jnp.concatenate(
                [centre.astype(jnp.bfloat16), jnp.zeros((LANES - SECTION, feat), jnp.bfloat16)], axis=0
            )
            wide = narrow.astype(jnp.float32)
            rounded.append(narrow)
            squares_of.append(row_of(jnp.sum(wide * wide, axis=1, keepdims=True)))
    full = jnp.max(full)
    table = jnp.concatenate(rounded, axis=0)
    lane = iota((LANES, LANES), 1)
    lost_all = jnp.zeros((LANES, 1), jnp.float32)
    sent_all = jnp.zeros((LANES, 1), jnp.float32)
    over = jnp.zeros((LANES, 1), jnp.float32)
    records = []
    for begin in range(0, total, LANES):
        x = got_ref[begin : begin + LANES, :]
        first = column_of(label_ref[0:1, begin : begin + LANES])
        is_other = column_of(label_ref[1:2, begin : begin + LANES]) > 0.5
        wide = x.astype(jnp.float32)
        squares = jnp.sum(wide * wide, axis=1, keepdims=True)
        inner = dot_nt(x, table)

        def distance(update):
            low, high = [
                squares_of[at] - 2.0 * inner[:, at * LANES : (at + 1) * LANES]
                for at in (update, 2 + update)
            ]
            return (squares + jnp.where(is_other, high, low)) / feat

        near = jnp.where(lane.astype(jnp.float32) == first, distance(0), 0.0)
        near = jnp.sum(near, axis=1, keepdims=True)
        score = jnp.where(lane < codes_two, distance(1), 0.0)
        mean = jnp.sum(score, axis=1, keepdims=True) / codes_two
        rest = jnp.where(lane < codes_two, score - mean, 0.0)
        record = rest.astype(jnp.bfloat16)
        lost = rest - record.astype(jnp.float32)
        is_live = first >= 0.0
        lost = jnp.where(is_live, jnp.sum(lost * lost, axis=1, keepdims=True), 0.0)
        sent = jnp.where(is_live, jnp.sum(score * score, axis=1, keepdims=True), 0.0)
        over = jnp.maximum(over, jnp.where(lost > (ROUNDING_ROW * ROUNDING_ROW) * sent, 1.0, 0.0))
        lost_all = lost_all + lost
        sent_all = sent_all + sent
        for place, term in enumerate(three_terms(mean) + three_terms(near)):
            record = jnp.where(lane == codes_two + place, term, record)
        records.append(record)
    over_all = jnp.sum(lost_all) > (ROUNDING_ALL * ROUNDING_ALL) * jnp.sum(sent_all)
    full = jnp.maximum(full, jnp.maximum(jnp.max(over), jnp.where(over_all, 1.0, 0.0)))
    for at, record in enumerate(records):
        record = jnp.where(lane == LANES - 1, full.astype(jnp.bfloat16), record)
        out_ref[at * LANES : (at + 1) * LANES, :] = record


def unpack_kernel(got_ref, slot_ref, all_ref, one_ref):
    total = got_ref.shape[0]
    rows = slot_ref.shape[1]
    codes_two = all_ref.shape[0]
    chosen = hot(iota((total, rows), 0) == slot_ref[...])
    moved = dot(got_ref[...].T, chosen)
    mean, near = [
        moved[begin : begin + 1] + (moved[begin + 1 : begin + 2] + moved[begin + 2 : begin + 3])
        for begin in (codes_two, codes_two + 3)
    ]
    all_ref[...] = moved[:codes_two] + mean
    one_ref[...] = near


def over_members(totals, counts):
    members = lax.axis_size("mem")
    clusters, feat = totals.shape
    share = -(-clusters // members)

    def swap(blocks):
        return lax.all_to_all(blocks, "mem", split_axis=0, concat_axis=0, tiled=True)

    padded = jnp.pad(totals.astype(jnp.bfloat16), ((0, members * share - clusters), (0, 0)))
    own = jnp.sum(swap(padded.reshape(members, share, feat)).astype(jnp.float32), axis=0)
    own = jnp.broadcast_to(own.astype(jnp.bfloat16)[None], (members, share, feat))
    summed = swap(own).reshape(members * share, feat)[:clusters].astype(jnp.float32)
    counted = jnp.sum(swap(jnp.broadcast_to(counts[None], (members, clusters))), axis=0)
    return summed, counted


def pick_block(total):
    for candidate in range(1024, 0, -1):
        if total % candidate == 0:
            return candidate
    return total


def general(embeddings, initial_centroids, row_owner, prefix_offset, first_assign, second_assign):
    row_count, feat_width = embeddings.shape
    group_codes = initial_centroids.shape[0]
    codes_two = initial_centroids.shape[1]
    clusters = group_codes * codes_two
    group_count = lax.axis_size("grp")
    member_count = lax.axis_size("mem")
    devices_all = group_count * member_count
    capacity = 2 * row_count // devices_all + 4
    slot_total = devices_all * capacity
    target = row_owner[:, 0]
    dest_table = (target[:, None] == jnp.arange(devices_all, dtype=jnp.int32)[None, :]).astype(
        jnp.int32
    )
    slot_rank = jnp.sum(jnp.cumsum(dest_table, axis=0) * dest_table, axis=1) - 1
    slot_index = target * capacity + slot_rank
    send_rows = jnp.zeros((slot_total, feat_width), jnp.bfloat16).at[slot_index].set(embeddings)
    labels = jnp.stack([prefix_offset, first_assign, second_assign], axis=1)
    send_labels = jnp.full((slot_total, 3), -1, jnp.int32).at[slot_index].set(labels)
    got_rows, got_labels = (
        lax.all_to_all(send_rows, ("grp", "mem"), split_axis=0, concat_axis=0, tiled=True),
        lax.all_to_all(send_labels, ("grp", "mem"), split_axis=0, concat_axis=0, tiled=True),
    )
    offsets = got_labels[:, 0]
    live = offsets >= 0
    ids_one = jnp.where(live, offsets * codes_two + got_labels[:, 1], -1)
    ids_two = jnp.where(live, offsets * codes_two + got_labels[:, 2], -1)
    squares = jnp.sum(jnp.square(got_rows.astype(jnp.float32)), axis=1)
    block_rows = pick_block(slot_total)
    block_count = slot_total // block_rows
    row_blocks = got_rows.reshape(block_count, block_rows, feat_width)
    cluster_range = jnp.arange(clusters, dtype=jnp.int32)

    def local_totals(cluster_ids):

        def add_block(carry, pieces):
            totals, counts = carry
            block_x, block_ids = pieces
            hot_table = (block_ids[:, None] == cluster_range[None, :]).astype(jnp.bfloat16)
            totals = totals + lax.dot_general(
                hot_table, block_x, (((0,), (0,)), ((), ())), preferred_element_type=jnp.float32
            )
            counts = counts + jnp.sum(hot_table, axis=0, dtype=jnp.float32)
            return ((totals, counts), None)

        start = (
            jnp.zeros((clusters, feat_width), jnp.float32),
            jnp.zeros((clusters,), jnp.float32),
        )
        result, unused = lax.scan(
            add_block, start, (row_blocks, cluster_ids.reshape(block_count, block_rows))
        )
        return result

    start_table = initial_centroids.reshape(clusters, feat_width).astype(jnp.float32)

    def update(earlier, cluster_ids):
        totals, counts = local_totals(cluster_ids)
        totals, counts = over_members(totals, counts)
        centre = (totals + PRIOR * earlier) / (counts[:, None] + PRIOR)
        return (centre, centre.astype(jnp.bfloat16))

    centre_one, rounded_one = update(start_table, ids_one)
    assigned = jnp.take(rounded_one, jnp.maximum(ids_one, 0), axis=0).astype(jnp.float32)
    first_local = (
        squares
        - 2.0 * jnp.sum(got_rows.astype(jnp.float32) * assigned, axis=1)
        + jnp.sum(assigned * assigned, axis=1)
    ) / feat_width
    centre_two, rounded_two = update(centre_one, ids_two)
    centre_squares = jnp.sum(jnp.square(rounded_two.astype(jnp.float32)), axis=1).reshape(
        group_codes, codes_two
    )
    code_range = jnp.arange(group_codes, dtype=jnp.int32)

    def score_block(pieces):
        block_x, block_offsets, block_sq = pieces
        raw = lax.dot_general(
            rounded_two, block_x, (((1,), (1,)), ((), ())), preferred_element_type=jnp.float32
        )
        raw = raw.reshape(group_codes, codes_two, block_rows)
        select = (block_offsets[None, :] == code_range[:, None]).astype(jnp.float32)
        inner = jnp.sum(raw * select[:, None, :], axis=0)
        norms = jnp.sum(centre_squares[:, :, None] * select[:, None, :], axis=0)
        return (block_sq[None, :] - 2.0 * inner + norms) / feat_width

    scored = lax.map(
        score_block,
        (
            row_blocks,
            offsets.reshape(block_count, block_rows),
            squares.reshape(block_count, block_rows),
        ),
    )
    all_local = jnp.transpose(scored, (1, 0, 2)).reshape(codes_two, slot_total)
    one_local = first_local[None, :]
    back_all, back_one = (
        lax.all_to_all(all_local, ("grp", "mem"), split_axis=1, concat_axis=1, tiled=True),
        lax.all_to_all(one_local, ("grp", "mem"), split_axis=1, concat_axis=1, tiled=True),
    )
    distances = jnp.take(back_all, slot_index, axis=1)
    first_distance = jnp.take(back_one[0], slot_index, axis=0)
    return (distances, first_distance)


def quick(embeddings, initial_centroids, row_owner, prefix_offset, first_assign, second_assign):
    rows, feat = embeddings.shape
    group_codes, codes_two = initial_centroids.shape[:2]
    groups = lax.axis_size("grp")
    members = lax.axis_size("mem")
    chips = groups // CORES * members
    total = chips * BLOCK
    shape = jax.ShapeDtypeStruct
    vmem = pl.BlockSpec(memory_space=pltpu.VMEM)
    same_core = [
        [group * members + member for group in range(core, groups, CORES) for member in range(members)]
        for core in range(CORES)
    ]

    def swap(array):
        blocks = array.reshape(chips, array.shape[0] // chips, array.shape[1])
        blocks = lax.all_to_all(
            blocks, ("grp", "mem"), split_axis=0, concat_axis=0, axis_index_groups=same_core, tiled=True
        )
        return blocks.reshape(array.shape)

    def other_core(array):
        return lax.ppermute(array, "grp", [(group, group ^ 1) for group in range(groups)])

    send, slot = call(
        lambda *refs: pack_kernel(members, group_codes, *refs),
        [shape((total, feat), jnp.bfloat16), shape((1, rows), jnp.int32)],
        [
            row_owner.reshape(1, rows),
            prefix_offset.reshape(1, rows),
            first_assign.reshape(1, rows),
            second_assign.reshape(1, rows),
            embeddings,
        ],
    )
    got = swap(send)
    part, label = call(
        lambda *refs: sums_kernel(members, *refs),
        [shape(((2 * CORES + 1) * SECTION, feat), jnp.bfloat16), shape((8, total), jnp.float32)],
        [got, initial_centroids],
        in_memory=[vmem, pl.BlockSpec(memory_space=pl.ANY)],
        scratch=[pltpu.VMEM((codes_two, feat), jnp.bfloat16), pltpu.SemaphoreType.DMA],
    )
    (record,) = call(
        lambda *refs: score_kernel(codes_two, *refs),
        [shape((total, LANES), jnp.bfloat16)],
        [got, part, other_core(part), label],
    )
    back = swap(record)
    full = jnp.max(back[:, LANES - 1 :].astype(jnp.float32), axis=0, keepdims=True)
    full = jnp.maximum(full, other_core(full))
    distances, first_distance = call(
        unpack_kernel,
        [shape((codes_two, rows), jnp.float32), shape((1, rows), jnp.float32)],
        [back, slot],
    )
    return distances, first_distance, full


def body(*inputs):
    distances, first_distance, full = quick(*inputs)
    return lax.cond(
        full[0, 0] > 0.5,
        lambda kept, given: general(*given),
        lambda kept, given: kept,
        (distances, first_distance[0]),
        inputs,
    )


def solution(mesh):
    placed = (
        P(("grp", "mem"), None),
        P("grp", None, None),
        P(("grp", "mem"), None),
        P(("grp", "mem")),
        P(("grp", "mem")),
        P(("grp", "mem")),
    )
    return jax.shard_map(
        body,
        mesh=mesh,
        in_specs=placed,
        out_specs=(P(None, ("grp", "mem")), P(("grp", "mem"))),
        check_vma=False,
    )
```

```python
import jax
import jax.numpy as jnp
from jax import lax
from jax.experimental import pallas as pl
from jax.experimental.pallas import tpu as pltpu
from jax.sharding import PartitionSpec as P

PRIOR = 16
BLOCK = 32
LANES = 128
SHARE = LANES // BLOCK
CORES = 2
ROWS_STEP = 512
STEP_SCORE = 512
SECTION = 112
FIRST, SECOND, SIDE = 0, 1, 2
ROUNDING_BLOCK = 4.5e-4
ROUNDING_ALL = 2.5e-4
NT = (((1,), (1,)), ((), ()))
VMEM_LIMIT = 48 * 1024 * 1024


def iota(shape, dim):
    return lax.broadcasted_iota(jnp.int32, shape, dim)


def hot(condition):
    return jnp.where(condition, 1.0, 0.0).astype(jnp.bfloat16)


def dot(a, b):
    return jnp.dot(a, b, preferred_element_type=jnp.float32)


def dot_nt(a, b):
    return lax.dot_general(a, b, NT, preferred_element_type=jnp.float32)


def three_terms(values):
    high = values.astype(jnp.bfloat16)
    rest = values - high.astype(jnp.float32)
    middle = rest.astype(jnp.bfloat16)
    low = (rest - middle.astype(jnp.float32)).astype(jnp.bfloat16)
    return high, middle, low


def call(kernel, out_shape, args, out_memory=None, in_memory=None, scratch=()):
    vmem = pl.BlockSpec(memory_space=pltpu.VMEM)
    return pl.pallas_call(
        kernel,
        out_shape=out_shape,
        in_specs=in_memory or [vmem] * len(args),
        out_specs=out_memory or [vmem] * len(out_shape),
        scratch_shapes=scratch,
        compiler_params=pltpu.CompilerParams(vmem_limit_bytes=VMEM_LIMIT),
    )(*args)


def rank_in_bin(member):
    bins = hot(member)
    before = hot(iota((LANES, LANES), 0) < iota((LANES, LANES), 1))
    base = jnp.zeros((member.shape[0], 1), jnp.float32)
    ranks = []
    for begin in range(0, member.shape[1], LANES):
        piece = bins[:, begin : begin + LANES]
        ranks.append(dot(piece, before) + base)
        base = base + jnp.sum(piece.astype(jnp.float32), axis=1, keepdims=True)
    rank = jnp.concatenate(ranks, axis=1)
    return jnp.sum(jnp.where(member, rank, 0.0), axis=0, keepdims=True)


def column_of(row):
    diagonal = iota((LANES, LANES), 0) == iota((LANES, LANES), 1)
    pieces = []
    for begin in range(0, row.shape[1], LANES):
        piece = jnp.where(diagonal, row[:, begin : begin + LANES], 0.0)
        pieces.append(jnp.sum(piece, axis=1, keepdims=True))
    return jnp.concatenate(pieces, axis=0)


def pack_kernel(members, group_codes, owner_ref, offset_ref, first_ref, second_ref, x_ref, send_ref, slot_ref):
    rows, feat = x_ref.shape
    chips = send_ref.shape[0] // BLOCK
    group = owner_ref[...] // members
    code = group * group_codes + offset_ref[...]
    chip = (group // CORES) * members + code % members
    rank = rank_in_bin(iota((chips, rows), 0) == chip).astype(jnp.int32)
    fits = rank < BLOCK - 1
    full = jnp.max(jnp.where(fits, 0.0, 1.0))
    slot = jnp.where(fits, chip * BLOCK + rank, -1)
    slot_ref[...] = slot
    labels = (first_ref[...] + 1) + LANES * second_ref[...] + LANES * LANES * (group % CORES)
    label_column = column_of(labels.astype(jnp.float32))
    slot_column = column_of(slot.astype(jnp.float32))
    x = x_ref[...]
    turn = lax.axis_index("mem") % SHARE
    lane = iota((8, LANES), 1)
    kind = iota((8, LANES), 0)
    full_row = jnp.full((1, feat - 3 * LANES), full, jnp.float32)
    half = BLOCK // 2
    is_last = iota((half, feat), 0) == half - 1
    lane_row = iota((1, LANES), 1).astype(jnp.float32)
    for begin in range(0, chips * BLOCK, ROWS_STEP):
        moved = dot(hot(iota((ROWS_STEP, rows), 0) + begin == slot), x)
        for inside in range(0, ROWS_STEP, LANES):
            packed = jnp.where(slot_column == lane_row + (begin + inside), label_column, 0.0)
            packed = jnp.sum(packed, axis=0, keepdims=True).astype(jnp.int32)
            kinds = jnp.where(kind == FIRST, packed % LANES, (packed // LANES) % LANES)
            kinds = jnp.where(kind == SIDE, packed // (LANES * LANES), kinds).astype(jnp.float32)
            for part in range(SHARE):
                own = pltpu.roll(kinds, ((turn - part + SHARE) % SHARE) * BLOCK, 1)
                own = jnp.where(lane // BLOCK == turn, own, 0.0)
                last = [own[kind : kind + 1] for kind in (FIRST, SECOND, SIDE)] + [full_row]
                last = jnp.concatenate(last, axis=1)
                at = inside + part * BLOCK
                send_ref[begin + at : begin + at + half, :] = moved[at : at + half].astype(jnp.bfloat16)
                at = at + half
                block = jnp.where(is_last, last, moved[at : at + half])
                send_ref[begin + at : begin + at + half, :] = block.astype(jnp.bfloat16)


def row_of(column):
    diagonal = iota((LANES, LANES), 0) == iota((LANES, LANES), 1)
    return jnp.sum(jnp.where(diagonal, column, 0.0), axis=0, keepdims=True)


def sums_kernel(members, got_ref, start_ref, part_ref, label_ref, mine, sem):
    total, feat = got_ref.shape
    group_codes, codes_two = start_ref.shape[:2]
    offset = (lax.axis_index("mem") + members * group_codes - group_codes * lax.axis_index("grp")) % members
    fetch = pltpu.make_async_copy(start_ref.at[jnp.minimum(offset, group_codes - 1)], mine, sem)
    fetch.start()
    chunks = []
    for begin in range(0, total, LANES):
        row = jnp.zeros((1, feat), jnp.float32)
        for at in range(begin, begin + LANES, BLOCK):
            row = row + got_ref[at + BLOCK - 8 : at + BLOCK, :].astype(jnp.float32)[7:8, :]
        chunks.append(row)

    def along(kind):
        return jnp.concatenate([row[:, kind * LANES : (kind + 1) * LANES] for row in chunks], axis=1)

    side = along(SIDE)
    first = along(FIRST) - 1.0
    second = jnp.where(first >= 0.0, along(SECOND) + side * LANES, -1.0)
    full = jnp.maximum(jnp.max(sum(row[:, 3 * LANES : 3 * LANES + 1] for row in chunks)), 0.0)
    first = jnp.where(first >= 0.0, first + side * LANES, -1.0)
    label_ref[...] = jnp.broadcast_to(first, (8, total))
    x = got_ref[...]
    cluster = iota((CORES * LANES, total), 0).astype(jnp.float32)
    is_count = iota((SECTION, feat), 0) == SECTION - 1
    for update, assigned in enumerate((first, second)):
        member = hot(cluster == assigned)
        totals = dot(member, x)
        counts = jnp.sum(member.astype(jnp.float32), axis=1, keepdims=True)
        for core in range(CORES):
            count = row_of(counts[core * LANES : (core + 1) * LANES])
            large = jnp.floor(count * (1.0 / LANES))
            count = [large, count - large * LANES, jnp.full((1, feat - 2 * LANES), full, jnp.float32)]
            section = jnp.where(
                is_count,
                jnp.concatenate(count, axis=1),
                totals[core * LANES : core * LANES + SECTION],
            )
            at = (update * CORES + core) * SECTION
            part_ref[at : at + SECTION, :] = section.astype(jnp.bfloat16)
    fetch.wait()
    at = 2 * CORES * SECTION
    part_ref[at : at + SECTION, :] = jnp.zeros((SECTION, feat), jnp.bfloat16)
    part_ref[at : at + codes_two, :] = mine[...]


def score_kernel(codes_two, got_ref, own_ref, other_ref, label_ref, out_ref):
    total, feat = got_ref.shape
    my_core = lax.axis_index("grp") % CORES
    count_row = SECTION - 1

    def both(at):
        own = own_ref[at : at + SECTION, :].astype(jnp.float32)
        return own + other_ref[at : at + SECTION, :].astype(jnp.float32)

    full = jnp.zeros((1, 1), jnp.float32)
    rounded, squares_of = [], []
    at = 2 * CORES * SECTION
    starts = [ref[at : at + SECTION, :].astype(jnp.float32) for ref in (own_ref, other_ref)]
    for core in range(CORES):
        centre = jnp.where(my_core == core, starts[0], starts[1])
        for update in range(2):
            sums = both((update * CORES + core) * SECTION)
            counts = sums[count_row : count_row + 1]
            full = jnp.maximum(full, counts[:, 2 * LANES : 2 * LANES + 1])
            counts = column_of(counts[:, :LANES] * LANES + counts[:, LANES : 2 * LANES])
            centre = (sums + PRIOR * centre) * (1.0 / (counts[:SECTION] + PRIOR))
            narrow = jnp.concatenate(
                [centre.astype(jnp.bfloat16), jnp.zeros((LANES - SECTION, feat), jnp.bfloat16)], axis=0
            )
            wide = narrow.astype(jnp.float32)
            rounded.append(narrow)
            squares_of.append(row_of(jnp.sum(wide * wide, axis=1, keepdims=True)) * (1.0 / feat))
    full = jnp.max(full)
    table = jnp.concatenate(rounded, axis=0)
    lane = iota((STEP_SCORE, LANES), 1)
    is_score = lane < codes_two
    lane_value = lane.astype(jnp.float32)
    diagonal = iota((LANES, LANES), 0) == iota((LANES, LANES), 1)
    ones = jnp.ones((LANES, LANES), jnp.bfloat16)
    spread = iota((2 * LANES, LANES), 0) // LANES
    spread = hot(iota((2 * LANES, LANES), 1) == codes_two + 1 + spread)
    excess_all = jnp.zeros((STEP_SCORE, LANES), jnp.float32)
    excess_block = []

    def across(values):
        return dot(values.astype(jnp.bfloat16), ones)

    for begin in range(0, total, STEP_SCORE):
        x = got_ref[begin : begin + STEP_SCORE, :]
        inner = dot_nt(x, table)
        key = [
            jnp.where(diagonal, label_ref[0:1, at : at + LANES], 0.0)
            for at in range(begin, begin + STEP_SCORE, LANES)
        ]
        key = across(jnp.concatenate(key, axis=0))
        is_other = key >= LANES
        first = jnp.where(is_other, key - LANES, key)
        wide = x.astype(jnp.float32)
        squares = jnp.sum(wide * wide, axis=1, keepdims=True) * (1.0 / feat)

        def distance(update):
            low, high = [
                squares_of[at] - (2.0 / feat) * inner[:, at * LANES : (at + 1) * LANES]
                for at in (update, 2 + update)
            ]
            return squares + jnp.where(is_other, high, low)

        near = jnp.where(lane_value == first, distance(0), 0.0)
        near_high = near.astype(jnp.bfloat16)
        near_low = (near - near_high.astype(jnp.float32)).astype(jnp.bfloat16)
        score = jnp.where(is_score, distance(1), 0.0)
        mean = (across(score) * (1.0 / codes_two)).astype(jnp.bfloat16).astype(jnp.float32)
        rest = jnp.where(is_score, score - mean, 0.0)
        record = rest.astype(jnp.bfloat16).astype(jnp.float32)
        lost = rest - record
        is_live = key >= 0.0
        lost = jnp.where(is_live, lost * lost, 0.0)
        sent = jnp.where(is_live, score * score, 0.0)
        excess_all = excess_all + (lost - (ROUNDING_ALL * ROUNDING_ALL) * sent)
        excess = lost - (ROUNDING_BLOCK * ROUNDING_BLOCK) * sent
        excess = jnp.sum(excess.reshape(STEP_SCORE // BLOCK, BLOCK // 8, 8, LANES), axis=1)
        excess_block.append(excess.reshape(STEP_SCORE // BLOCK * 8, LANES))
        near = dot(jnp.concatenate([near_high, near_low], axis=1), spread)
        record = jnp.where(lane == codes_two, mean, record + near)
        out_ref[begin : begin + STEP_SCORE, :] = record.astype(jnp.bfloat16)
    excess = across(jnp.concatenate(excess_block, axis=0))
    excess = jnp.sum(excess.reshape(total // BLOCK, 8, LANES), axis=1)
    full = jnp.maximum(full, jnp.where(jnp.max(excess) > 0.0, 1.0, 0.0))
    full = jnp.maximum(full, jnp.where(jnp.sum(excess_all) > 0.0, 1.0, 0.0))
    for begin in range(0, total, BLOCK):
        tile = out_ref[begin : begin + 16, :].astype(jnp.float32)
        tile = jnp.where(iota((16, LANES), 1) == LANES - 1, full, tile)
        out_ref[begin : begin + 16, :] = tile.astype(jnp.bfloat16)


def unpack_kernel(got_ref, slot_ref, all_ref, one_ref):
    total = got_ref.shape[0]
    rows = slot_ref.shape[1]
    codes_two = all_ref.shape[0]
    chosen = hot(iota((total, rows), 0) == slot_ref[...])
    moved = dot(got_ref[...].T, chosen)
    mean = moved[codes_two : codes_two + 1]
    near = moved[codes_two + 1 : codes_two + 2] + moved[codes_two + 2 : codes_two + 3]
    all_ref[...] = moved[:codes_two] + mean
    one_ref[...] = near


def over_members(totals, counts):
    members = lax.axis_size("mem")
    clusters, feat = totals.shape
    share = -(-clusters // members)

    def swap(blocks):
        return lax.all_to_all(blocks, "mem", split_axis=0, concat_axis=0, tiled=True)

    padded = jnp.pad(totals.astype(jnp.bfloat16), ((0, members * share - clusters), (0, 0)))
    own = jnp.sum(swap(padded.reshape(members, share, feat)).astype(jnp.float32), axis=0)
    own = jnp.broadcast_to(own.astype(jnp.bfloat16)[None], (members, share, feat))
    summed = swap(own).reshape(members * share, feat)[:clusters].astype(jnp.float32)
    counted = jnp.sum(swap(jnp.broadcast_to(counts[None], (members, clusters))), axis=0)
    return summed, counted


def pick_block(total):
    for candidate in range(1024, 0, -1):
        if total % candidate == 0:
            return candidate
    return total


def general(embeddings, initial_centroids, row_owner, prefix_offset, first_assign, second_assign):
    row_count, feat_width = embeddings.shape
    group_codes = initial_centroids.shape[0]
    codes_two = initial_centroids.shape[1]
    clusters = group_codes * codes_two
    group_count = lax.axis_size("grp")
    member_count = lax.axis_size("mem")
    devices_all = group_count * member_count
    capacity = 2 * row_count // devices_all + 4
    slot_total = devices_all * capacity
    target = row_owner[:, 0]
    dest_table = (target[:, None] == jnp.arange(devices_all, dtype=jnp.int32)[None, :]).astype(
        jnp.int32
    )
    slot_rank = jnp.sum(jnp.cumsum(dest_table, axis=0) * dest_table, axis=1) - 1
    slot_index = target * capacity + slot_rank
    send_rows = jnp.zeros((slot_total, feat_width), jnp.bfloat16).at[slot_index].set(embeddings)
    labels = jnp.stack([prefix_offset, first_assign, second_assign], axis=1)
    send_labels = jnp.full((slot_total, 3), -1, jnp.int32).at[slot_index].set(labels)
    got_rows, got_labels = (
        lax.all_to_all(send_rows, ("grp", "mem"), split_axis=0, concat_axis=0, tiled=True),
        lax.all_to_all(send_labels, ("grp", "mem"), split_axis=0, concat_axis=0, tiled=True),
    )
    offsets = got_labels[:, 0]
    live = offsets >= 0
    ids_one = jnp.where(live, offsets * codes_two + got_labels[:, 1], -1)
    ids_two = jnp.where(live, offsets * codes_two + got_labels[:, 2], -1)
    squares = jnp.sum(jnp.square(got_rows.astype(jnp.float32)), axis=1)
    block_rows = pick_block(slot_total)
    block_count = slot_total // block_rows
    row_blocks = got_rows.reshape(block_count, block_rows, feat_width)
    cluster_range = jnp.arange(clusters, dtype=jnp.int32)

    def local_totals(cluster_ids):

        def add_block(carry, pieces):
            totals, counts = carry
            block_x, block_ids = pieces
            hot_table = (block_ids[:, None] == cluster_range[None, :]).astype(jnp.bfloat16)
            totals = totals + lax.dot_general(
                hot_table, block_x, (((0,), (0,)), ((), ())), preferred_element_type=jnp.float32
            )
            counts = counts + jnp.sum(hot_table, axis=0, dtype=jnp.float32)
            return ((totals, counts), None)

        start = (
            jnp.zeros((clusters, feat_width), jnp.float32),
            jnp.zeros((clusters,), jnp.float32),
        )
        result, unused = lax.scan(
            add_block, start, (row_blocks, cluster_ids.reshape(block_count, block_rows))
        )
        return result

    start_table = initial_centroids.reshape(clusters, feat_width).astype(jnp.float32)

    def update(earlier, cluster_ids):
        totals, counts = local_totals(cluster_ids)
        totals, counts = over_members(totals, counts)
        centre = (totals + PRIOR * earlier) / (counts[:, None] + PRIOR)
        return (centre, centre.astype(jnp.bfloat16))

    centre_one, rounded_one = update(start_table, ids_one)
    assigned = jnp.take(rounded_one, jnp.maximum(ids_one, 0), axis=0).astype(jnp.float32)
    first_local = (
        squares
        - 2.0 * jnp.sum(got_rows.astype(jnp.float32) * assigned, axis=1)
        + jnp.sum(assigned * assigned, axis=1)
    ) / feat_width
    centre_two, rounded_two = update(centre_one, ids_two)
    centre_squares = jnp.sum(jnp.square(rounded_two.astype(jnp.float32)), axis=1).reshape(
        group_codes, codes_two
    )
    code_range = jnp.arange(group_codes, dtype=jnp.int32)

    def score_block(pieces):
        block_x, block_offsets, block_sq = pieces
        raw = lax.dot_general(
            rounded_two, block_x, (((1,), (1,)), ((), ())), preferred_element_type=jnp.float32
        )
        raw = raw.reshape(group_codes, codes_two, block_rows)
        select = (block_offsets[None, :] == code_range[:, None]).astype(jnp.float32)
        inner = jnp.sum(raw * select[:, None, :], axis=0)
        norms = jnp.sum(centre_squares[:, :, None] * select[:, None, :], axis=0)
        return (block_sq[None, :] - 2.0 * inner + norms) / feat_width

    scored = lax.map(
        score_block,
        (
            row_blocks,
            offsets.reshape(block_count, block_rows),
            squares.reshape(block_count, block_rows),
        ),
    )
    all_local = jnp.transpose(scored, (1, 0, 2)).reshape(codes_two, slot_total)
    one_local = first_local[None, :]
    back_all, back_one = (
        lax.all_to_all(all_local, ("grp", "mem"), split_axis=1, concat_axis=1, tiled=True),
        lax.all_to_all(one_local, ("grp", "mem"), split_axis=1, concat_axis=1, tiled=True),
    )
    distances = jnp.take(back_all, slot_index, axis=1)
    first_distance = jnp.take(back_one[0], slot_index, axis=0)
    return (distances, first_distance)


def quick(embeddings, initial_centroids, row_owner, prefix_offset, first_assign, second_assign):
    rows, feat = embeddings.shape
    group_codes, codes_two = initial_centroids.shape[:2]
    groups = lax.axis_size("grp")
    members = lax.axis_size("mem")
    chips = groups // CORES * members
    total = chips * BLOCK
    shape = jax.ShapeDtypeStruct
    vmem = pl.BlockSpec(memory_space=pltpu.VMEM)
    same_core = [
        [group * members + member for group in range(core, groups, CORES) for member in range(members)]
        for core in range(CORES)
    ]

    def swap(array):
        blocks = array.reshape(chips, array.shape[0] // chips, array.shape[1])
        blocks = lax.all_to_all(
            blocks, ("grp", "mem"), split_axis=0, concat_axis=0, axis_index_groups=same_core, tiled=True
        )
        return blocks.reshape(array.shape)

    def other_core(array):
        return lax.ppermute(array, "grp", [(group, group ^ 1) for group in range(groups)])

    send, slot = call(
        lambda *refs: pack_kernel(members, group_codes, *refs),
        [shape((total, feat), jnp.bfloat16), shape((1, rows), jnp.int32)],
        [
            row_owner.reshape(1, rows),
            prefix_offset.reshape(1, rows),
            first_assign.reshape(1, rows),
            second_assign.reshape(1, rows),
            embeddings,
        ],
    )
    got = swap(send)
    part, label = call(
        lambda *refs: sums_kernel(members, *refs),
        [shape(((2 * CORES + 1) * SECTION, feat), jnp.bfloat16), shape((8, total), jnp.float32)],
        [got, initial_centroids],
        in_memory=[vmem, pl.BlockSpec(memory_space=pl.ANY)],
        scratch=[pltpu.VMEM((codes_two, feat), jnp.bfloat16), pltpu.SemaphoreType.DMA],
    )
    (record,) = call(
        lambda *refs: score_kernel(codes_two, *refs),
        [shape((total, LANES), jnp.bfloat16)],
        [got, part, other_core(part), label],
    )
    back = swap(record)
    full = jnp.max(back[:, LANES - 1 :].astype(jnp.float32), axis=0, keepdims=True)
    full = jnp.maximum(full, other_core(full))
    distances, first_distance = call(
        unpack_kernel,
        [shape((codes_two, rows), jnp.float32), shape((1, rows), jnp.float32)],
        [back, slot],
    )
    return distances, first_distance, full


def body(*inputs):
    distances, first_distance, full = quick(*inputs)
    return lax.cond(
        full[0, 0] > 0.5,
        lambda kept, given: general(*given),
        lambda kept, given: kept,
        (distances, first_distance[0]),
        inputs,
    )


def solution(mesh):
    placed = (
        P(("grp", "mem"), None),
        P("grp", None, None),
        P(("grp", "mem"), None),
        P(("grp", "mem")),
        P(("grp", "mem")),
        P(("grp", "mem")),
    )
    return jax.shard_map(
        body,
        mesh=mesh,
        in_specs=placed,
        out_specs=(P(None, ("grp", "mem")), P(("grp", "mem"))),
        check_vma=False,
    )
```

```python
import jax
import jax.numpy as jnp
from jax import lax
from jax.experimental import pallas as pl
from jax.experimental.pallas import tpu as pltpu
from jax.sharding import PartitionSpec as P

PRIOR = 16
BLOCK = 24
KEEP = 22
MOVED = 16
LANES = 128
CORES = 2
SECTION = 112
SECOND, CHIP = 256, 256 * 128
FULL = 128
STEP_SCORE = 384
ROUNDING_BLOCK = 4.5e-4
ROUNDING_ALL = 2.5e-4
NT = (((1,), (1,)), ((), ()))
VMEM_LIMIT = 48 * 1024 * 1024


def iota(shape, dim):
    return lax.broadcasted_iota(jnp.int32, shape, dim)


def hot(condition):
    return jnp.where(condition, 1.0, 0.0).astype(jnp.bfloat16)


def dot(a, b):
    return jnp.dot(a, b, preferred_element_type=jnp.float32)


def dot_nt(a, b):
    return lax.dot_general(a, b, NT, preferred_element_type=jnp.float32)


def three_terms(values):
    high = values.astype(jnp.bfloat16)
    rest = values - high.astype(jnp.float32)
    middle = rest.astype(jnp.bfloat16)
    low = (rest - middle.astype(jnp.float32)).astype(jnp.bfloat16)
    return high, middle, low


def call(kernel, out_shape, args, out_memory=None, in_memory=None, scratch=()):
    vmem = pl.BlockSpec(memory_space=pltpu.VMEM)
    return pl.pallas_call(
        kernel,
        out_shape=out_shape,
        in_specs=in_memory or [vmem] * len(args),
        out_specs=out_memory or [vmem] * len(out_shape),
        scratch_shapes=scratch,
        compiler_params=pltpu.CompilerParams(vmem_limit_bytes=VMEM_LIMIT),
    )(*args)


def rank_in_bin(member):
    bins = hot(member)
    before = hot(iota((LANES, LANES), 0) < iota((LANES, LANES), 1))
    base = jnp.zeros((member.shape[0], 1), jnp.float32)
    ranks = []
    for begin in range(0, member.shape[1], LANES):
        piece = bins[:, begin : begin + LANES]
        ranks.append(dot(piece, before) + base)
        base = base + jnp.sum(piece.astype(jnp.float32), axis=1, keepdims=True)
    rank = jnp.concatenate(ranks, axis=1)
    return jnp.sum(jnp.where(member, rank, 0.0), axis=0, keepdims=True)


def column_of(row):
    diagonal = iota((LANES, LANES), 0) == iota((LANES, LANES), 1)
    pieces = []
    for begin in range(0, row.shape[1], LANES):
        piece = jnp.where(diagonal, row[:, begin : begin + LANES], 0.0)
        pieces.append(jnp.sum(piece, axis=1, keepdims=True))
    return jnp.concatenate(pieces, axis=0)


def highest(values):
    return jnp.max(values, axis=(0, 1), keepdims=True)


def split_kernel(members, group_codes, owner_ref, offset_ref, first_ref, second_ref, x_ref, move_ref, info_ref):
    rows, feat = x_ref.shape
    chips = lax.axis_size("grp") // CORES * members
    group = owner_ref[...] // members
    code = group * group_codes + offset_ref[...]
    chip = (group // CORES) * members + code % members
    rank = rank_in_bin(iota((chips, rows), 0) == chip).astype(jnp.int32)
    moves = rank >= KEEP
    place = rank_in_bin((iota((16, rows), 0) == 0) & moves).astype(jnp.int32)
    fits = place < MOVED - 1
    full = highest(jnp.where(moves & ~fits, 1.0, 0.0))
    place = jnp.where(moves & fits, place, -1)
    labels = first_ref[...] + 1 + LANES * (group % CORES) + SECOND * second_ref[...] + CHIP * chip
    info = [chip, rank, place, labels, jnp.broadcast_to(full.astype(jnp.int32), (1, rows))]
    info_ref[...] = jnp.concatenate(info + [jnp.zeros((3, rows), jnp.int32)], axis=0)
    moved = dot(hot(iota((MOVED, rows), 0) == place), x_ref[...])
    column = column_of(labels.astype(jnp.float32))
    packed = jnp.where(column_of(place.astype(jnp.float32)) == iota((1, LANES), 1).astype(jnp.float32), column, 0.0)
    packed = jnp.sum(packed, axis=0, keepdims=True).astype(jnp.int32)
    last = [packed % SECOND, (packed // SECOND) % LANES, packed // CHIP]
    last = [part.astype(jnp.float32) for part in last] + [jnp.broadcast_to(full, (1, feat - 3 * LANES))]
    last = jnp.concatenate(last, axis=1)
    move_ref[...] = jnp.where(iota((MOVED, feat), 0) == MOVED - 1, last, moved).astype(jnp.bfloat16)


def pack_kernel(x_ref, info_ref, came_ref, send_ref, slot_ref, came_slot_ref):
    rows, feat = x_ref.shape
    chips = send_ref.shape[0] // BLOCK
    run = feat // 2
    in_run = run // BLOCK
    chip, rank, labels = info_ref[0:1, :], info_ref[1:2, :], info_ref[3:4, :]
    full = info_ref[4:5, 0:1].astype(jnp.float32)
    kept = rank < KEEP
    slot = jnp.where(kept, chip * BLOCK + rank, -1)
    slot_ref[...] = slot
    kept_of = jnp.sum(hot((iota((chips, rows), 0) == chip) & kept).astype(jnp.float32), axis=1, keepdims=True)
    came = came_ref[...]
    came_last = came.astype(jnp.float32)[MOVED - 1 : MOVED]
    came_first = came_last[:, 0:LANES]
    came_chip = came_last[:, 2 * LANES : 3 * LANES]
    member = (iota((chips, LANES), 0).astype(jnp.float32) == came_chip) & (came_first > 0.5)
    after = jnp.sum(jnp.where(member, kept_of, 0.0), axis=0, keepdims=True) + rank_in_bin(member)
    fits = after < BLOCK - 1
    is_live = came_first > 0.5
    full = jnp.maximum(full, came_last[:, 3 * LANES : 3 * LANES + 1])
    full = jnp.maximum(full, highest(jnp.where(is_live & ~fits, 1.0, 0.0)))
    came_slot = jnp.where(is_live & fits, came_chip * BLOCK + after, -1.0)
    came_slot_ref[...] = jnp.broadcast_to(came_slot, (8, LANES)).astype(jnp.int32)
    came_labels = came_first + SECOND * came_last[:, LANES : 2 * LANES]
    label_column = jnp.concatenate(
        [column_of((labels % CHIP).astype(jnp.float32)), column_of(came_labels)[:MOVED]], axis=0
    )
    slot_column = jnp.concatenate([column_of(slot.astype(jnp.float32)), column_of(came_slot)[:MOVED]], axis=0)
    came_slot = came_slot.astype(jnp.int32)
    source, target = iota((run, run), 0).astype(jnp.float32), iota((run, run), 1).astype(jnp.float32)
    source = source - jnp.floor((source + 0.5) * (1.0 / BLOCK)) * BLOCK
    begin = ((lax.axis_index("mem") % in_run) * BLOCK).astype(jnp.float32)
    turn = hot(target == begin + source)
    block_of = jnp.floor((iota((in_run, run), 1).astype(jnp.float32) + 0.5) * (1.0 / BLOCK))
    in_block = block_of == iota((in_run, run), 0).astype(jnp.float32)
    lane_id = iota((1, LANES), 1)
    lane = lane_id.astype(jnp.float32)
    x = x_ref[...]
    for begin in range(0, chips * BLOCK, run):
        packed = []
        for at in range(begin, begin + run, LANES):
            part = jnp.where(slot_column == lane + at, label_column, 0.0)
            packed.append(jnp.sum(part, axis=0, keepdims=True).astype(jnp.int32))
        packed = jnp.concatenate(packed, axis=1)
        first = jnp.where(in_block, (packed % SECOND).astype(jnp.float32), 0.0)
        second = jnp.where(in_block, (packed // SECOND).astype(jnp.float32) + FULL * full, 0.0)
        last = dot(jnp.concatenate([first, second], axis=0).astype(jnp.bfloat16), turn)
        last = jnp.concatenate([last[:in_run], last[in_run:]], axis=1).astype(jnp.bfloat16)
        extra = jnp.concatenate([came, last], axis=0)
        position = jnp.where(lane_id < MOVED, came_slot - begin, (lane_id - MOVED) * BLOCK + BLOCK - 1)
        chosen = hot(iota((run, MOVED + in_run), 0) == position[:, : MOVED + in_run])
        moved = dot(hot(iota((run, rows), 0) + begin == slot), x) + dot(chosen, extra)
        send_ref[begin : begin + run, :] = moved.astype(jnp.bfloat16)


def row_of(column):
    diagonal = iota((LANES, LANES), 0) == iota((LANES, LANES), 1)
    return jnp.sum(jnp.where(diagonal, column, 0.0), axis=0, keepdims=True)


def sums_kernel(members, got_ref, start_ref, part_ref, label_ref, mine, sem):
    total, feat = got_ref.shape
    group_codes, codes_two = start_ref.shape[:2]
    offset = (lax.axis_index("mem") + members * group_codes - group_codes * lax.axis_index("grp")) % members
    fetch = pltpu.make_async_copy(start_ref.at[jnp.minimum(offset, group_codes - 1)], mine, sem)
    fetch.start()
    run = feat // 2
    runs = []
    for begin in range(0, total, run):
        row = jnp.zeros((1, feat), jnp.float32)
        for at in range(begin, begin + run, BLOCK):
            row = row + got_ref[at + BLOCK - 8 : at + BLOCK, :].astype(jnp.float32)[7:8, :]
        runs.append(row)
    first = jnp.concatenate([row[:, :run] for row in runs], axis=1) - 1.0
    second = jnp.concatenate([row[:, run:] for row in runs], axis=1)
    full = jnp.where(jnp.max(second) >= FULL, 1.0, 0.0)
    second = jnp.where(second >= FULL, second - FULL, second)
    second = jnp.where(first >= LANES, second + LANES, second)
    second = jnp.where(first >= 0.0, second, -1.0)
    label_ref[...] = jnp.broadcast_to(first, (8, total))
    x = got_ref[...]
    cluster = iota((CORES * LANES, total), 0).astype(jnp.float32)
    is_count = iota((SECTION, feat), 0) == SECTION - 1
    for update, assigned in enumerate((first, second)):
        member = hot(cluster == assigned)
        totals = dot(member, x)
        counts = jnp.sum(member.astype(jnp.float32), axis=1, keepdims=True)
        for core in range(CORES):
            count = row_of(counts[core * LANES : (core + 1) * LANES])
            large = jnp.floor(count * (1.0 / LANES))
            count = [large, count - large * LANES, jnp.full((1, feat - 2 * LANES), full, jnp.float32)]
            section = jnp.where(
                is_count,
                jnp.concatenate(count, axis=1),
                totals[core * LANES : core * LANES + SECTION],
            )
            at = (update * CORES + core) * SECTION
            part_ref[at : at + SECTION, :] = section.astype(jnp.bfloat16)
    fetch.wait()
    at = 2 * CORES * SECTION
    part_ref[at : at + SECTION, :] = jnp.zeros((SECTION, feat), jnp.bfloat16)
    part_ref[at : at + codes_two, :] = mine[...]


def score_kernel(codes_two, got_ref, own_ref, other_ref, label_ref, out_ref):
    total, feat = got_ref.shape
    my_core = lax.axis_index("grp") % CORES
    count_row = SECTION - 1

    def both(at):
        own = own_ref[at : at + SECTION, :].astype(jnp.float32)
        return own + other_ref[at : at + SECTION, :].astype(jnp.float32)

    full = jnp.zeros((1, 1), jnp.float32)
    rounded, squares_of = [], []
    at = 2 * CORES * SECTION
    starts = [ref[at : at + SECTION, :].astype(jnp.float32) for ref in (own_ref, other_ref)]
    for core in range(CORES):
        centre = jnp.where(my_core == core, starts[0], starts[1])
        for update in range(2):
            sums = both((update * CORES + core) * SECTION)
            counts = sums[count_row : count_row + 1]
            full = jnp.maximum(full, counts[:, 2 * LANES : 2 * LANES + 1])
            counts = column_of(counts[:, :LANES] * LANES + counts[:, LANES : 2 * LANES])
            centre = (sums + PRIOR * centre) * (1.0 / (counts[:SECTION] + PRIOR))
            narrow = jnp.concatenate(
                [centre.astype(jnp.bfloat16), jnp.zeros((LANES - SECTION, feat), jnp.bfloat16)], axis=0
            )
            wide = narrow.astype(jnp.float32)
            rounded.append(narrow)
            squares_of.append(row_of(jnp.sum(wide * wide, axis=1, keepdims=True)) * (1.0 / feat))
    full = jnp.max(full)
    table = jnp.concatenate(rounded, axis=0)
    lane = iota((STEP_SCORE, LANES), 1)
    is_score = lane < codes_two
    lane_value = lane.astype(jnp.float32)
    diagonal = iota((LANES, LANES), 0) == iota((LANES, LANES), 1)
    ones = jnp.ones((LANES, LANES), jnp.bfloat16)
    spread = iota((2 * LANES, LANES), 0) // LANES
    spread = hot(iota((2 * LANES, LANES), 1) == codes_two + 1 + spread)
    excess_all = jnp.zeros((STEP_SCORE, LANES), jnp.float32)
    excess_block = []

    def across(values):
        return dot(values.astype(jnp.bfloat16), ones)

    for begin in range(0, total, STEP_SCORE):
        x = got_ref[begin : begin + STEP_SCORE, :]
        inner = dot_nt(x, table)
        key = [
            jnp.where(diagonal, label_ref[0:1, at : at + LANES], 0.0)
            for at in range(begin, begin + STEP_SCORE, LANES)
        ]
        key = across(jnp.concatenate(key, axis=0))
        is_other = key >= LANES
        first = jnp.where(is_other, key - LANES, key)
        wide = x.astype(jnp.float32)
        squares = jnp.sum(wide * wide, axis=1, keepdims=True) * (1.0 / feat)

        def distance(update):
            low, high = [
                squares_of[at] - (2.0 / feat) * inner[:, at * LANES : (at + 1) * LANES]
                for at in (update, 2 + update)
            ]
            return squares + jnp.where(is_other, high, low)

        near = jnp.where(lane_value == first, distance(0), 0.0)
        near_high = near.astype(jnp.bfloat16)
        near_low = (near - near_high.astype(jnp.float32)).astype(jnp.bfloat16)
        score = jnp.where(is_score, distance(1), 0.0)
        mean = (across(score) * (1.0 / codes_two)).astype(jnp.bfloat16).astype(jnp.float32)
        rest = jnp.where(is_score, score - mean, 0.0)
        record = rest.astype(jnp.bfloat16).astype(jnp.float32)
        lost = rest - record
        is_live = key >= 0.0
        lost = jnp.where(is_live, lost * lost, 0.0)
        sent = jnp.where(is_live, score * score, 0.0)
        excess_all = excess_all + (lost - (ROUNDING_ALL * ROUNDING_ALL) * sent)
        excess = lost - (ROUNDING_BLOCK * ROUNDING_BLOCK) * sent
        excess = jnp.sum(excess.reshape(STEP_SCORE // BLOCK, BLOCK // 8, 8, LANES), axis=1)
        excess_block.append(excess.reshape(STEP_SCORE // BLOCK * 8, LANES))
        near = dot(jnp.concatenate([near_high, near_low], axis=1), spread)
        record = jnp.where(lane == codes_two, mean, record + near)
        out_ref[begin : begin + STEP_SCORE, :] = record.astype(jnp.bfloat16)
    excess = across(jnp.concatenate(excess_block, axis=0))
    excess = jnp.sum(excess.reshape(total // BLOCK, 8, LANES), axis=1)
    full = jnp.maximum(full, jnp.where(jnp.max(excess) > 0.0, 1.0, 0.0))
    full = jnp.maximum(full, jnp.where(jnp.sum(excess_all) > 0.0, 1.0, 0.0))
    for begin in range(0, total, STEP_SCORE):
        record = out_ref[begin : begin + STEP_SCORE, :].astype(jnp.float32)
        record = jnp.where(lane == LANES - 1, full, record)
        out_ref[begin : begin + STEP_SCORE, :] = record.astype(jnp.bfloat16)


def return_kernel(got_ref, came_slot_ref, out_ref):
    total = got_ref.shape[0]
    got = got_ref[...]
    full = highest(jnp.where(iota((total, LANES), 1) == LANES - 1, got.astype(jnp.float32), 0.0))
    slot = column_of(came_slot_ref[0:1, :].astype(jnp.float32))[:MOVED]
    moved = dot(hot(iota((MOVED, total), 1).astype(jnp.float32) == slot), got)
    out_ref[...] = jnp.where(iota((MOVED, LANES), 1) == LANES - 1, full, moved).astype(jnp.bfloat16)


def unpack_kernel(got_ref, slot_ref, back_ref, info_ref, all_ref, one_ref, full_ref):
    total = got_ref.shape[0]
    rows = slot_ref.shape[1]
    codes_two = all_ref.shape[0]
    back = back_ref[...].astype(jnp.float32)
    own = jnp.max(got_ref[:, LANES - 1 :].astype(jnp.float32))
    full_ref[0, 0] = jnp.maximum(own, jnp.max(back[:, LANES - 1 :]))
    moved = dot(got_ref[...].T, hot(iota((total, rows), 0) == slot_ref[...]))
    moved = moved + dot(back.T.astype(jnp.bfloat16), hot(iota((MOVED, rows), 0) == info_ref[2:3, :]))
    mean = moved[codes_two : codes_two + 1]
    near = moved[codes_two + 1 : codes_two + 2] + moved[codes_two + 2 : codes_two + 3]
    all_ref[...] = moved[:codes_two] + mean
    one_ref[...] = near


def over_members(totals, counts):
    members = lax.axis_size("mem")
    clusters, feat = totals.shape
    share = -(-clusters // members)

    def swap(blocks):
        return lax.all_to_all(blocks, "mem", split_axis=0, concat_axis=0, tiled=True)

    padded = jnp.pad(totals.astype(jnp.bfloat16), ((0, members * share - clusters), (0, 0)))
    own = jnp.sum(swap(padded.reshape(members, share, feat)).astype(jnp.float32), axis=0)
    own = jnp.broadcast_to(own.astype(jnp.bfloat16)[None], (members, share, feat))
    summed = swap(own).reshape(members * share, feat)[:clusters].astype(jnp.float32)
    counted = jnp.sum(swap(jnp.broadcast_to(counts[None], (members, clusters))), axis=0)
    return summed, counted


def pick_block(total):
    for candidate in range(1024, 0, -1):
        if total % candidate == 0:
            return candidate
    return total


def general(embeddings, initial_centroids, row_owner, prefix_offset, first_assign, second_assign):
    row_count, feat_width = embeddings.shape
    group_codes = initial_centroids.shape[0]
    codes_two = initial_centroids.shape[1]
    clusters = group_codes * codes_two
    group_count = lax.axis_size("grp")
    member_count = lax.axis_size("mem")
    devices_all = group_count * member_count
    capacity = 2 * row_count // devices_all + 4
    slot_total = devices_all * capacity
    target = row_owner[:, 0]
    dest_table = (target[:, None] == jnp.arange(devices_all, dtype=jnp.int32)[None, :]).astype(
        jnp.int32
    )
    slot_rank = jnp.sum(jnp.cumsum(dest_table, axis=0) * dest_table, axis=1) - 1
    slot_index = target * capacity + slot_rank
    send_rows = jnp.zeros((slot_total, feat_width), jnp.bfloat16).at[slot_index].set(embeddings)
    labels = jnp.stack([prefix_offset, first_assign, second_assign], axis=1)
    send_labels = jnp.full((slot_total, 3), -1, jnp.int32).at[slot_index].set(labels)
    got_rows, got_labels = (
        lax.all_to_all(send_rows, ("grp", "mem"), split_axis=0, concat_axis=0, tiled=True),
        lax.all_to_all(send_labels, ("grp", "mem"), split_axis=0, concat_axis=0, tiled=True),
    )
    offsets = got_labels[:, 0]
    live = offsets >= 0
    ids_one = jnp.where(live, offsets * codes_two + got_labels[:, 1], -1)
    ids_two = jnp.where(live, offsets * codes_two + got_labels[:, 2], -1)
    squares = jnp.sum(jnp.square(got_rows.astype(jnp.float32)), axis=1)
    block_rows = pick_block(slot_total)
    block_count = slot_total // block_rows
    row_blocks = got_rows.reshape(block_count, block_rows, feat_width)
    cluster_range = jnp.arange(clusters, dtype=jnp.int32)

    def local_totals(cluster_ids):

        def add_block(carry, pieces):
            totals, counts = carry
            block_x, block_ids = pieces
            hot_table = (block_ids[:, None] == cluster_range[None, :]).astype(jnp.bfloat16)
            totals = totals + lax.dot_general(
                hot_table, block_x, (((0,), (0,)), ((), ())), preferred_element_type=jnp.float32
            )
            counts = counts + jnp.sum(hot_table, axis=0, dtype=jnp.float32)
            return ((totals, counts), None)

        start = (
            jnp.zeros((clusters, feat_width), jnp.float32),
            jnp.zeros((clusters,), jnp.float32),
        )
        result, unused = lax.scan(
            add_block, start, (row_blocks, cluster_ids.reshape(block_count, block_rows))
        )
        return result

    start_table = initial_centroids.reshape(clusters, feat_width).astype(jnp.float32)

    def update(earlier, cluster_ids):
        totals, counts = local_totals(cluster_ids)
        totals, counts = over_members(totals, counts)
        centre = (totals + PRIOR * earlier) / (counts[:, None] + PRIOR)
        return (centre, centre.astype(jnp.bfloat16))

    centre_one, rounded_one = update(start_table, ids_one)
    assigned = jnp.take(rounded_one, jnp.maximum(ids_one, 0), axis=0).astype(jnp.float32)
    first_local = (
        squares
        - 2.0 * jnp.sum(got_rows.astype(jnp.float32) * assigned, axis=1)
        + jnp.sum(assigned * assigned, axis=1)
    ) / feat_width
    centre_two, rounded_two = update(centre_one, ids_two)
    centre_squares = jnp.sum(jnp.square(rounded_two.astype(jnp.float32)), axis=1).reshape(
        group_codes, codes_two
    )
    code_range = jnp.arange(group_codes, dtype=jnp.int32)

    def score_block(pieces):
        block_x, block_offsets, block_sq = pieces
        raw = lax.dot_general(
            rounded_two, block_x, (((1,), (1,)), ((), ())), preferred_element_type=jnp.float32
        )
        raw = raw.reshape(group_codes, codes_two, block_rows)
        select = (block_offsets[None, :] == code_range[:, None]).astype(jnp.float32)
        inner = jnp.sum(raw * select[:, None, :], axis=0)
        norms = jnp.sum(centre_squares[:, :, None] * select[:, None, :], axis=0)
        return (block_sq[None, :] - 2.0 * inner + norms) / feat_width

    scored = lax.map(
        score_block,
        (
            row_blocks,
            offsets.reshape(block_count, block_rows),
            squares.reshape(block_count, block_rows),
        ),
    )
    all_local = jnp.transpose(scored, (1, 0, 2)).reshape(codes_two, slot_total)
    one_local = first_local[None, :]
    back_all, back_one = (
        lax.all_to_all(all_local, ("grp", "mem"), split_axis=1, concat_axis=1, tiled=True),
        lax.all_to_all(one_local, ("grp", "mem"), split_axis=1, concat_axis=1, tiled=True),
    )
    distances = jnp.take(back_all, slot_index, axis=1)
    first_distance = jnp.take(back_one[0], slot_index, axis=0)
    return (distances, first_distance)


def quick(embeddings, initial_centroids, row_owner, prefix_offset, first_assign, second_assign):
    rows, feat = embeddings.shape
    group_codes, codes_two = initial_centroids.shape[:2]
    groups = lax.axis_size("grp")
    members = lax.axis_size("mem")
    chips = groups // CORES * members
    total = chips * BLOCK
    shape = jax.ShapeDtypeStruct
    vmem = pl.BlockSpec(memory_space=pltpu.VMEM)
    same_core = [
        [group * members + member for group in range(core, groups, CORES) for member in range(members)]
        for core in range(CORES)
    ]

    def swap(array):
        blocks = array.reshape(chips, array.shape[0] // chips, array.shape[1])
        blocks = lax.all_to_all(
            blocks, ("grp", "mem"), split_axis=0, concat_axis=0, axis_index_groups=same_core, tiled=True
        )
        return blocks.reshape(array.shape)

    def other_core(array):
        return lax.ppermute(array, "grp", [(group, group ^ 1) for group in range(groups)])

    move, info = call(
        lambda *refs: split_kernel(members, group_codes, *refs),
        [shape((MOVED, feat), jnp.bfloat16), shape((8, rows), jnp.int32)],
        [
            row_owner.reshape(1, rows),
            prefix_offset.reshape(1, rows),
            first_assign.reshape(1, rows),
            second_assign.reshape(1, rows),
            embeddings,
        ],
    )
    send, slot, came_slot = call(
        pack_kernel,
        [
            shape((total, feat), jnp.bfloat16),
            shape((1, rows), jnp.int32),
            shape((8, LANES), jnp.int32),
        ],
        [embeddings, info, other_core(move)],
    )
    got = swap(send)
    part, label = call(
        lambda *refs: sums_kernel(members, *refs),
        [shape(((2 * CORES + 1) * SECTION, feat), jnp.bfloat16), shape((8, total), jnp.float32)],
        [got, initial_centroids],
        in_memory=[vmem, pl.BlockSpec(memory_space=pl.ANY)],
        scratch=[pltpu.VMEM((codes_two, feat), jnp.bfloat16), pltpu.SemaphoreType.DMA],
    )
    (record,) = call(
        lambda *refs: score_kernel(codes_two, *refs),
        [shape((total, LANES), jnp.bfloat16)],
        [got, part, other_core(part), label],
    )
    back = swap(record)
    (came_back,) = call(return_kernel, [shape((MOVED, LANES), jnp.bfloat16)], [back, came_slot])
    return call(
        unpack_kernel,
        [shape((codes_two, rows), jnp.float32), shape((1, rows), jnp.float32), shape((1, 1), jnp.float32)],
        [back, slot, other_core(came_back), info],
        out_memory=[vmem, vmem, pl.BlockSpec(memory_space=pltpu.SMEM)],
    )


def body(*inputs):
    distances, first_distance, full = quick(*inputs)
    return lax.cond(
        full[0, 0] > 0.5,
        lambda kept, given: general(*given),
        lambda kept, given: kept,
        (distances, first_distance[0]),
        inputs,
    )


def solution(mesh):
    placed = (
        P(("grp", "mem"), None),
        P("grp", None, None),
        P(("grp", "mem"), None),
        P(("grp", "mem")),
        P(("grp", "mem")),
        P(("grp", "mem")),
    )
    return jax.shard_map(
        body,
        mesh=mesh,
        in_specs=placed,
        out_specs=(P(None, ("grp", "mem")), P(("grp", "mem"))),
        check_vma=False,
    )
```

```python
import jax
import jax.numpy as jnp
from jax import lax
from jax.experimental import pallas as pl
from jax.experimental.pallas import tpu as pltpu
from jax.sharding import PartitionSpec as P

PRIOR = 16
BLOCK = 24
KEEP = 22
MOVED = 16
LANES = 128
CORES = 2
SECTION = 112
SECOND, CHIP = 256, 256 * 128
FULL = 128
STEP_SCORE = 384
ROUNDING_BLOCK = 4.5e-4
ROUNDING_ALL = 2.5e-4
NT = (((1,), (1,)), ((), ()))
VMEM_LIMIT = 48 * 1024 * 1024


def iota(shape, dim):
    return lax.broadcasted_iota(jnp.int32, shape, dim)


def hot(condition):
    return jnp.where(condition, 1.0, 0.0).astype(jnp.bfloat16)


def dot(a, b):
    return jnp.dot(a, b, preferred_element_type=jnp.float32)


def dot_nt(a, b):
    return lax.dot_general(a, b, NT, preferred_element_type=jnp.float32)


def three_terms(values):
    high = values.astype(jnp.bfloat16)
    rest = values - high.astype(jnp.float32)
    middle = rest.astype(jnp.bfloat16)
    low = (rest - middle.astype(jnp.float32)).astype(jnp.bfloat16)
    return high, middle, low


def call(kernel, out_shape, args, out_memory=None, in_memory=None, scratch=(), cost=None):
    vmem = pl.BlockSpec(memory_space=pltpu.VMEM)
    return pl.pallas_call(
        kernel,
        out_shape=out_shape,
        in_specs=in_memory or [vmem] * len(args),
        out_specs=out_memory or [vmem] * len(out_shape),
        scratch_shapes=scratch,
        cost_estimate=cost,
        compiler_params=pltpu.CompilerParams(vmem_limit_bytes=VMEM_LIMIT),
    )(*args)


def rank_in_bin(member):
    bins = hot(member)
    before = hot(iota((LANES, LANES), 0) < iota((LANES, LANES), 1))
    base = jnp.zeros((member.shape[0], 1), jnp.float32)
    ranks = []
    for begin in range(0, member.shape[1], LANES):
        piece = bins[:, begin : begin + LANES]
        ranks.append(dot(piece, before) + base)
        base = base + jnp.sum(piece.astype(jnp.float32), axis=1, keepdims=True)
    rank = jnp.concatenate(ranks, axis=1)
    return jnp.sum(jnp.where(member, rank, 0.0), axis=0, keepdims=True)


def column_of(row):
    diagonal = iota((LANES, LANES), 0) == iota((LANES, LANES), 1)
    pieces = []
    for begin in range(0, row.shape[1], LANES):
        piece = jnp.where(diagonal, row[:, begin : begin + LANES], 0.0)
        pieces.append(jnp.sum(piece, axis=1, keepdims=True))
    return jnp.concatenate(pieces, axis=0)


def highest(values):
    return jnp.max(values, axis=(0, 1), keepdims=True)


def split_kernel(
    members, group_codes, owner_ref, offset_ref, first_ref, second_ref, x_ref, move_ref, info_ref
):
    rows, feat = x_ref.shape
    chips = lax.axis_size("grp") // CORES * members
    group = owner_ref[...] // members
    code = group * group_codes + offset_ref[...]
    chip = (group // CORES) * members + code % members
    rank = rank_in_bin(iota((chips, rows), 0) == chip).astype(jnp.int32)
    moves = rank >= KEEP
    place = rank_in_bin((iota((16, rows), 0) == 0) & moves).astype(jnp.int32)
    fits = place < MOVED - 1
    full = highest(jnp.where(moves & ~fits, 1.0, 0.0))
    place = jnp.where(moves & fits, place, -1)
    labels = first_ref[...] + 1 + LANES * (group % CORES) + SECOND * second_ref[...] + CHIP * chip
    info = [chip, rank, place, labels, jnp.broadcast_to(full.astype(jnp.int32), (1, rows))]
    info_ref[...] = jnp.concatenate(info + [jnp.zeros((3, rows), jnp.int32)], axis=0)
    column = column_of(labels.astype(jnp.float32))
    packed = jnp.where(column_of(place.astype(jnp.float32)) == iota((1, LANES), 1).astype(jnp.float32), column, 0.0)
    packed = jnp.sum(packed, axis=0, keepdims=True).astype(jnp.int32)
    last = [packed % SECOND, (packed // SECOND) % LANES, packed // CHIP]
    last = [part.astype(jnp.float32) for part in last] + [jnp.broadcast_to(full, (1, feat - 3 * LANES))]
    last = jnp.concatenate(last, axis=1)
    moved = dot(hot(iota((MOVED, rows), 0) == place), x_ref[...])
    move_ref[...] = jnp.where(iota((MOVED, feat), 0) == MOVED - 1, last, moved).astype(jnp.bfloat16)


def pack_kernel(
    members, x_ref, info_ref, came_ref, start_ref, send_ref, slot_ref, came_slot_ref, own_start_ref, x, mine, sem
):
    rows, feat = x_ref.shape
    group_codes, codes_two = start_ref.shape[:2]
    offset = (lax.axis_index("mem") + members * group_codes - group_codes * lax.axis_index("grp")) % members
    fetch_start = pltpu.make_async_copy(start_ref.at[jnp.minimum(offset, group_codes - 1)], mine, sem.at[1])
    fetch = pltpu.make_async_copy(x_ref, x, sem.at[0])
    fetch.start()
    fetch_start.start()
    chips = send_ref.shape[0] // BLOCK
    run = feat // 2
    in_run = run // BLOCK
    chip, rank, labels = info_ref[0:1, :], info_ref[1:2, :], info_ref[3:4, :]
    full = info_ref[4:5, 0:1].astype(jnp.float32)
    kept = rank < KEEP
    slot = jnp.where(kept, chip * BLOCK + rank, -1)
    slot_ref[...] = slot
    kept_of = jnp.sum(hot((iota((chips, rows), 0) == chip) & kept).astype(jnp.float32), axis=1, keepdims=True)
    came = came_ref[...]
    came_last = came.astype(jnp.float32)[MOVED - 1 : MOVED]
    came_first = came_last[:, 0:LANES]
    came_chip = came_last[:, 2 * LANES : 3 * LANES]
    member = (iota((chips, LANES), 0).astype(jnp.float32) == came_chip) & (came_first > 0.5)
    after = jnp.sum(jnp.where(member, kept_of, 0.0), axis=0, keepdims=True) + rank_in_bin(member)
    fits = after < BLOCK - 1
    is_live = came_first > 0.5
    full = jnp.maximum(full, came_last[:, 3 * LANES : 3 * LANES + 1])
    full = jnp.maximum(full, highest(jnp.where(is_live & ~fits, 1.0, 0.0)))
    came_slot = jnp.where(is_live & fits, came_chip * BLOCK + after, -1.0)
    came_slot_ref[...] = jnp.broadcast_to(came_slot, (8, LANES)).astype(jnp.int32)
    came_labels = came_first + SECOND * came_last[:, LANES : 2 * LANES]
    label_column = jnp.concatenate(
        [column_of((labels % CHIP).astype(jnp.float32)), column_of(came_labels)[:MOVED]], axis=0
    )
    slot_column = jnp.concatenate([column_of(slot.astype(jnp.float32)), column_of(came_slot)[:MOVED]], axis=0)
    came_slot = came_slot.astype(jnp.int32)
    source, target = iota((run, run), 0).astype(jnp.float32), iota((run, run), 1).astype(jnp.float32)
    source = source - jnp.floor((source + 0.5) * (1.0 / BLOCK)) * BLOCK
    begin = ((lax.axis_index("mem") % in_run) * BLOCK).astype(jnp.float32)
    turn = hot(target == begin + source)
    block_of = jnp.floor((iota((in_run, run), 1).astype(jnp.float32) + 0.5) * (1.0 / BLOCK))
    in_block = block_of == iota((in_run, run), 0).astype(jnp.float32)
    lane = iota((1, LANES), 1).astype(jnp.float32)
    packed = []
    for at in range(0, chips * BLOCK, LANES):
        part = jnp.where(slot_column == lane + at, label_column, 0.0)
        packed.append(jnp.sum(part, axis=0, keepdims=True).astype(jnp.int32))
    packed = jnp.concatenate(packed, axis=1)
    labels = [(packed % SECOND).astype(jnp.float32), (packed // SECOND).astype(jnp.float32) + FULL * full]
    last = [
        jnp.where(in_block, part[:, at : at + run], 0.0)
        for part in labels
        for at in range(0, chips * BLOCK, run)
    ]
    last = dot(jnp.concatenate(last, axis=0).astype(jnp.bfloat16), turn)
    last = jnp.concatenate([last[:chips], last[chips:]], axis=1).astype(jnp.bfloat16)
    extra = jnp.concatenate([last, came], axis=0)
    lane_id = iota((1, LANES), 1)
    position = jnp.concatenate([came_slot[:, :MOVED], jnp.full((1, LANES - MOVED), -1, jnp.int32)], axis=1)
    position = jnp.where(lane_id < chips, lane_id * BLOCK + BLOCK - 1, pltpu.roll(position, chips, 1))
    position = position[:, : chips + MOVED]
    fetch_start.wait()
    own_start_ref[...] = jnp.zeros((SECTION, feat), jnp.bfloat16)
    own_start_ref[0:codes_two, :] = mine[...]
    fetch.wait()
    step = chips * BLOCK // 2
    for begin in range(0, chips * BLOCK, step):
        moved = dot(hot(iota((step, rows), 0) + begin == slot), x[...])
        moved = moved + dot(hot(iota((step, chips + MOVED), 0) + begin == position), extra)
        send_ref[begin : begin + step, :] = moved.astype(jnp.bfloat16)


def row_of(column):
    diagonal = iota((LANES, LANES), 0) == iota((LANES, LANES), 1)
    return jnp.sum(jnp.where(diagonal, column, 0.0), axis=0, keepdims=True)


def sums_kernel(got_ref, part_ref, label_ref):
    total, feat = got_ref.shape
    run = feat // 2
    runs = []
    for begin in range(0, total, run):
        row = jnp.zeros((1, feat), jnp.float32)
        for at in range(begin, begin + run, BLOCK):
            row = row + got_ref[at + BLOCK - 8 : at + BLOCK, :].astype(jnp.float32)[7:8, :]
        runs.append(row)
    first = jnp.concatenate([row[:, :run] for row in runs], axis=1) - 1.0
    second = jnp.concatenate([row[:, run:] for row in runs], axis=1)
    full = jnp.where(jnp.max(second) >= FULL, 1.0, 0.0)
    second = jnp.where(second >= FULL, second - FULL, second)
    second = jnp.where(first >= LANES, second + LANES, second)
    second = jnp.where(first >= 0.0, second, -1.0)
    label_ref[...] = jnp.broadcast_to(first, (8, total))
    x = got_ref[...]
    cluster = iota((CORES * LANES, total), 0).astype(jnp.float32)
    is_count = iota((SECTION, feat), 0) == SECTION - 1
    member = hot(jnp.concatenate([cluster == first, cluster == second], axis=0))
    totals = dot(member, x)
    counts = jnp.sum(member.astype(jnp.float32), axis=1, keepdims=True)
    for section in range(2 * CORES):
        begin, at = section * LANES, section * SECTION
        count = row_of(counts[begin : begin + LANES])
        large = jnp.floor(count * (1.0 / LANES))
        count = [large, count - large * LANES, jnp.full((1, feat - 2 * LANES), full, jnp.float32)]
        count = jnp.concatenate(count, axis=1)
        sums = jnp.where(is_count, count, totals[begin : begin + SECTION])
        part_ref[at : at + SECTION, :] = sums.astype(jnp.bfloat16)


def prepare_kernel(got_ref, label_ref, key_ref, squares_ref):
    total, feat = got_ref.shape
    diagonal = iota((LANES, LANES), 0) == iota((LANES, LANES), 1)
    ones = jnp.ones((LANES, LANES), jnp.bfloat16)
    for begin in range(0, total, STEP_SCORE):
        key = [
            jnp.where(diagonal, label_ref[0:1, at : at + LANES], 0.0)
            for at in range(begin, begin + STEP_SCORE, LANES)
        ]
        key = jnp.concatenate(key, axis=0).astype(jnp.bfloat16)
        key_ref[begin : begin + STEP_SCORE, :] = dot(key, ones)
        wide = got_ref[begin : begin + STEP_SCORE, :].astype(jnp.float32)
        squares = jnp.sum(wide * wide, axis=1, keepdims=True) * (1.0 / feat)
        squares_ref[begin : begin + STEP_SCORE, :] = jnp.broadcast_to(squares, (STEP_SCORE, LANES))


def score_kernel(
    codes_two, got_ref, own_ref, other_ref, own_start_ref, other_start_ref, key_ref, squares_ref, out_ref
):
    total, feat = got_ref.shape
    my_core = lax.axis_index("grp") % CORES
    count_row = SECTION - 1

    def both(at):
        own = own_ref[at : at + SECTION, :].astype(jnp.float32)
        return own + other_ref[at : at + SECTION, :].astype(jnp.float32)

    full = jnp.zeros((1, 1), jnp.float32)
    rounded, squares_of = [], []
    starts = [ref[...].astype(jnp.float32) for ref in (own_start_ref, other_start_ref)]
    for core in range(CORES):
        centre = jnp.where(my_core == core, starts[0], starts[1])
        for update in range(2):
            sums = both((update * CORES + core) * SECTION)
            counts = sums[count_row : count_row + 1]
            full = jnp.maximum(full, counts[:, 2 * LANES : 2 * LANES + 1])
            counts = column_of(counts[:, :LANES] * LANES + counts[:, LANES : 2 * LANES])
            centre = (sums + PRIOR * centre) * (1.0 / (counts[:SECTION] + PRIOR))
            narrow = jnp.concatenate(
                [centre.astype(jnp.bfloat16), jnp.zeros((LANES - SECTION, feat), jnp.bfloat16)], axis=0
            )
            wide = narrow.astype(jnp.float32)
            rounded.append(narrow)
            squares_of.append(row_of(jnp.sum(wide * wide, axis=1, keepdims=True)) * (1.0 / feat))
    full = jnp.max(full)
    table = jnp.concatenate(rounded, axis=0)
    lane = iota((STEP_SCORE, LANES), 1)
    is_score = lane < codes_two
    lane_value = lane.astype(jnp.float32)
    ones = jnp.ones((LANES, LANES), jnp.bfloat16)
    spread = iota((2 * LANES, LANES), 0) // LANES
    spread = hot(iota((2 * LANES, LANES), 1) == codes_two + 1 + spread)
    excess_all = jnp.zeros((STEP_SCORE, LANES), jnp.float32)
    excess_block = []

    def across(values):
        return dot(values.astype(jnp.bfloat16), ones)

    for begin in range(0, total, STEP_SCORE):
        x = got_ref[begin : begin + STEP_SCORE, :]
        inner = dot_nt(x, table)
        key = key_ref[begin : begin + STEP_SCORE, :]
        is_other = key >= LANES
        first = jnp.where(is_other, key - LANES, key)
        squares = squares_ref[begin : begin + STEP_SCORE, :]

        def distance(update):
            low, high = [
                squares_of[at] - (2.0 / feat) * inner[:, at * LANES : (at + 1) * LANES]
                for at in (update, 2 + update)
            ]
            return squares + jnp.where(is_other, high, low)

        near = jnp.where(lane_value == first, distance(0), 0.0)
        near_high = near.astype(jnp.bfloat16)
        near_low = (near - near_high.astype(jnp.float32)).astype(jnp.bfloat16)
        score = jnp.where(is_score, distance(1), 0.0)
        mean = (across(score) * (1.0 / codes_two)).astype(jnp.bfloat16).astype(jnp.float32)
        rest = jnp.where(is_score, score - mean, 0.0)
        record = rest.astype(jnp.bfloat16).astype(jnp.float32)
        lost = rest - record
        is_live = key >= 0.0
        lost = jnp.where(is_live, lost * lost, 0.0)
        sent = jnp.where(is_live, score * score, 0.0)
        excess_all = excess_all + (lost - (ROUNDING_ALL * ROUNDING_ALL) * sent)
        excess = lost - (ROUNDING_BLOCK * ROUNDING_BLOCK) * sent
        excess = jnp.sum(excess.reshape(STEP_SCORE // BLOCK, BLOCK // 8, 8, LANES), axis=1)
        excess_block.append(excess.reshape(STEP_SCORE // BLOCK * 8, LANES))
        near = dot(jnp.concatenate([near_high, near_low], axis=1), spread)
        record = jnp.where(lane == codes_two, mean, record + near)
        out_ref[begin : begin + STEP_SCORE, :] = record.astype(jnp.bfloat16)
    excess = across(jnp.concatenate(excess_block, axis=0))
    excess = jnp.sum(excess.reshape(total // BLOCK, 8, LANES), axis=1)
    full = jnp.maximum(full, jnp.where(jnp.max(excess) > 0.0, 1.0, 0.0))
    full = jnp.maximum(full, jnp.where(jnp.sum(excess_all) > 0.0, 1.0, 0.0))
    for begin in range(0, total, STEP_SCORE):
        record = out_ref[begin : begin + STEP_SCORE, :].astype(jnp.float32)
        record = jnp.where(lane == LANES - 1, full, record)
        out_ref[begin : begin + STEP_SCORE, :] = record.astype(jnp.bfloat16)


def return_kernel(got_ref, came_slot_ref, out_ref):
    total = got_ref.shape[0]
    got = got_ref[...]
    full = highest(jnp.where(iota((total, LANES), 1) == LANES - 1, got.astype(jnp.float32), 0.0))
    slot = column_of(came_slot_ref[0:1, :].astype(jnp.float32))[:MOVED]
    moved = dot(hot(iota((MOVED, total), 1).astype(jnp.float32) == slot), got)
    out_ref[...] = jnp.where(iota((MOVED, LANES), 1) == LANES - 1, full, moved).astype(jnp.bfloat16)


def gather_kernel(got_ref, slot_ref, out_ref):
    total = got_ref.shape[0]
    rows = slot_ref.shape[1]
    out_ref[...] = dot(got_ref[...].T, hot(iota((total, rows), 0) == slot_ref[...]))


def unpack_kernel(gathered_ref, own_ref, back_ref, info_ref, all_ref, one_ref, full_ref):
    rows = info_ref.shape[1]
    codes_two = all_ref.shape[0]
    back = back_ref[...].astype(jnp.float32)
    full = jnp.maximum(own_ref[...].astype(jnp.float32), back)
    full_ref[0, 0] = jnp.max(full[:, LANES - 1 :])
    moved = dot(back.T.astype(jnp.bfloat16), hot(iota((MOVED, rows), 0) == info_ref[2:3, :]))
    moved = gathered_ref[...] + moved
    mean = moved[codes_two : codes_two + 1]
    near = moved[codes_two + 1 : codes_two + 2] + moved[codes_two + 2 : codes_two + 3]
    all_ref[...] = moved[:codes_two] + mean
    one_ref[...] = near


def over_members(totals, counts):
    members = lax.axis_size("mem")
    clusters, feat = totals.shape
    share = -(-clusters // members)

    def swap(blocks):
        return lax.all_to_all(blocks, "mem", split_axis=0, concat_axis=0, tiled=True)

    padded = jnp.pad(totals.astype(jnp.bfloat16), ((0, members * share - clusters), (0, 0)))
    own = jnp.sum(swap(padded.reshape(members, share, feat)).astype(jnp.float32), axis=0)
    own = jnp.broadcast_to(own.astype(jnp.bfloat16)[None], (members, share, feat))
    summed = swap(own).reshape(members * share, feat)[:clusters].astype(jnp.float32)
    counted = jnp.sum(swap(jnp.broadcast_to(counts[None], (members, clusters))), axis=0)
    return summed, counted


def pick_block(total):
    for candidate in range(1024, 0, -1):
        if total % candidate == 0:
            return candidate
    return total


def general(embeddings, initial_centroids, row_owner, prefix_offset, first_assign, second_assign):
    row_count, feat_width = embeddings.shape
    group_codes = initial_centroids.shape[0]
    codes_two = initial_centroids.shape[1]
    clusters = group_codes * codes_two
    group_count = lax.axis_size("grp")
    member_count = lax.axis_size("mem")
    devices_all = group_count * member_count
    capacity = 2 * row_count // devices_all + 4
    slot_total = devices_all * capacity
    target = row_owner[:, 0]
    dest_table = (target[:, None] == jnp.arange(devices_all, dtype=jnp.int32)[None, :]).astype(
        jnp.int32
    )
    slot_rank = jnp.sum(jnp.cumsum(dest_table, axis=0) * dest_table, axis=1) - 1
    slot_index = target * capacity + slot_rank
    send_rows = jnp.zeros((slot_total, feat_width), jnp.bfloat16).at[slot_index].set(embeddings)
    labels = jnp.stack([prefix_offset, first_assign, second_assign], axis=1)
    send_labels = jnp.full((slot_total, 3), -1, jnp.int32).at[slot_index].set(labels)
    got_rows, got_labels = (
        lax.all_to_all(send_rows, ("grp", "mem"), split_axis=0, concat_axis=0, tiled=True),
        lax.all_to_all(send_labels, ("grp", "mem"), split_axis=0, concat_axis=0, tiled=True),
    )
    offsets = got_labels[:, 0]
    live = offsets >= 0
    ids_one = jnp.where(live, offsets * codes_two + got_labels[:, 1], -1)
    ids_two = jnp.where(live, offsets * codes_two + got_labels[:, 2], -1)
    squares = jnp.sum(jnp.square(got_rows.astype(jnp.float32)), axis=1)
    block_rows = pick_block(slot_total)
    block_count = slot_total // block_rows
    row_blocks = got_rows.reshape(block_count, block_rows, feat_width)
    cluster_range = jnp.arange(clusters, dtype=jnp.int32)

    def local_totals(cluster_ids):

        def add_block(carry, pieces):
            totals, counts = carry
            block_x, block_ids = pieces
            hot_table = (block_ids[:, None] == cluster_range[None, :]).astype(jnp.bfloat16)
            totals = totals + lax.dot_general(
                hot_table, block_x, (((0,), (0,)), ((), ())), preferred_element_type=jnp.float32
            )
            counts = counts + jnp.sum(hot_table, axis=0, dtype=jnp.float32)
            return ((totals, counts), None)

        start = (
            jnp.zeros((clusters, feat_width), jnp.float32),
            jnp.zeros((clusters,), jnp.float32),
        )
        result, unused = lax.scan(
            add_block, start, (row_blocks, cluster_ids.reshape(block_count, block_rows))
        )
        return result

    start_table = initial_centroids.reshape(clusters, feat_width).astype(jnp.float32)

    def update(earlier, cluster_ids):
        totals, counts = local_totals(cluster_ids)
        totals, counts = over_members(totals, counts)
        centre = (totals + PRIOR * earlier) / (counts[:, None] + PRIOR)
        return (centre, centre.astype(jnp.bfloat16))

    centre_one, rounded_one = update(start_table, ids_one)
    assigned = jnp.take(rounded_one, jnp.maximum(ids_one, 0), axis=0).astype(jnp.float32)
    first_local = (
        squares
        - 2.0 * jnp.sum(got_rows.astype(jnp.float32) * assigned, axis=1)
        + jnp.sum(assigned * assigned, axis=1)
    ) / feat_width
    centre_two, rounded_two = update(centre_one, ids_two)
    centre_squares = jnp.sum(jnp.square(rounded_two.astype(jnp.float32)), axis=1).reshape(
        group_codes, codes_two
    )
    code_range = jnp.arange(group_codes, dtype=jnp.int32)

    def score_block(pieces):
        block_x, block_offsets, block_sq = pieces
        raw = lax.dot_general(
            rounded_two, block_x, (((1,), (1,)), ((), ())), preferred_element_type=jnp.float32
        )
        raw = raw.reshape(group_codes, codes_two, block_rows)
        select = (block_offsets[None, :] == code_range[:, None]).astype(jnp.float32)
        inner = jnp.sum(raw * select[:, None, :], axis=0)
        norms = jnp.sum(centre_squares[:, :, None] * select[:, None, :], axis=0)
        return (block_sq[None, :] - 2.0 * inner + norms) / feat_width

    scored = lax.map(
        score_block,
        (
            row_blocks,
            offsets.reshape(block_count, block_rows),
            squares.reshape(block_count, block_rows),
        ),
    )
    all_local = jnp.transpose(scored, (1, 0, 2)).reshape(codes_two, slot_total)
    one_local = first_local[None, :]
    back_all, back_one = (
        lax.all_to_all(all_local, ("grp", "mem"), split_axis=1, concat_axis=1, tiled=True),
        lax.all_to_all(one_local, ("grp", "mem"), split_axis=1, concat_axis=1, tiled=True),
    )
    distances = jnp.take(back_all, slot_index, axis=1)
    first_distance = jnp.take(back_one[0], slot_index, axis=0)
    return (distances, first_distance)


def quick(embeddings, initial_centroids, row_owner, prefix_offset, first_assign, second_assign):
    rows, feat = embeddings.shape
    group_codes, codes_two = initial_centroids.shape[:2]
    groups = lax.axis_size("grp")
    members = lax.axis_size("mem")
    chips = groups // CORES * members
    total = chips * BLOCK
    shape = jax.ShapeDtypeStruct
    vmem = pl.BlockSpec(memory_space=pltpu.VMEM)
    beside = pl.CostEstimate(flops=2_000_000_000, bytes_accessed=10_000_000, transcendentals=0)
    same_core = [
        [group * members + member for group in range(core, groups, CORES) for member in range(members)]
        for core in range(CORES)
    ]

    def swap(array):
        blocks = array.reshape(chips, array.shape[0] // chips, array.shape[1])
        blocks = lax.all_to_all(
            blocks, ("grp", "mem"), split_axis=0, concat_axis=0, axis_index_groups=same_core, tiled=True
        )
        return blocks.reshape(array.shape)

    def other_core(array):
        return lax.ppermute(array, "grp", [(group, group ^ 1) for group in range(groups)])

    move, info = call(
        lambda *refs: split_kernel(members, group_codes, *refs),
        [shape((MOVED, feat), jnp.bfloat16), shape((8, rows), jnp.int32)],
        [
            row_owner.reshape(1, rows),
            prefix_offset.reshape(1, rows),
            first_assign.reshape(1, rows),
            second_assign.reshape(1, rows),
            embeddings,
        ],
    )
    any_memory = pl.BlockSpec(memory_space=pl.ANY)
    send, slot, came_slot, own_start = call(
        lambda *refs: pack_kernel(members, *refs),
        [
            shape((total, feat), jnp.bfloat16),
            shape((1, rows), jnp.int32),
            shape((8, LANES), jnp.int32),
            shape((SECTION, feat), jnp.bfloat16),
        ],
        [embeddings, info, other_core(move), initial_centroids],
        in_memory=[any_memory, vmem, vmem, any_memory],
        scratch=[
            pltpu.VMEM((rows, feat), jnp.bfloat16),
            pltpu.VMEM((codes_two, feat), jnp.bfloat16),
            pltpu.SemaphoreType.DMA((2,)),
        ],
    )
    other_start = other_core(own_start)
    got = swap(send)
    part, label = call(
        sums_kernel,
        [shape((2 * CORES * SECTION, feat), jnp.bfloat16), shape((8, total), jnp.float32)],
        [got],
    )
    other_part = other_core(part)
    key, squares = call(
        prepare_kernel,
        [shape((total, LANES), jnp.float32)] * 2,
        [got, label],
        cost=beside,
    )
    (record,) = call(
        lambda *refs: score_kernel(codes_two, *refs),
        [shape((total, LANES), jnp.bfloat16)],
        [got, part, other_part, own_start, other_start, key, squares],
    )
    back = swap(record)
    (came_back,) = call(return_kernel, [shape((MOVED, LANES), jnp.bfloat16)], [back, came_slot])
    other_back = other_core(came_back)
    (gathered,) = call(gather_kernel, [shape((LANES, rows), jnp.float32)], [back, slot], cost=beside)
    return call(
        unpack_kernel,
        [shape((codes_two, rows), jnp.float32), shape((1, rows), jnp.float32), shape((1, 1), jnp.float32)],
        [gathered, came_back, other_back, info],
        out_memory=[vmem, vmem, pl.BlockSpec(memory_space=pltpu.SMEM)],
    )


def body(*inputs):
    distances, first_distance, full = quick(*inputs)
    return lax.cond(
        full[0, 0] > 0.5,
        lambda kept, given: general(*given),
        lambda kept, given: kept,
        (distances, first_distance[0]),
        inputs,
    )


def solution(mesh):
    placed = (
        P(("grp", "mem"), None),
        P("grp", None, None),
        P(("grp", "mem"), None),
        P(("grp", "mem")),
        P(("grp", "mem")),
        P(("grp", "mem")),
    )
    return jax.shard_map(
        body,
        mesh=mesh,
        in_specs=placed,
        out_specs=(P(None, ("grp", "mem")), P(("grp", "mem"))),
        check_vma=False,
    )
```

```python
import jax
import jax.numpy as jnp
from jax import lax
from jax.experimental import pallas as pl
from jax.experimental.pallas import tpu as pltpu
from jax.sharding import PartitionSpec as P

PRIOR = 16
BLOCK = 24
KEEP = 22
MOVED = 16
LANES = 128
CORES = 2
SECTION = 112
SECOND, CHIP = 256, 256 * 128
FULL = 128
STEP_SCORE = 384
ROUNDING_BLOCK = 4.5e-4
ROUNDING_ALL = 2.5e-4
NT = (((1,), (1,)), ((), ()))
VMEM_LIMIT = 48 * 1024 * 1024


def iota(shape, dim):
    return lax.broadcasted_iota(jnp.int32, shape, dim)


def hot(condition):
    return jnp.where(condition, 1.0, 0.0).astype(jnp.bfloat16)


def dot(a, b):
    return jnp.dot(a, b, preferred_element_type=jnp.float32)


def dot_nt(a, b):
    return lax.dot_general(a, b, NT, preferred_element_type=jnp.float32)


def three_terms(values):
    high = values.astype(jnp.bfloat16)
    rest = values - high.astype(jnp.float32)
    middle = rest.astype(jnp.bfloat16)
    low = (rest - middle.astype(jnp.float32)).astype(jnp.bfloat16)
    return high, middle, low


def call(kernel, out_shape, args, out_memory=None, in_memory=None, scratch=()):
    vmem = pl.BlockSpec(memory_space=pltpu.VMEM)
    return pl.pallas_call(
        kernel,
        out_shape=out_shape,
        in_specs=in_memory or [vmem] * len(args),
        out_specs=out_memory or [vmem] * len(out_shape),
        scratch_shapes=scratch,
        compiler_params=pltpu.CompilerParams(vmem_limit_bytes=VMEM_LIMIT),
    )(*args)


def rank_in_bin(member):
    bins = hot(member)
    before = hot(iota((LANES, LANES), 0) < iota((LANES, LANES), 1))
    base = jnp.zeros((member.shape[0], 1), jnp.float32)
    ranks = []
    for begin in range(0, member.shape[1], LANES):
        piece = bins[:, begin : begin + LANES]
        ranks.append(dot(piece, before) + base)
        base = base + jnp.sum(piece.astype(jnp.float32), axis=1, keepdims=True)
    rank = jnp.concatenate(ranks, axis=1)
    return jnp.sum(jnp.where(member, rank, 0.0), axis=0, keepdims=True)


def column_of(row):
    diagonal = iota((LANES, LANES), 0) == iota((LANES, LANES), 1)
    pieces = []
    for begin in range(0, row.shape[1], LANES):
        piece = jnp.where(diagonal, row[:, begin : begin + LANES], 0.0)
        pieces.append(jnp.sum(piece, axis=1, keepdims=True))
    return jnp.concatenate(pieces, axis=0)


def highest(values):
    return jnp.max(values, axis=(0, 1), keepdims=True)


def split_kernel(
    members, group_codes, owner_ref, offset_ref, first_ref, second_ref, x_ref, move_ref, info_ref
):
    rows, feat = x_ref.shape
    chips = lax.axis_size("grp") // CORES * members
    group = owner_ref[...] // members
    code = group * group_codes + offset_ref[...]
    chip = (group // CORES) * members + code % members
    rank = rank_in_bin(iota((chips, rows), 0) == chip).astype(jnp.int32)
    moves = rank >= KEEP
    place = rank_in_bin((iota((16, rows), 0) == 0) & moves).astype(jnp.int32)
    fits = place < MOVED - 1
    full = highest(jnp.where(moves & ~fits, 1.0, 0.0))
    place = jnp.where(moves & fits, place, -1)
    labels = first_ref[...] + 1 + LANES * (group % CORES) + SECOND * second_ref[...] + CHIP * chip
    info = [chip, rank, place, labels, jnp.broadcast_to(full.astype(jnp.int32), (1, rows))]
    info_ref[...] = jnp.concatenate(info + [jnp.zeros((3, rows), jnp.int32)], axis=0)
    column = column_of(labels.astype(jnp.float32))
    packed = jnp.where(column_of(place.astype(jnp.float32)) == iota((1, LANES), 1).astype(jnp.float32), column, 0.0)
    packed = jnp.sum(packed, axis=0, keepdims=True).astype(jnp.int32)
    last = [packed % SECOND, (packed // SECOND) % LANES, packed // CHIP]
    last = [part.astype(jnp.float32) for part in last] + [jnp.broadcast_to(full, (1, feat - 3 * LANES))]
    last = jnp.concatenate(last, axis=1)
    moved = dot(hot(iota((MOVED, rows), 0) == place), x_ref[...])
    move_ref[...] = jnp.where(iota((MOVED, feat), 0) == MOVED - 1, last, moved).astype(jnp.bfloat16)


def pack_kernel(
    members, x_ref, info_ref, came_ref, start_ref, send_ref, slot_ref, came_slot_ref, own_start_ref, x, mine, sem
):
    rows, feat = x_ref.shape
    group_codes, codes_two = start_ref.shape[:2]
    offset = (lax.axis_index("mem") + members * group_codes - group_codes * lax.axis_index("grp")) % members
    fetch_start = pltpu.make_async_copy(start_ref.at[jnp.minimum(offset, group_codes - 1)], mine, sem.at[1])
    fetch = pltpu.make_async_copy(x_ref, x, sem.at[0])
    fetch.start()
    fetch_start.start()
    chips = send_ref.shape[0] // BLOCK
    run = feat // 2
    in_run = run // BLOCK
    chip, rank, labels = info_ref[0:1, :], info_ref[1:2, :], info_ref[3:4, :]
    full = info_ref[4:5, 0:1].astype(jnp.float32)
    kept = rank < KEEP
    slot = jnp.where(kept, chip * BLOCK + rank, -1)
    slot_ref[...] = slot
    kept_of = jnp.sum(hot((iota((chips, rows), 0) == chip) & kept).astype(jnp.float32), axis=1, keepdims=True)
    came = came_ref[...]
    came_last = came.astype(jnp.float32)[MOVED - 1 : MOVED]
    came_first = came_last[:, 0:LANES]
    came_chip = came_last[:, 2 * LANES : 3 * LANES]
    member = (iota((chips, LANES), 0).astype(jnp.float32) == came_chip) & (came_first > 0.5)
    after = jnp.sum(jnp.where(member, kept_of, 0.0), axis=0, keepdims=True) + rank_in_bin(member)
    fits = after < BLOCK - 1
    is_live = came_first > 0.5
    full = jnp.maximum(full, came_last[:, 3 * LANES : 3 * LANES + 1])
    full = jnp.maximum(full, highest(jnp.where(is_live & ~fits, 1.0, 0.0)))
    came_slot = jnp.where(is_live & fits, came_chip * BLOCK + after, -1.0)
    came_slot_ref[...] = jnp.broadcast_to(came_slot, (8, LANES)).astype(jnp.int32)
    came_labels = came_first + SECOND * came_last[:, LANES : 2 * LANES]
    label_column = jnp.concatenate(
        [column_of((labels % CHIP).astype(jnp.float32)), column_of(came_labels)[:MOVED]], axis=0
    )
    slot_column = jnp.concatenate([column_of(slot.astype(jnp.float32)), column_of(came_slot)[:MOVED]], axis=0)
    came_slot = came_slot.astype(jnp.int32)
    source, target = iota((run, run), 0).astype(jnp.float32), iota((run, run), 1).astype(jnp.float32)
    source = source - jnp.floor((source + 0.5) * (1.0 / BLOCK)) * BLOCK
    begin = ((lax.axis_index("mem") % in_run) * BLOCK).astype(jnp.float32)
    turn = hot(target == begin + source)
    block_of = jnp.floor((iota((in_run, run), 1).astype(jnp.float32) + 0.5) * (1.0 / BLOCK))
    in_block = block_of == iota((in_run, run), 0).astype(jnp.float32)
    lane = iota((1, LANES), 1).astype(jnp.float32)
    packed = []
    for at in range(0, chips * BLOCK, LANES):
        part = jnp.where(slot_column == lane + at, label_column, 0.0)
        packed.append(jnp.sum(part, axis=0, keepdims=True).astype(jnp.int32))
    packed = jnp.concatenate(packed, axis=1)
    labels = [(packed % SECOND).astype(jnp.float32), (packed // SECOND).astype(jnp.float32) + FULL * full]
    last = [
        jnp.where(in_block, part[:, at : at + run], 0.0)
        for part in labels
        for at in range(0, chips * BLOCK, run)
    ]
    last = dot(jnp.concatenate(last, axis=0).astype(jnp.bfloat16), turn)
    last = jnp.concatenate([last[:chips], last[chips:]], axis=1).astype(jnp.bfloat16)
    extra = jnp.concatenate([last, came], axis=0)
    lane_id = iota((1, LANES), 1)
    position = jnp.concatenate([came_slot[:, :MOVED], jnp.full((1, LANES - MOVED), -1, jnp.int32)], axis=1)
    position = jnp.where(lane_id < chips, lane_id * BLOCK + BLOCK - 1, pltpu.roll(position, chips, 1))
    position = position[:, : chips + MOVED]
    fetch_start.wait()
    own_start_ref[...] = jnp.zeros((SECTION, feat), jnp.bfloat16)
    own_start_ref[0:codes_two, :] = mine[...]
    fetch.wait()
    step = chips * BLOCK // 2
    for begin in range(0, chips * BLOCK, step):
        moved = dot(hot(iota((step, rows), 0) + begin == slot), x[...])
        moved = moved + dot(hot(iota((step, chips + MOVED), 0) + begin == position), extra)
        send_ref[begin : begin + step, :] = moved.astype(jnp.bfloat16)


def row_of(column):
    diagonal = iota((LANES, LANES), 0) == iota((LANES, LANES), 1)
    return jnp.sum(jnp.where(diagonal, column, 0.0), axis=0, keepdims=True)


def sums_kernel(got_ref, part_ref, label_ref):
    total, feat = got_ref.shape
    run = feat // 2
    runs = []
    for begin in range(0, total, run):
        row = jnp.zeros((1, feat), jnp.float32)
        for at in range(begin, begin + run, BLOCK):
            row = row + got_ref[at + BLOCK - 8 : at + BLOCK, :].astype(jnp.float32)[7:8, :]
        runs.append(row)
    first = jnp.concatenate([row[:, :run] for row in runs], axis=1) - 1.0
    second = jnp.concatenate([row[:, run:] for row in runs], axis=1)
    full = jnp.where(jnp.max(second) >= FULL, 1.0, 0.0)
    second = jnp.where(second >= FULL, second - FULL, second)
    second = jnp.where(first >= LANES, second + LANES, second)
    second = jnp.where(first >= 0.0, second, -1.0)
    label_ref[...] = jnp.broadcast_to(first, (8, total))
    x = got_ref[...]
    cluster = iota((CORES * LANES, total), 0).astype(jnp.float32)
    is_count = iota((SECTION, feat), 0) == SECTION - 1
    member = hot(jnp.concatenate([cluster == first, cluster == second], axis=0))
    totals = dot(member, x)
    counts = jnp.sum(member.astype(jnp.float32), axis=1, keepdims=True)
    for section in range(2 * CORES):
        begin, at = section * LANES, section * SECTION
        count = row_of(counts[begin : begin + LANES])
        large = jnp.floor(count * (1.0 / LANES))
        count = [large, count - large * LANES, jnp.full((1, feat - 2 * LANES), full, jnp.float32)]
        count = jnp.concatenate(count, axis=1)
        sums = jnp.where(is_count, count, totals[begin : begin + SECTION])
        part_ref[at : at + SECTION, :] = sums.astype(jnp.bfloat16)


def prepare_kernel(got_ref, label_ref, key_ref, squares_ref):
    total, feat = got_ref.shape
    diagonal = iota((LANES, LANES), 0) == iota((LANES, LANES), 1)
    ones = jnp.ones((LANES, LANES), jnp.bfloat16)
    for begin in range(0, total, STEP_SCORE):
        key = [
            jnp.where(diagonal, label_ref[0:1, at : at + LANES], 0.0)
            for at in range(begin, begin + STEP_SCORE, LANES)
        ]
        key = jnp.concatenate(key, axis=0).astype(jnp.bfloat16)
        key_ref[begin : begin + STEP_SCORE, :] = dot(key, ones)
        wide = got_ref[begin : begin + STEP_SCORE, :].astype(jnp.float32)
        squares = jnp.sum(wide * wide, axis=1, keepdims=True) * (1.0 / feat)
        squares_ref[begin : begin + STEP_SCORE, :] = jnp.broadcast_to(squares, (STEP_SCORE, LANES))


def score_kernel(
    codes_two, got_ref, own_ref, other_ref, own_start_ref, other_start_ref, key_ref, squares_ref, out_ref
):
    total, feat = got_ref.shape
    my_core = lax.axis_index("grp") % CORES
    count_row = SECTION - 1

    def both(at):
        own = own_ref[at : at + SECTION, :].astype(jnp.float32)
        return own + other_ref[at : at + SECTION, :].astype(jnp.float32)

    full = jnp.zeros((1, 1), jnp.float32)
    rounded, squares_of = [], []
    starts = [ref[...].astype(jnp.float32) for ref in (own_start_ref, other_start_ref)]
    for core in range(CORES):
        centre = jnp.where(my_core == core, starts[0], starts[1])
        for update in range(2):
            sums = both((update * CORES + core) * SECTION)
            counts = sums[count_row : count_row + 1]
            full = jnp.maximum(full, counts[:, 2 * LANES : 2 * LANES + 1])
            counts = column_of(counts[:, :LANES] * LANES + counts[:, LANES : 2 * LANES])
            centre = (sums + PRIOR * centre) * (1.0 / (counts[:SECTION] + PRIOR))
            narrow = jnp.concatenate(
                [centre.astype(jnp.bfloat16), jnp.zeros((LANES - SECTION, feat), jnp.bfloat16)], axis=0
            )
            wide = narrow.astype(jnp.float32)
            rounded.append(narrow)
            squares_of.append(row_of(jnp.sum(wide * wide, axis=1, keepdims=True)) * (1.0 / feat))
    full = jnp.max(full)
    table = jnp.concatenate(rounded, axis=0)
    lane = iota((STEP_SCORE, LANES), 1)
    is_score = lane < codes_two
    lane_value = lane.astype(jnp.float32)
    ones = jnp.ones((LANES, LANES), jnp.bfloat16)
    spread = iota((2 * LANES, LANES), 0) // LANES
    spread = hot(iota((2 * LANES, LANES), 1) == codes_two + 1 + spread)
    excess_all = jnp.zeros((STEP_SCORE, LANES), jnp.float32)
    excess_block = []

    def across(values):
        return dot(values.astype(jnp.bfloat16), ones)

    for begin in range(0, total, STEP_SCORE):
        x = got_ref[begin : begin + STEP_SCORE, :]
        inner = dot_nt(x, table)
        key = key_ref[begin : begin + STEP_SCORE, :]
        is_other = key >= LANES
        first = jnp.where(is_other, key - LANES, key)
        squares = squares_ref[begin : begin + STEP_SCORE, :]

        def distance(update):
            low, high = [
                squares_of[at] - (2.0 / feat) * inner[:, at * LANES : (at + 1) * LANES]
                for at in (update, 2 + update)
            ]
            return squares + jnp.where(is_other, high, low)

        near = jnp.where(lane_value == first, distance(0), 0.0)
        near_high = near.astype(jnp.bfloat16)
        near_low = (near - near_high.astype(jnp.float32)).astype(jnp.bfloat16)
        score = jnp.where(is_score, distance(1), 0.0)
        mean = (across(score) * (1.0 / codes_two)).astype(jnp.bfloat16).astype(jnp.float32)
        rest = jnp.where(is_score, score - mean, 0.0)
        record = rest.astype(jnp.bfloat16).astype(jnp.float32)
        lost = rest - record
        is_live = key >= 0.0
        lost = jnp.where(is_live, lost * lost, 0.0)
        sent = jnp.where(is_live, score * score, 0.0)
        excess_all = excess_all + (lost - (ROUNDING_ALL * ROUNDING_ALL) * sent)
        excess = lost - (ROUNDING_BLOCK * ROUNDING_BLOCK) * sent
        excess = jnp.sum(excess.reshape(STEP_SCORE // BLOCK, BLOCK // 8, 8, LANES), axis=1)
        excess_block.append(excess.reshape(STEP_SCORE // BLOCK * 8, LANES))
        near = dot(jnp.concatenate([near_high, near_low], axis=1), spread)
        record = jnp.where(lane == codes_two, mean, record + near)
        out_ref[begin : begin + STEP_SCORE, :] = record.astype(jnp.bfloat16)
    excess = across(jnp.concatenate(excess_block, axis=0))
    excess = jnp.sum(excess.reshape(total // BLOCK, 8, LANES), axis=1)
    full = jnp.maximum(full, jnp.where(jnp.max(excess) > 0.0, 1.0, 0.0))
    full = jnp.maximum(full, jnp.where(jnp.sum(excess_all) > 0.0, 1.0, 0.0))
    for begin in range(0, total, STEP_SCORE):
        record = out_ref[begin : begin + STEP_SCORE, :].astype(jnp.float32)
        record = jnp.where(lane == LANES - 1, full, record)
        out_ref[begin : begin + STEP_SCORE, :] = record.astype(jnp.bfloat16)


def return_kernel(got_ref, came_slot_ref, out_ref):
    total = got_ref.shape[0]
    got = got_ref[...]
    full = highest(jnp.where(iota((total, LANES), 1) == LANES - 1, got.astype(jnp.float32), 0.0))
    slot = column_of(came_slot_ref[0:1, :].astype(jnp.float32))[:MOVED]
    moved = dot(hot(iota((MOVED, total), 1).astype(jnp.float32) == slot), got)
    out_ref[...] = jnp.where(iota((MOVED, LANES), 1) == LANES - 1, full, moved).astype(jnp.bfloat16)


def gather_kernel(got_ref, slot_ref, out_ref):
    total = got_ref.shape[0]
    rows = slot_ref.shape[1]
    out_ref[...] = dot(got_ref[...].T, hot(iota((total, rows), 0) == slot_ref[...]))


def unpack_kernel(gathered_ref, own_ref, back_ref, info_ref, all_ref, one_ref, full_ref):
    rows = info_ref.shape[1]
    codes_two = all_ref.shape[0]
    back = back_ref[...].astype(jnp.float32)
    full = jnp.maximum(own_ref[...].astype(jnp.float32), back)
    full_ref[0, 0] = jnp.max(full[:, LANES - 1 :])
    moved = dot(back.T.astype(jnp.bfloat16), hot(iota((MOVED, rows), 0) == info_ref[2:3, :]))
    moved = gathered_ref[...] + moved
    mean = moved[codes_two : codes_two + 1]
    near = moved[codes_two + 1 : codes_two + 2] + moved[codes_two + 2 : codes_two + 3]
    all_ref[...] = moved[:codes_two] + mean
    one_ref[...] = near


def over_members(totals, counts):
    members = lax.axis_size("mem")
    clusters, feat = totals.shape
    share = -(-clusters // members)

    def swap(blocks):
        return lax.all_to_all(blocks, "mem", split_axis=0, concat_axis=0, tiled=True)

    padded = jnp.pad(totals.astype(jnp.bfloat16), ((0, members * share - clusters), (0, 0)))
    own = jnp.sum(swap(padded.reshape(members, share, feat)).astype(jnp.float32), axis=0)
    own = jnp.broadcast_to(own.astype(jnp.bfloat16)[None], (members, share, feat))
    summed = swap(own).reshape(members * share, feat)[:clusters].astype(jnp.float32)
    counted = jnp.sum(swap(jnp.broadcast_to(counts[None], (members, clusters))), axis=0)
    return summed, counted


def pick_block(total):
    for candidate in range(1024, 0, -1):
        if total % candidate == 0:
            return candidate
    return total


def general(embeddings, initial_centroids, row_owner, prefix_offset, first_assign, second_assign):
    row_count, feat_width = embeddings.shape
    group_codes = initial_centroids.shape[0]
    codes_two = initial_centroids.shape[1]
    clusters = group_codes * codes_two
    group_count = lax.axis_size("grp")
    member_count = lax.axis_size("mem")
    devices_all = group_count * member_count
    capacity = 2 * row_count // devices_all + 4
    slot_total = devices_all * capacity
    target = row_owner[:, 0]
    dest_table = (target[:, None] == jnp.arange(devices_all, dtype=jnp.int32)[None, :]).astype(
        jnp.int32
    )
    slot_rank = jnp.sum(jnp.cumsum(dest_table, axis=0) * dest_table, axis=1) - 1
    slot_index = target * capacity + slot_rank
    send_rows = jnp.zeros((slot_total, feat_width), jnp.bfloat16).at[slot_index].set(embeddings)
    labels = jnp.stack([prefix_offset, first_assign, second_assign], axis=1)
    send_labels = jnp.full((slot_total, 3), -1, jnp.int32).at[slot_index].set(labels)
    got_rows, got_labels = (
        lax.all_to_all(send_rows, ("grp", "mem"), split_axis=0, concat_axis=0, tiled=True),
        lax.all_to_all(send_labels, ("grp", "mem"), split_axis=0, concat_axis=0, tiled=True),
    )
    offsets = got_labels[:, 0]
    live = offsets >= 0
    ids_one = jnp.where(live, offsets * codes_two + got_labels[:, 1], -1)
    ids_two = jnp.where(live, offsets * codes_two + got_labels[:, 2], -1)
    squares = jnp.sum(jnp.square(got_rows.astype(jnp.float32)), axis=1)
    block_rows = pick_block(slot_total)
    block_count = slot_total // block_rows
    row_blocks = got_rows.reshape(block_count, block_rows, feat_width)
    cluster_range = jnp.arange(clusters, dtype=jnp.int32)

    def local_totals(cluster_ids):

        def add_block(carry, pieces):
            totals, counts = carry
            block_x, block_ids = pieces
            hot_table = (block_ids[:, None] == cluster_range[None, :]).astype(jnp.bfloat16)
            totals = totals + lax.dot_general(
                hot_table, block_x, (((0,), (0,)), ((), ())), preferred_element_type=jnp.float32
            )
            counts = counts + jnp.sum(hot_table, axis=0, dtype=jnp.float32)
            return ((totals, counts), None)

        start = (
            jnp.zeros((clusters, feat_width), jnp.float32),
            jnp.zeros((clusters,), jnp.float32),
        )
        result, unused = lax.scan(
            add_block, start, (row_blocks, cluster_ids.reshape(block_count, block_rows))
        )
        return result

    start_table = initial_centroids.reshape(clusters, feat_width).astype(jnp.float32)

    def update(earlier, cluster_ids):
        totals, counts = local_totals(cluster_ids)
        totals, counts = over_members(totals, counts)
        centre = (totals + PRIOR * earlier) / (counts[:, None] + PRIOR)
        return (centre, centre.astype(jnp.bfloat16))

    centre_one, rounded_one = update(start_table, ids_one)
    assigned = jnp.take(rounded_one, jnp.maximum(ids_one, 0), axis=0).astype(jnp.float32)
    first_local = (
        squares
        - 2.0 * jnp.sum(got_rows.astype(jnp.float32) * assigned, axis=1)
        + jnp.sum(assigned * assigned, axis=1)
    ) / feat_width
    centre_two, rounded_two = update(centre_one, ids_two)
    centre_squares = jnp.sum(jnp.square(rounded_two.astype(jnp.float32)), axis=1).reshape(
        group_codes, codes_two
    )
    code_range = jnp.arange(group_codes, dtype=jnp.int32)

    def score_block(pieces):
        block_x, block_offsets, block_sq = pieces
        raw = lax.dot_general(
            rounded_two, block_x, (((1,), (1,)), ((), ())), preferred_element_type=jnp.float32
        )
        raw = raw.reshape(group_codes, codes_two, block_rows)
        select = (block_offsets[None, :] == code_range[:, None]).astype(jnp.float32)
        inner = jnp.sum(raw * select[:, None, :], axis=0)
        norms = jnp.sum(centre_squares[:, :, None] * select[:, None, :], axis=0)
        return (block_sq[None, :] - 2.0 * inner + norms) / feat_width

    scored = lax.map(
        score_block,
        (
            row_blocks,
            offsets.reshape(block_count, block_rows),
            squares.reshape(block_count, block_rows),
        ),
    )
    all_local = jnp.transpose(scored, (1, 0, 2)).reshape(codes_two, slot_total)
    one_local = first_local[None, :]
    back_all, back_one = (
        lax.all_to_all(all_local, ("grp", "mem"), split_axis=1, concat_axis=1, tiled=True),
        lax.all_to_all(one_local, ("grp", "mem"), split_axis=1, concat_axis=1, tiled=True),
    )
    distances = jnp.take(back_all, slot_index, axis=1)
    first_distance = jnp.take(back_one[0], slot_index, axis=0)
    return (distances, first_distance)


def quick(embeddings, initial_centroids, row_owner, prefix_offset, first_assign, second_assign):
    rows, feat = embeddings.shape
    group_codes, codes_two = initial_centroids.shape[:2]
    groups = lax.axis_size("grp")
    members = lax.axis_size("mem")
    chips = groups // CORES * members
    total = chips * BLOCK
    shape = jax.ShapeDtypeStruct
    vmem = pl.BlockSpec(memory_space=pltpu.VMEM)
    same_core = [
        [group * members + member for group in range(core, groups, CORES) for member in range(members)]
        for core in range(CORES)
    ]

    def swap(array):
        blocks = array.reshape(chips, array.shape[0] // chips, array.shape[1])
        blocks = lax.all_to_all(
            blocks, ("grp", "mem"), split_axis=0, concat_axis=0, axis_index_groups=same_core, tiled=True
        )
        return blocks.reshape(array.shape)

    def other_core(array):
        return lax.ppermute(array, "grp", [(group, group ^ 1) for group in range(groups)])

    move, info = call(
        lambda *refs: split_kernel(members, group_codes, *refs),
        [shape((MOVED, feat), jnp.bfloat16), shape((8, rows), jnp.int32)],
        [
            row_owner.reshape(1, rows),
            prefix_offset.reshape(1, rows),
            first_assign.reshape(1, rows),
            second_assign.reshape(1, rows),
            embeddings,
        ],
    )
    any_memory = pl.BlockSpec(memory_space=pl.ANY)
    send, slot, came_slot, own_start = call(
        lambda *refs: pack_kernel(members, *refs),
        [
            shape((total, feat), jnp.bfloat16),
            shape((1, rows), jnp.int32),
            shape((8, LANES), jnp.int32),
            shape((SECTION, feat), jnp.bfloat16),
        ],
        [embeddings, info, other_core(move), initial_centroids],
        in_memory=[any_memory, vmem, vmem, any_memory],
        scratch=[
            pltpu.VMEM((rows, feat), jnp.bfloat16),
            pltpu.VMEM((codes_two, feat), jnp.bfloat16),
            pltpu.SemaphoreType.DMA((2,)),
        ],
    )
    other_start = other_core(own_start)
    got = swap(send)
    part, label = call(
        sums_kernel,
        [shape((2 * CORES * SECTION, feat), jnp.bfloat16), shape((8, total), jnp.float32)],
        [got],
    )
    other_part = other_core(part)
    key, squares = call(
        prepare_kernel,
        [shape((total, LANES), jnp.float32)] * 2,
        [got, label],
    )
    (record,) = call(
        lambda *refs: score_kernel(codes_two, *refs),
        [shape((total, LANES), jnp.bfloat16)],
        [got, part, other_part, own_start, other_start, key, squares],
    )
    back = swap(record)
    (came_back,) = call(return_kernel, [shape((MOVED, LANES), jnp.bfloat16)], [back, came_slot])
    other_back = other_core(came_back)
    (gathered,) = call(gather_kernel, [shape((LANES, rows), jnp.float32)], [back, slot])
    return call(
        unpack_kernel,
        [shape((codes_two, rows), jnp.float32), shape((1, rows), jnp.float32), shape((1, 1), jnp.float32)],
        [gathered, came_back, other_back, info],
        out_memory=[vmem, vmem, pl.BlockSpec(memory_space=pltpu.SMEM)],
    )


def body(*inputs):
    distances, first_distance, full = quick(*inputs)
    return lax.cond(
        full[0, 0] > 0.5,
        lambda kept, given: general(*given),
        lambda kept, given: kept,
        (distances, first_distance[0]),
        inputs,
    )


def solution(mesh):
    placed = (
        P(("grp", "mem"), None),
        P("grp", None, None),
        P(("grp", "mem"), None),
        P(("grp", "mem")),
        P(("grp", "mem")),
        P(("grp", "mem")),
    )
    return jax.shard_map(
        body,
        mesh=mesh,
        in_specs=placed,
        out_specs=(P(None, ("grp", "mem")), P(("grp", "mem"))),
        check_vma=False,
    )
```

```python
import jax
import jax.numpy as jnp
from jax import lax
from jax.experimental import pallas as pl
from jax.experimental.pallas import tpu as pltpu
from jax.sharding import PartitionSpec as P

PRIOR = 16
BLOCK = 24
KEEP = 22
MOVED = 16
LANES = 128
CORES = 2
SECTION = 112
SECOND, CHIP = 256, 256 * 128
FULL = 128
STEP_SCORE = 384
ROUNDING_BLOCK = 4.5e-4
ROUNDING_ALL = 2.5e-4
NT = (((1,), (1,)), ((), ()))
VMEM_LIMIT = 48 * 1024 * 1024


def iota(shape, dim):
    return lax.broadcasted_iota(jnp.int32, shape, dim)


def hot(condition):
    return jnp.where(condition, 1.0, 0.0).astype(jnp.bfloat16)


def dot(a, b):
    return jnp.dot(a, b, preferred_element_type=jnp.float32)


def dot_nt(a, b):
    return lax.dot_general(a, b, NT, preferred_element_type=jnp.float32)


def three_terms(values):
    high = values.astype(jnp.bfloat16)
    rest = values - high.astype(jnp.float32)
    middle = rest.astype(jnp.bfloat16)
    low = (rest - middle.astype(jnp.float32)).astype(jnp.bfloat16)
    return high, middle, low


def call(kernel, out_shape, args, out_memory=None, in_memory=None, scratch=()):
    vmem = pl.BlockSpec(memory_space=pltpu.VMEM)
    return pl.pallas_call(
        kernel,
        out_shape=out_shape,
        in_specs=in_memory or [vmem] * len(args),
        out_specs=out_memory or [vmem] * len(out_shape),
        scratch_shapes=scratch,
        compiler_params=pltpu.CompilerParams(vmem_limit_bytes=VMEM_LIMIT),
    )(*args)


def rank_in_bin(member):
    bins = hot(member)
    before = hot(iota((LANES, LANES), 0) < iota((LANES, LANES), 1))
    base = jnp.zeros((member.shape[0], 1), jnp.float32)
    ranks = []
    for begin in range(0, member.shape[1], LANES):
        piece = bins[:, begin : begin + LANES]
        ranks.append(dot(piece, before) + base)
        base = base + jnp.sum(piece.astype(jnp.float32), axis=1, keepdims=True)
    rank = jnp.concatenate(ranks, axis=1)
    return jnp.sum(jnp.where(member, rank, 0.0), axis=0, keepdims=True)


def column_of(row):
    diagonal = iota((LANES, LANES), 0) == iota((LANES, LANES), 1)
    pieces = []
    for begin in range(0, row.shape[1], LANES):
        piece = jnp.where(diagonal, row[:, begin : begin + LANES], 0.0)
        pieces.append(jnp.sum(piece, axis=1, keepdims=True))
    return jnp.concatenate(pieces, axis=0)


def highest(values):
    return jnp.max(values, axis=(0, 1), keepdims=True)


def split_kernel(
    members, group_codes, owner_ref, offset_ref, first_ref, second_ref, x_ref, move_ref, info_ref
):
    rows, feat = x_ref.shape
    chips = lax.axis_size("grp") // CORES * members
    group = owner_ref[...] // members
    code = group * group_codes + offset_ref[...]
    chip = (group // CORES) * members + code % members
    rank = rank_in_bin(iota((chips, rows), 0) == chip).astype(jnp.int32)
    moves = rank >= KEEP
    place = rank_in_bin((iota((16, rows), 0) == 0) & moves).astype(jnp.int32)
    fits = place < MOVED - 1
    full = highest(jnp.where(moves & ~fits, 1.0, 0.0))
    place = jnp.where(moves & fits, place, -1)
    labels = first_ref[...] + 1 + LANES * (group % CORES) + SECOND * second_ref[...] + CHIP * chip
    info = [chip, rank, place, labels, jnp.broadcast_to(full.astype(jnp.int32), (1, rows))]
    info_ref[...] = jnp.concatenate(info + [jnp.zeros((3, rows), jnp.int32)], axis=0)
    column = column_of(labels.astype(jnp.float32))
    packed = jnp.where(column_of(place.astype(jnp.float32)) == iota((1, LANES), 1).astype(jnp.float32), column, 0.0)
    packed = jnp.sum(packed, axis=0, keepdims=True).astype(jnp.int32)
    last = [packed % SECOND, (packed // SECOND) % LANES, packed // CHIP]
    last = [part.astype(jnp.float32) for part in last] + [jnp.broadcast_to(full, (1, feat - 3 * LANES))]
    last = jnp.concatenate(last, axis=1)
    moved = dot(hot(iota((MOVED, rows), 0) == place), x_ref[...])
    move_ref[...] = jnp.where(iota((MOVED, feat), 0) == MOVED - 1, last, moved).astype(jnp.bfloat16)


def pack_kernel(
    members, x_ref, info_ref, came_ref, start_ref, send_ref, slot_ref, came_slot_ref, own_start_ref, x, mine, sem
):
    rows, feat = x_ref.shape
    group_codes, codes_two = start_ref.shape[:2]
    offset = (lax.axis_index("mem") + members * group_codes - group_codes * lax.axis_index("grp")) % members
    fetch_start = pltpu.make_async_copy(start_ref.at[jnp.minimum(offset, group_codes - 1)], mine, sem.at[1])
    fetch = pltpu.make_async_copy(x_ref, x, sem.at[0])
    fetch.start()
    fetch_start.start()
    chips = send_ref.shape[0] // BLOCK
    run = feat // 2
    in_run = run // BLOCK
    chip, rank, labels = info_ref[0:1, :], info_ref[1:2, :], info_ref[3:4, :]
    full = info_ref[4:5, 0:1].astype(jnp.float32)
    kept = rank < KEEP
    slot = jnp.where(kept, chip * BLOCK + rank, -1)
    slot_ref[...] = slot
    kept_of = jnp.sum(hot((iota((chips, rows), 0) == chip) & kept).astype(jnp.float32), axis=1, keepdims=True)
    came = came_ref[...]
    came_last = came.astype(jnp.float32)[MOVED - 1 : MOVED]
    came_first = came_last[:, 0:LANES]
    came_chip = came_last[:, 2 * LANES : 3 * LANES]
    member = (iota((chips, LANES), 0).astype(jnp.float32) == came_chip) & (came_first > 0.5)
    after = jnp.sum(jnp.where(member, kept_of, 0.0), axis=0, keepdims=True) + rank_in_bin(member)
    fits = after < BLOCK - 1
    is_live = came_first > 0.5
    full = jnp.maximum(full, came_last[:, 3 * LANES : 3 * LANES + 1])
    full = jnp.maximum(full, highest(jnp.where(is_live & ~fits, 1.0, 0.0)))
    came_slot = jnp.where(is_live & fits, came_chip * BLOCK + after, -1.0)
    came_slot_ref[...] = jnp.broadcast_to(came_slot, (8, LANES)).astype(jnp.int32)
    came_labels = came_first + SECOND * came_last[:, LANES : 2 * LANES]
    label_column = jnp.concatenate(
        [column_of((labels % CHIP).astype(jnp.float32)), column_of(came_labels)[:MOVED]], axis=0
    )
    slot_column = jnp.concatenate([column_of(slot.astype(jnp.float32)), column_of(came_slot)[:MOVED]], axis=0)
    came_slot = came_slot.astype(jnp.int32)
    source, target = iota((run, run), 0).astype(jnp.float32), iota((run, run), 1).astype(jnp.float32)
    source = source - jnp.floor((source + 0.5) * (1.0 / BLOCK)) * BLOCK
    begin = ((lax.axis_index("mem") % in_run) * BLOCK).astype(jnp.float32)
    turn = hot(target == begin + source)
    block_of = jnp.floor((iota((in_run, run), 1).astype(jnp.float32) + 0.5) * (1.0 / BLOCK))
    in_block = block_of == iota((in_run, run), 0).astype(jnp.float32)
    lane = iota((1, LANES), 1).astype(jnp.float32)
    packed = []
    for at in range(0, chips * BLOCK, LANES):
        part = jnp.where(slot_column == lane + at, label_column, 0.0)
        packed.append(jnp.sum(part, axis=0, keepdims=True).astype(jnp.int32))
    packed = jnp.concatenate(packed, axis=1)
    labels = [(packed % SECOND).astype(jnp.float32), (packed // SECOND).astype(jnp.float32) + FULL * full]
    last = [
        jnp.where(in_block, part[:, at : at + run], 0.0)
        for part in labels
        for at in range(0, chips * BLOCK, run)
    ]
    last = dot(jnp.concatenate(last, axis=0).astype(jnp.bfloat16), turn)
    last = jnp.concatenate([last[:chips], last[chips:]], axis=1).astype(jnp.bfloat16)
    extra = jnp.concatenate([last, came], axis=0)
    lane_id = iota((1, LANES), 1)
    position = jnp.concatenate([came_slot[:, :MOVED], jnp.full((1, LANES - MOVED), -1, jnp.int32)], axis=1)
    position = jnp.where(lane_id < chips, lane_id * BLOCK + BLOCK - 1, pltpu.roll(position, chips, 1))
    position = position[:, : chips + MOVED]
    fetch_start.wait()
    own_start_ref[...] = jnp.zeros((SECTION, feat), jnp.bfloat16)
    own_start_ref[0:codes_two, :] = mine[...]
    fetch.wait()
    step = chips * BLOCK // 2
    for begin in range(0, chips * BLOCK, step):
        moved = dot(hot(iota((step, rows), 0) + begin == slot), x[...])
        moved = moved + dot(hot(iota((step, chips + MOVED), 0) + begin == position), extra)
        send_ref[begin : begin + step, :] = moved.astype(jnp.bfloat16)


def row_of(column):
    diagonal = iota((LANES, LANES), 0) == iota((LANES, LANES), 1)
    return jnp.sum(jnp.where(diagonal, column, 0.0), axis=0, keepdims=True)


def sums_kernel(got_ref, own_start_ref, part_ref, label_ref):
    total, feat = got_ref.shape
    run = feat // 2
    runs = []
    for begin in range(0, total, run):
        row = jnp.zeros((1, feat), jnp.float32)
        for at in range(begin, begin + run, BLOCK):
            row = row + got_ref[at + BLOCK - 8 : at + BLOCK, :].astype(jnp.float32)[7:8, :]
        runs.append(row)
    first = jnp.concatenate([row[:, :run] for row in runs], axis=1) - 1.0
    second = jnp.concatenate([row[:, run:] for row in runs], axis=1)
    full = jnp.where(jnp.max(second) >= FULL, 1.0, 0.0)
    second = jnp.where(second >= FULL, second - FULL, second)
    second = jnp.where(first >= LANES, second + LANES, second)
    second = jnp.where(first >= 0.0, second, -1.0)
    full_lanes = jnp.broadcast_to(full, (1, total))
    label_ref[...] = jnp.concatenate([first, second, full_lanes, jnp.zeros((5, total), jnp.float32)], axis=0)
    update_sums(got_ref, first, full, part_ref)
    part_ref[CORES * SECTION :, :] = own_start_ref[...]


def second_kernel(got_ref, label_ref, part_ref):
    update_sums(got_ref, label_ref[1:2, :], jnp.max(label_ref[2:3, :]), part_ref)


def update_sums(got_ref, assigned, full, part_ref):
    total, feat = got_ref.shape
    cluster = iota((CORES * LANES, total), 0).astype(jnp.float32)
    is_count = iota((SECTION, feat), 0) == SECTION - 1
    member = hot(cluster == assigned)
    totals = dot(member, got_ref[...])
    counts = jnp.sum(member.astype(jnp.float32), axis=1, keepdims=True)
    for core in range(CORES):
        begin, at = core * LANES, core * SECTION
        count = row_of(counts[begin : begin + LANES])
        large = jnp.floor(count * (1.0 / LANES))
        count = [large, count - large * LANES, jnp.full((1, feat - 2 * LANES), full, jnp.float32)]
        count = jnp.concatenate(count, axis=1)
        sums = jnp.where(is_count, count, totals[begin : begin + SECTION])
        part_ref[at : at + SECTION, :] = sums.astype(jnp.bfloat16)


def prepare_kernel(got_ref, label_ref, key_ref, squares_ref):
    total, feat = got_ref.shape
    diagonal = iota((LANES, LANES), 0) == iota((LANES, LANES), 1)
    ones = jnp.ones((LANES, LANES), jnp.bfloat16)
    for begin in range(0, total, STEP_SCORE):
        key = [
            jnp.where(diagonal, label_ref[0:1, at : at + LANES], 0.0)
            for at in range(begin, begin + STEP_SCORE, LANES)
        ]
        key = jnp.concatenate(key, axis=0).astype(jnp.bfloat16)
        key_ref[begin : begin + STEP_SCORE, :] = dot(key, ones)
        wide = got_ref[begin : begin + STEP_SCORE, :].astype(jnp.float32)
        squares = jnp.sum(wide * wide, axis=1, keepdims=True) * (1.0 / feat)
        squares_ref[begin : begin + STEP_SCORE, :] = jnp.broadcast_to(squares, (STEP_SCORE, LANES))


def score_kernel(
    codes_two,
    got_ref,
    own_first_ref,
    own_second_ref,
    other_first_ref,
    other_second_ref,
    key_ref,
    squares_ref,
    out_ref,
):
    total, feat = got_ref.shape
    my_core = lax.axis_index("grp") % CORES
    count_row = SECTION - 1

    own_refs, other_refs = (own_first_ref, own_second_ref), (other_first_ref, other_second_ref)

    def both(update, core):
        rows = slice(core * SECTION, (core + 1) * SECTION)
        own = own_refs[update][rows, :].astype(jnp.float32)
        return own + other_refs[update][rows, :].astype(jnp.float32)

    full = jnp.zeros((1, 1), jnp.float32)
    rounded, squares_of = [], []
    starts = [ref[CORES * SECTION :, :].astype(jnp.float32) for ref in (own_first_ref, other_first_ref)]
    for core in range(CORES):
        centre = jnp.where(my_core == core, starts[0], starts[1])
        for update in range(2):
            sums = both(update, core)
            counts = sums[count_row : count_row + 1]
            full = jnp.maximum(full, counts[:, 2 * LANES : 2 * LANES + 1])
            counts = column_of(counts[:, :LANES] * LANES + counts[:, LANES : 2 * LANES])
            centre = (sums + PRIOR * centre) * (1.0 / (counts[:SECTION] + PRIOR))
            narrow = jnp.concatenate(
                [centre.astype(jnp.bfloat16), jnp.zeros((LANES - SECTION, feat), jnp.bfloat16)], axis=0
            )
            wide = narrow.astype(jnp.float32)
            rounded.append(narrow)
            squares_of.append(row_of(jnp.sum(wide * wide, axis=1, keepdims=True)) * (1.0 / feat))
    full = jnp.max(full)
    table = jnp.concatenate(rounded, axis=0)
    lane = iota((STEP_SCORE, LANES), 1)
    is_score = lane < codes_two
    lane_value = lane.astype(jnp.float32)
    ones = jnp.ones((LANES, LANES), jnp.bfloat16)
    spread = iota((2 * LANES, LANES), 0) // LANES
    spread = hot(iota((2 * LANES, LANES), 1) == codes_two + 1 + spread)
    excess_all = jnp.zeros((STEP_SCORE, LANES), jnp.float32)
    excess_block = []

    def across(values):
        return dot(values.astype(jnp.bfloat16), ones)

    for begin in range(0, total, STEP_SCORE):
        x = got_ref[begin : begin + STEP_SCORE, :]
        inner = dot_nt(x, table)
        key = key_ref[begin : begin + STEP_SCORE, :]
        is_other = key >= LANES
        first = jnp.where(is_other, key - LANES, key)
        squares = squares_ref[begin : begin + STEP_SCORE, :]

        def distance(update):
            low, high = [
                squares_of[at] - (2.0 / feat) * inner[:, at * LANES : (at + 1) * LANES]
                for at in (update, 2 + update)
            ]
            return squares + jnp.where(is_other, high, low)

        near = jnp.where(lane_value == first, distance(0), 0.0)
        near_high = near.astype(jnp.bfloat16)
        near_low = (near - near_high.astype(jnp.float32)).astype(jnp.bfloat16)
        score = jnp.where(is_score, distance(1), 0.0)
        mean = (across(score) * (1.0 / codes_two)).astype(jnp.bfloat16).astype(jnp.float32)
        rest = jnp.where(is_score, score - mean, 0.0)
        record = rest.astype(jnp.bfloat16).astype(jnp.float32)
        lost = rest - record
        is_live = key >= 0.0
        lost = jnp.where(is_live, lost * lost, 0.0)
        sent = jnp.where(is_live, score * score, 0.0)
        excess_all = excess_all + (lost - (ROUNDING_ALL * ROUNDING_ALL) * sent)
        excess = lost - (ROUNDING_BLOCK * ROUNDING_BLOCK) * sent
        excess = jnp.sum(excess.reshape(STEP_SCORE // BLOCK, BLOCK // 8, 8, LANES), axis=1)
        excess_block.append(excess.reshape(STEP_SCORE // BLOCK * 8, LANES))
        near = dot(jnp.concatenate([near_high, near_low], axis=1), spread)
        record = jnp.where(lane == codes_two, mean, record + near)
        out_ref[begin : begin + STEP_SCORE, :] = record.astype(jnp.bfloat16)
    excess = across(jnp.concatenate(excess_block, axis=0))
    excess = jnp.sum(excess.reshape(total // BLOCK, 8, LANES), axis=1)
    full = jnp.maximum(full, jnp.where(jnp.max(excess) > 0.0, 1.0, 0.0))
    full = jnp.maximum(full, jnp.where(jnp.sum(excess_all) > 0.0, 1.0, 0.0))
    for begin in range(0, total, STEP_SCORE):
        record = out_ref[begin : begin + STEP_SCORE, :].astype(jnp.float32)
        record = jnp.where(lane == LANES - 1, full, record)
        out_ref[begin : begin + STEP_SCORE, :] = record.astype(jnp.bfloat16)


def return_kernel(got_ref, came_slot_ref, out_ref):
    total = got_ref.shape[0]
    got = got_ref[...]
    full = highest(jnp.where(iota((total, LANES), 1) == LANES - 1, got.astype(jnp.float32), 0.0))
    slot = column_of(came_slot_ref[0:1, :].astype(jnp.float32))[:MOVED]
    moved = dot(hot(iota((MOVED, total), 1).astype(jnp.float32) == slot), got)
    out_ref[...] = jnp.where(iota((MOVED, LANES), 1) == LANES - 1, full, moved).astype(jnp.bfloat16)


def gather_kernel(got_ref, slot_ref, out_ref):
    total = got_ref.shape[0]
    rows = slot_ref.shape[1]
    out_ref[...] = dot(got_ref[...].T, hot(iota((total, rows), 0) == slot_ref[...]))


def unpack_kernel(gathered_ref, own_ref, back_ref, info_ref, all_ref, one_ref, full_ref):
    rows = info_ref.shape[1]
    codes_two = all_ref.shape[0]
    back = back_ref[...].astype(jnp.float32)
    full = jnp.maximum(own_ref[...].astype(jnp.float32), back)
    full_ref[0, 0] = jnp.max(full[:, LANES - 1 :])
    moved = dot(back.T.astype(jnp.bfloat16), hot(iota((MOVED, rows), 0) == info_ref[2:3, :]))
    moved = gathered_ref[...] + moved
    mean = moved[codes_two : codes_two + 1]
    near = moved[codes_two + 1 : codes_two + 2] + moved[codes_two + 2 : codes_two + 3]
    all_ref[...] = moved[:codes_two] + mean
    one_ref[...] = near


def over_members(totals, counts):
    members = lax.axis_size("mem")
    clusters, feat = totals.shape
    share = -(-clusters // members)

    def swap(blocks):
        return lax.all_to_all(blocks, "mem", split_axis=0, concat_axis=0, tiled=True)

    padded = jnp.pad(totals.astype(jnp.bfloat16), ((0, members * share - clusters), (0, 0)))
    own = jnp.sum(swap(padded.reshape(members, share, feat)).astype(jnp.float32), axis=0)
    own = jnp.broadcast_to(own.astype(jnp.bfloat16)[None], (members, share, feat))
    summed = swap(own).reshape(members * share, feat)[:clusters].astype(jnp.float32)
    counted = jnp.sum(swap(jnp.broadcast_to(counts[None], (members, clusters))), axis=0)
    return summed, counted


def pick_block(total):
    for candidate in range(1024, 0, -1):
        if total % candidate == 0:
            return candidate
    return total


def general(embeddings, initial_centroids, row_owner, prefix_offset, first_assign, second_assign):
    row_count, feat_width = embeddings.shape
    group_codes = initial_centroids.shape[0]
    codes_two = initial_centroids.shape[1]
    clusters = group_codes * codes_two
    group_count = lax.axis_size("grp")
    member_count = lax.axis_size("mem")
    devices_all = group_count * member_count
    capacity = 2 * row_count // devices_all + 4
    slot_total = devices_all * capacity
    target = row_owner[:, 0]
    dest_table = (target[:, None] == jnp.arange(devices_all, dtype=jnp.int32)[None, :]).astype(
        jnp.int32
    )
    slot_rank = jnp.sum(jnp.cumsum(dest_table, axis=0) * dest_table, axis=1) - 1
    slot_index = target * capacity + slot_rank
    send_rows = jnp.zeros((slot_total, feat_width), jnp.bfloat16).at[slot_index].set(embeddings)
    labels = jnp.stack([prefix_offset, first_assign, second_assign], axis=1)
    send_labels = jnp.full((slot_total, 3), -1, jnp.int32).at[slot_index].set(labels)
    got_rows, got_labels = (
        lax.all_to_all(send_rows, ("grp", "mem"), split_axis=0, concat_axis=0, tiled=True),
        lax.all_to_all(send_labels, ("grp", "mem"), split_axis=0, concat_axis=0, tiled=True),
    )
    offsets = got_labels[:, 0]
    live = offsets >= 0
    ids_one = jnp.where(live, offsets * codes_two + got_labels[:, 1], -1)
    ids_two = jnp.where(live, offsets * codes_two + got_labels[:, 2], -1)
    squares = jnp.sum(jnp.square(got_rows.astype(jnp.float32)), axis=1)
    block_rows = pick_block(slot_total)
    block_count = slot_total // block_rows
    row_blocks = got_rows.reshape(block_count, block_rows, feat_width)
    cluster_range = jnp.arange(clusters, dtype=jnp.int32)

    def local_totals(cluster_ids):

        def add_block(carry, pieces):
            totals, counts = carry
            block_x, block_ids = pieces
            hot_table = (block_ids[:, None] == cluster_range[None, :]).astype(jnp.bfloat16)
            totals = totals + lax.dot_general(
                hot_table, block_x, (((0,), (0,)), ((), ())), preferred_element_type=jnp.float32
            )
            counts = counts + jnp.sum(hot_table, axis=0, dtype=jnp.float32)
            return ((totals, counts), None)

        start = (
            jnp.zeros((clusters, feat_width), jnp.float32),
            jnp.zeros((clusters,), jnp.float32),
        )
        result, unused = lax.scan(
            add_block, start, (row_blocks, cluster_ids.reshape(block_count, block_rows))
        )
        return result

    start_table = initial_centroids.reshape(clusters, feat_width).astype(jnp.float32)

    def update(earlier, cluster_ids):
        totals, counts = local_totals(cluster_ids)
        totals, counts = over_members(totals, counts)
        centre = (totals + PRIOR * earlier) / (counts[:, None] + PRIOR)
        return (centre, centre.astype(jnp.bfloat16))

    centre_one, rounded_one = update(start_table, ids_one)
    assigned = jnp.take(rounded_one, jnp.maximum(ids_one, 0), axis=0).astype(jnp.float32)
    first_local = (
        squares
        - 2.0 * jnp.sum(got_rows.astype(jnp.float32) * assigned, axis=1)
        + jnp.sum(assigned * assigned, axis=1)
    ) / feat_width
    centre_two, rounded_two = update(centre_one, ids_two)
    centre_squares = jnp.sum(jnp.square(rounded_two.astype(jnp.float32)), axis=1).reshape(
        group_codes, codes_two
    )
    code_range = jnp.arange(group_codes, dtype=jnp.int32)

    def score_block(pieces):
        block_x, block_offsets, block_sq = pieces
        raw = lax.dot_general(
            rounded_two, block_x, (((1,), (1,)), ((), ())), preferred_element_type=jnp.float32
        )
        raw = raw.reshape(group_codes, codes_two, block_rows)
        select = (block_offsets[None, :] == code_range[:, None]).astype(jnp.float32)
        inner = jnp.sum(raw * select[:, None, :], axis=0)
        norms = jnp.sum(centre_squares[:, :, None] * select[:, None, :], axis=0)
        return (block_sq[None, :] - 2.0 * inner + norms) / feat_width

    scored = lax.map(
        score_block,
        (
            row_blocks,
            offsets.reshape(block_count, block_rows),
            squares.reshape(block_count, block_rows),
        ),
    )
    all_local = jnp.transpose(scored, (1, 0, 2)).reshape(codes_two, slot_total)
    one_local = first_local[None, :]
    back_all, back_one = (
        lax.all_to_all(all_local, ("grp", "mem"), split_axis=1, concat_axis=1, tiled=True),
        lax.all_to_all(one_local, ("grp", "mem"), split_axis=1, concat_axis=1, tiled=True),
    )
    distances = jnp.take(back_all, slot_index, axis=1)
    first_distance = jnp.take(back_one[0], slot_index, axis=0)
    return (distances, first_distance)


def quick(embeddings, initial_centroids, row_owner, prefix_offset, first_assign, second_assign):
    rows, feat = embeddings.shape
    group_codes, codes_two = initial_centroids.shape[:2]
    groups = lax.axis_size("grp")
    members = lax.axis_size("mem")
    chips = groups // CORES * members
    total = chips * BLOCK
    shape = jax.ShapeDtypeStruct
    vmem = pl.BlockSpec(memory_space=pltpu.VMEM)
    same_core = [
        [group * members + member for group in range(core, groups, CORES) for member in range(members)]
        for core in range(CORES)
    ]

    def swap(array):
        blocks = array.reshape(chips, array.shape[0] // chips, array.shape[1])
        blocks = lax.all_to_all(
            blocks, ("grp", "mem"), split_axis=0, concat_axis=0, axis_index_groups=same_core, tiled=True
        )
        return blocks.reshape(array.shape)

    def other_core(array):
        return lax.ppermute(array, "grp", [(group, group ^ 1) for group in range(groups)])

    move, info = call(
        lambda *refs: split_kernel(members, group_codes, *refs),
        [shape((MOVED, feat), jnp.bfloat16), shape((8, rows), jnp.int32)],
        [
            row_owner.reshape(1, rows),
            prefix_offset.reshape(1, rows),
            first_assign.reshape(1, rows),
            second_assign.reshape(1, rows),
            embeddings,
        ],
    )
    any_memory = pl.BlockSpec(memory_space=pl.ANY)
    send, slot, came_slot, own_start = call(
        lambda *refs: pack_kernel(members, *refs),
        [
            shape((total, feat), jnp.bfloat16),
            shape((1, rows), jnp.int32),
            shape((8, LANES), jnp.int32),
            shape((SECTION, feat), jnp.bfloat16),
        ],
        [embeddings, info, other_core(move), initial_centroids],
        in_memory=[any_memory, vmem, vmem, any_memory],
        scratch=[
            pltpu.VMEM((rows, feat), jnp.bfloat16),
            pltpu.VMEM((codes_two, feat), jnp.bfloat16),
            pltpu.SemaphoreType.DMA((2,)),
        ],
    )
    got = swap(send)
    part = shape((CORES * SECTION, feat), jnp.bfloat16)
    with_start = shape(((CORES + 1) * SECTION, feat), jnp.bfloat16)
    first_part, label = call(sums_kernel, [with_start, shape((8, total), jnp.float32)], [got, own_start])
    other_first = other_core(first_part)
    (second_part,) = call(second_kernel, [part], [got, label])
    other_second = other_core(second_part)
    key, squares = call(
        prepare_kernel,
        [shape((total, LANES), jnp.float32)] * 2,
        [got, label],
    )
    (record,) = call(
        lambda *refs: score_kernel(codes_two, *refs),
        [shape((total, LANES), jnp.bfloat16)],
        [got, first_part, second_part, other_first, other_second, key, squares],
    )
    back = swap(record)
    (came_back,) = call(return_kernel, [shape((MOVED, LANES), jnp.bfloat16)], [back, came_slot])
    other_back = other_core(came_back)
    (gathered,) = call(gather_kernel, [shape((LANES, rows), jnp.float32)], [back, slot])
    return call(
        unpack_kernel,
        [shape((codes_two, rows), jnp.float32), shape((1, rows), jnp.float32), shape((1, 1), jnp.float32)],
        [gathered, came_back, other_back, info],
        out_memory=[vmem, vmem, pl.BlockSpec(memory_space=pltpu.SMEM)],
    )


def body(*inputs):
    distances, first_distance, full = quick(*inputs)
    return lax.cond(
        full[0, 0] > 0.5,
        lambda kept, given: general(*given),
        lambda kept, given: kept,
        (distances, first_distance[0]),
        inputs,
    )


def solution(mesh):
    placed = (
        P(("grp", "mem"), None),
        P("grp", None, None),
        P(("grp", "mem"), None),
        P(("grp", "mem")),
        P(("grp", "mem")),
        P(("grp", "mem")),
    )
    return jax.shard_map(
        body,
        mesh=mesh,
        in_specs=placed,
        out_specs=(P(None, ("grp", "mem")), P(("grp", "mem"))),
        check_vma=False,
    )
```

```python
import jax
import jax.numpy as jnp
from jax import lax
from jax.experimental import pallas as pl
from jax.experimental.pallas import tpu as pltpu
from jax.sharding import PartitionSpec as P

PRIOR = 16
BLOCK = 24
KEEP = 22
MOVED = 16
LANES = 128
CORES = 2
SECTION = 112
SECOND, CHIP = 256, 256 * 128
FULL = 128
STEP_SCORE = 384
ROUNDING_BLOCK = 4.5e-4
ROUNDING_ALL = 2.5e-4
NT = (((1,), (1,)), ((), ()))
VMEM_LIMIT = 48 * 1024 * 1024


def iota(shape, dim):
    return lax.broadcasted_iota(jnp.int32, shape, dim)


def hot(condition):
    return jnp.where(condition, 1.0, 0.0).astype(jnp.bfloat16)


def dot(a, b):
    return jnp.dot(a, b, preferred_element_type=jnp.float32)


def dot_nt(a, b):
    return lax.dot_general(a, b, NT, preferred_element_type=jnp.float32)


def three_terms(values):
    high = values.astype(jnp.bfloat16)
    rest = values - high.astype(jnp.float32)
    middle = rest.astype(jnp.bfloat16)
    low = (rest - middle.astype(jnp.float32)).astype(jnp.bfloat16)
    return high, middle, low


def call(kernel, out_shape, args, out_memory=None, in_memory=None, scratch=()):
    vmem = pl.BlockSpec(memory_space=pltpu.VMEM)
    return pl.pallas_call(
        kernel,
        out_shape=out_shape,
        in_specs=in_memory or [vmem] * len(args),
        out_specs=out_memory or [vmem] * len(out_shape),
        scratch_shapes=scratch,
        compiler_params=pltpu.CompilerParams(vmem_limit_bytes=VMEM_LIMIT),
    )(*args)


def rank_in_bin(member):
    bins = hot(member)
    before = hot(iota((LANES, LANES), 0) < iota((LANES, LANES), 1))
    base = jnp.zeros((member.shape[0], 1), jnp.float32)
    ranks = []
    for begin in range(0, member.shape[1], LANES):
        piece = bins[:, begin : begin + LANES]
        ranks.append(dot(piece, before) + base)
        base = base + jnp.sum(piece.astype(jnp.float32), axis=1, keepdims=True)
    rank = jnp.concatenate(ranks, axis=1)
    return jnp.sum(jnp.where(member, rank, 0.0), axis=0, keepdims=True)


def column_of(row):
    diagonal = iota((LANES, LANES), 0) == iota((LANES, LANES), 1)
    pieces = []
    for begin in range(0, row.shape[1], LANES):
        piece = jnp.where(diagonal, row[:, begin : begin + LANES], 0.0)
        pieces.append(jnp.sum(piece, axis=1, keepdims=True))
    return jnp.concatenate(pieces, axis=0)


def highest(values):
    return jnp.max(values, axis=(0, 1), keepdims=True)


def split_kernel(
    members, group_codes, owner_ref, offset_ref, first_ref, second_ref, x_ref, move_ref, info_ref
):
    rows, feat = x_ref.shape
    chips = lax.axis_size("grp") // CORES * members
    group = owner_ref[...] // members
    code = group * group_codes + offset_ref[...]
    chip = (group // CORES) * members + code % members
    rank = rank_in_bin(iota((chips, rows), 0) == chip).astype(jnp.int32)
    moves = rank >= KEEP
    place = rank_in_bin((iota((16, rows), 0) == 0) & moves).astype(jnp.int32)
    fits = place < MOVED - 1
    full = highest(jnp.where(moves & ~fits, 1.0, 0.0))
    place = jnp.where(moves & fits, place, -1)
    labels = first_ref[...] + 1 + LANES * (group % CORES) + SECOND * second_ref[...] + CHIP * chip
    info = [chip, rank, place, labels, jnp.broadcast_to(full.astype(jnp.int32), (1, rows))]
    info_ref[...] = jnp.concatenate(info + [jnp.zeros((3, rows), jnp.int32)], axis=0)
    column = column_of(labels.astype(jnp.float32))
    packed = jnp.where(column_of(place.astype(jnp.float32)) == iota((1, LANES), 1).astype(jnp.float32), column, 0.0)
    packed = jnp.sum(packed, axis=0, keepdims=True).astype(jnp.int32)
    last = [packed % SECOND, (packed // SECOND) % LANES, packed // CHIP]
    last = [part.astype(jnp.float32) for part in last] + [jnp.broadcast_to(full, (1, feat - 3 * LANES))]
    last = jnp.concatenate(last, axis=1)
    moved = dot(hot(iota((MOVED, rows), 0) == place), x_ref[...])
    move_ref[...] = jnp.where(iota((MOVED, feat), 0) == MOVED - 1, last, moved).astype(jnp.bfloat16)


def label_kernel(info_ref, out_ref):
    chip, rank, labels = info_ref[0:1, :], info_ref[1:2, :], info_ref[3:4, :]
    slot = jnp.where(rank < KEEP, chip * BLOCK + rank, -1)
    slot_column = column_of(slot.astype(jnp.float32))
    label_column = column_of((labels % CHIP).astype(jnp.float32))
    lane = iota((1, LANES), 1).astype(jnp.float32)
    for at in range(0, out_ref.shape[1], LANES):
        part = jnp.where(slot_column == lane + at, label_column, 0.0)
        part = jnp.sum(part, axis=0, keepdims=True)
        out_ref[:, at : at + LANES] = jnp.broadcast_to(part, (8, LANES))


def pack_kernel(
    members, x_ref, info_ref, label_ref, came_ref, start_ref, send_ref, slot_ref, came_slot_ref, own_start_ref, x, mine, sem
):
    rows, feat = x_ref.shape
    group_codes, codes_two = start_ref.shape[:2]
    offset = (lax.axis_index("mem") + members * group_codes - group_codes * lax.axis_index("grp")) % members
    fetch_start = pltpu.make_async_copy(start_ref.at[jnp.minimum(offset, group_codes - 1)], mine, sem.at[1])
    fetch = pltpu.make_async_copy(x_ref, x, sem.at[0])
    fetch.start()
    fetch_start.start()
    chips = send_ref.shape[0] // BLOCK
    run = feat // 2
    in_run = run // BLOCK
    chip, rank, labels = info_ref[0:1, :], info_ref[1:2, :], info_ref[3:4, :]
    full = info_ref[4:5, 0:1].astype(jnp.float32)
    kept = rank < KEEP
    slot = jnp.where(kept, chip * BLOCK + rank, -1)
    slot_ref[...] = slot
    kept_of = jnp.sum(hot((iota((chips, rows), 0) == chip) & kept).astype(jnp.float32), axis=1, keepdims=True)
    came = came_ref[...]
    came_last = came.astype(jnp.float32)[MOVED - 1 : MOVED]
    came_first = came_last[:, 0:LANES]
    came_chip = came_last[:, 2 * LANES : 3 * LANES]
    member = (iota((chips, LANES), 0).astype(jnp.float32) == came_chip) & (came_first > 0.5)
    after = jnp.sum(jnp.where(member, kept_of, 0.0), axis=0, keepdims=True) + rank_in_bin(member)
    fits = after < BLOCK - 1
    is_live = came_first > 0.5
    full = jnp.maximum(full, came_last[:, 3 * LANES : 3 * LANES + 1])
    full = jnp.maximum(full, highest(jnp.where(is_live & ~fits, 1.0, 0.0)))
    came_slot = jnp.where(is_live & fits, came_chip * BLOCK + after, -1.0)
    came_slot_ref[...] = jnp.broadcast_to(came_slot, (8, LANES)).astype(jnp.int32)
    came_labels = came_first + SECOND * came_last[:, LANES : 2 * LANES]
    label_column = column_of(came_labels)[:MOVED]
    slot_column = column_of(came_slot)[:MOVED]
    came_slot = came_slot.astype(jnp.int32)
    source, target = iota((run, run), 0).astype(jnp.float32), iota((run, run), 1).astype(jnp.float32)
    source = source - jnp.floor((source + 0.5) * (1.0 / BLOCK)) * BLOCK
    begin = ((lax.axis_index("mem") % in_run) * BLOCK).astype(jnp.float32)
    turn = hot(target == begin + source)
    block_of = jnp.floor((iota((in_run, run), 1).astype(jnp.float32) + 0.5) * (1.0 / BLOCK))
    in_block = block_of == iota((in_run, run), 0).astype(jnp.float32)
    lane = iota((1, LANES), 1).astype(jnp.float32)
    packed = []
    for at in range(0, chips * BLOCK, LANES):
        part = jnp.where(slot_column == lane + at, label_column, 0.0)
        part = jnp.sum(part, axis=0, keepdims=True) + label_ref[0:1, at : at + LANES]
        packed.append(part.astype(jnp.int32))
    packed = jnp.concatenate(packed, axis=1)
    labels = [(packed % SECOND).astype(jnp.float32), (packed // SECOND).astype(jnp.float32) + FULL * full]
    last = [
        jnp.where(in_block, part[:, at : at + run], 0.0)
        for part in labels
        for at in range(0, chips * BLOCK, run)
    ]
    last = dot(jnp.concatenate(last, axis=0).astype(jnp.bfloat16), turn)
    last = jnp.concatenate([last[:chips], last[chips:]], axis=1).astype(jnp.bfloat16)
    extra = jnp.concatenate([last, came], axis=0)
    lane_id = iota((1, LANES), 1)
    position = jnp.concatenate([came_slot[:, :MOVED], jnp.full((1, LANES - MOVED), -1, jnp.int32)], axis=1)
    position = jnp.where(lane_id < chips, lane_id * BLOCK + BLOCK - 1, pltpu.roll(position, chips, 1))
    position = position[:, : chips + MOVED]
    fetch_start.wait()
    own_start_ref[...] = jnp.zeros((SECTION, feat), jnp.bfloat16)
    own_start_ref[0:codes_two, :] = mine[...]
    fetch.wait()
    step = chips * BLOCK // 2
    for begin in range(0, chips * BLOCK, step):
        moved = dot(hot(iota((step, rows), 0) + begin == slot), x[...])
        moved = moved + dot(hot(iota((step, chips + MOVED), 0) + begin == position), extra)
        send_ref[begin : begin + step, :] = moved.astype(jnp.bfloat16)


def row_of(column):
    diagonal = iota((LANES, LANES), 0) == iota((LANES, LANES), 1)
    return jnp.sum(jnp.where(diagonal, column, 0.0), axis=0, keepdims=True)


def sums_kernel(got_ref, part_ref, label_ref):
    total, feat = got_ref.shape
    run = feat // 2
    runs = []
    for begin in range(0, total, run):
        row = jnp.zeros((1, feat), jnp.float32)
        for at in range(begin, begin + run, BLOCK):
            row = row + got_ref[at + BLOCK - 8 : at + BLOCK, :].astype(jnp.float32)[7:8, :]
        runs.append(row)
    first = jnp.concatenate([row[:, :run] for row in runs], axis=1) - 1.0
    second = jnp.concatenate([row[:, run:] for row in runs], axis=1)
    full = jnp.where(jnp.max(second) >= FULL, 1.0, 0.0)
    second = jnp.where(second >= FULL, second - FULL, second)
    second = jnp.where(first >= LANES, second + LANES, second)
    second = jnp.where(first >= 0.0, second, -1.0)
    label_ref[...] = jnp.broadcast_to(first, (8, total))
    x = got_ref[...]
    cluster = iota((CORES * LANES, total), 0).astype(jnp.float32)
    is_count = iota((SECTION, feat), 0) == SECTION - 1
    member = hot(jnp.concatenate([cluster == first, cluster == second], axis=0))
    totals = dot(member, x)
    counts = jnp.sum(member.astype(jnp.float32), axis=1, keepdims=True)
    for section in range(2 * CORES):
        begin, at = section * LANES, section * SECTION
        count = row_of(counts[begin : begin + LANES])
        large = jnp.floor(count * (1.0 / LANES))
        count = [large, count - large * LANES, jnp.full((1, feat - 2 * LANES), full, jnp.float32)]
        count = jnp.concatenate(count, axis=1)
        sums = jnp.where(is_count, count, totals[begin : begin + SECTION])
        part_ref[at : at + SECTION, :] = sums.astype(jnp.bfloat16)


def prepare_kernel(got_ref, label_ref, key_ref, squares_ref):
    total, feat = got_ref.shape
    diagonal = iota((LANES, LANES), 0) == iota((LANES, LANES), 1)
    ones = jnp.ones((LANES, LANES), jnp.bfloat16)
    for begin in range(0, total, STEP_SCORE):
        key = [
            jnp.where(diagonal, label_ref[0:1, at : at + LANES], 0.0)
            for at in range(begin, begin + STEP_SCORE, LANES)
        ]
        key = jnp.concatenate(key, axis=0).astype(jnp.bfloat16)
        key_ref[begin : begin + STEP_SCORE, :] = dot(key, ones)
        wide = got_ref[begin : begin + STEP_SCORE, :].astype(jnp.float32)
        squares = jnp.sum(wide * wide, axis=1, keepdims=True) * (1.0 / feat)
        squares_ref[begin : begin + STEP_SCORE, :] = jnp.broadcast_to(squares, (STEP_SCORE, LANES))


def score_kernel(
    codes_two, got_ref, own_ref, other_ref, own_start_ref, other_start_ref, key_ref, squares_ref, out_ref
):
    total, feat = got_ref.shape
    my_core = lax.axis_index("grp") % CORES
    count_row = SECTION - 1

    def both(at):
        own = own_ref[at : at + SECTION, :].astype(jnp.float32)
        return own + other_ref[at : at + SECTION, :].astype(jnp.float32)

    full = jnp.zeros((1, 1), jnp.float32)
    rounded, squares_of = [], []
    starts = [ref[...].astype(jnp.float32) for ref in (own_start_ref, other_start_ref)]
    for core in range(CORES):
        centre = jnp.where(my_core == core, starts[0], starts[1])
        for update in range(2):
            sums = both((update * CORES + core) * SECTION)
            counts = sums[count_row : count_row + 1]
            full = jnp.maximum(full, counts[:, 2 * LANES : 2 * LANES + 1])
            counts = column_of(counts[:, :LANES] * LANES + counts[:, LANES : 2 * LANES])
            centre = (sums + PRIOR * centre) * (1.0 / (counts[:SECTION] + PRIOR))
            narrow = jnp.concatenate(
                [centre.astype(jnp.bfloat16), jnp.zeros((LANES - SECTION, feat), jnp.bfloat16)], axis=0
            )
            wide = narrow.astype(jnp.float32)
            rounded.append(narrow)
            squares_of.append(row_of(jnp.sum(wide * wide, axis=1, keepdims=True)) * (1.0 / feat))
    full = jnp.max(full)
    table = jnp.concatenate(rounded, axis=0)
    lane = iota((STEP_SCORE, LANES), 1)
    is_score = lane < codes_two
    lane_value = lane.astype(jnp.float32)
    ones = jnp.ones((LANES, LANES), jnp.bfloat16)
    spread = iota((2 * LANES, LANES), 0) // LANES
    spread = hot(iota((2 * LANES, LANES), 1) == codes_two + 1 + spread)
    excess_all = jnp.zeros((STEP_SCORE, LANES), jnp.float32)
    excess_block = []

    def across(values):
        return dot(values.astype(jnp.bfloat16), ones)

    for begin in range(0, total, STEP_SCORE):
        x = got_ref[begin : begin + STEP_SCORE, :]
        inner = dot_nt(x, table)
        key = key_ref[begin : begin + STEP_SCORE, :]
        is_other = key >= LANES
        first = jnp.where(is_other, key - LANES, key)
        squares = squares_ref[begin : begin + STEP_SCORE, :]

        def distance(update):
            low, high = [
                squares_of[at] - (2.0 / feat) * inner[:, at * LANES : (at + 1) * LANES]
                for at in (update, 2 + update)
            ]
            return squares + jnp.where(is_other, high, low)

        near = jnp.where(lane_value == first, distance(0), 0.0)
        near_high = near.astype(jnp.bfloat16)
        near_low = (near - near_high.astype(jnp.float32)).astype(jnp.bfloat16)
        score = jnp.where(is_score, distance(1), 0.0)
        mean = (across(score) * (1.0 / codes_two)).astype(jnp.bfloat16).astype(jnp.float32)
        rest = jnp.where(is_score, score - mean, 0.0)
        record = rest.astype(jnp.bfloat16).astype(jnp.float32)
        lost = rest - record
        is_live = key >= 0.0
        lost = jnp.where(is_live, lost * lost, 0.0)
        sent = jnp.where(is_live, score * score, 0.0)
        excess_all = excess_all + (lost - (ROUNDING_ALL * ROUNDING_ALL) * sent)
        excess = lost - (ROUNDING_BLOCK * ROUNDING_BLOCK) * sent
        excess = jnp.sum(excess.reshape(STEP_SCORE // BLOCK, BLOCK // 8, 8, LANES), axis=1)
        excess_block.append(excess.reshape(STEP_SCORE // BLOCK * 8, LANES))
        near = dot(jnp.concatenate([near_high, near_low], axis=1), spread)
        record = jnp.where(lane == codes_two, mean, record + near)
        out_ref[begin : begin + STEP_SCORE, :] = record.astype(jnp.bfloat16)
    excess = across(jnp.concatenate(excess_block, axis=0))
    excess = jnp.sum(excess.reshape(total // BLOCK, 8, LANES), axis=1)
    full = jnp.maximum(full, jnp.where(jnp.max(excess) > 0.0, 1.0, 0.0))
    full = jnp.maximum(full, jnp.where(jnp.sum(excess_all) > 0.0, 1.0, 0.0))
    for begin in range(0, total, STEP_SCORE):
        record = out_ref[begin : begin + STEP_SCORE, :].astype(jnp.float32)
        record = jnp.where(lane == LANES - 1, full, record)
        out_ref[begin : begin + STEP_SCORE, :] = record.astype(jnp.bfloat16)


def return_kernel(got_ref, came_slot_ref, out_ref):
    total = got_ref.shape[0]
    got = got_ref[...]
    full = highest(jnp.where(iota((total, LANES), 1) == LANES - 1, got.astype(jnp.float32), 0.0))
    slot = column_of(came_slot_ref[0:1, :].astype(jnp.float32))[:MOVED]
    moved = dot(hot(iota((MOVED, total), 1).astype(jnp.float32) == slot), got)
    out_ref[...] = jnp.where(iota((MOVED, LANES), 1) == LANES - 1, full, moved).astype(jnp.bfloat16)


def gather_kernel(got_ref, slot_ref, out_ref):
    total = got_ref.shape[0]
    rows = slot_ref.shape[1]
    out_ref[...] = dot(got_ref[...].T, hot(iota((total, rows), 0) == slot_ref[...]))


def unpack_kernel(gathered_ref, own_ref, back_ref, info_ref, all_ref, one_ref, full_ref):
    rows = info_ref.shape[1]
    codes_two = all_ref.shape[0]
    back = back_ref[...].astype(jnp.float32)
    full = jnp.maximum(own_ref[...].astype(jnp.float32), back)
    full_ref[0, 0] = jnp.max(full[:, LANES - 1 :])
    moved = dot(back.T.astype(jnp.bfloat16), hot(iota((MOVED, rows), 0) == info_ref[2:3, :]))
    moved = gathered_ref[...] + moved
    mean = moved[codes_two : codes_two + 1]
    near = moved[codes_two + 1 : codes_two + 2] + moved[codes_two + 2 : codes_two + 3]
    all_ref[...] = moved[:codes_two] + mean
    one_ref[...] = near


def over_members(totals, counts):
    members = lax.axis_size("mem")
    clusters, feat = totals.shape
    share = -(-clusters // members)

    def swap(blocks):
        return lax.all_to_all(blocks, "mem", split_axis=0, concat_axis=0, tiled=True)

    padded = jnp.pad(totals.astype(jnp.bfloat16), ((0, members * share - clusters), (0, 0)))
    own = jnp.sum(swap(padded.reshape(members, share, feat)).astype(jnp.float32), axis=0)
    own = jnp.broadcast_to(own.astype(jnp.bfloat16)[None], (members, share, feat))
    summed = swap(own).reshape(members * share, feat)[:clusters].astype(jnp.float32)
    counted = jnp.sum(swap(jnp.broadcast_to(counts[None], (members, clusters))), axis=0)
    return summed, counted


def pick_block(total):
    for candidate in range(1024, 0, -1):
        if total % candidate == 0:
            return candidate
    return total


def general(embeddings, initial_centroids, row_owner, prefix_offset, first_assign, second_assign):
    row_count, feat_width = embeddings.shape
    group_codes = initial_centroids.shape[0]
    codes_two = initial_centroids.shape[1]
    clusters = group_codes * codes_two
    group_count = lax.axis_size("grp")
    member_count = lax.axis_size("mem")
    devices_all = group_count * member_count
    capacity = 2 * row_count // devices_all + 4
    slot_total = devices_all * capacity
    target = row_owner[:, 0]
    dest_table = (target[:, None] == jnp.arange(devices_all, dtype=jnp.int32)[None, :]).astype(
        jnp.int32
    )
    slot_rank = jnp.sum(jnp.cumsum(dest_table, axis=0) * dest_table, axis=1) - 1
    slot_index = target * capacity + slot_rank
    send_rows = jnp.zeros((slot_total, feat_width), jnp.bfloat16).at[slot_index].set(embeddings)
    labels = jnp.stack([prefix_offset, first_assign, second_assign], axis=1)
    send_labels = jnp.full((slot_total, 3), -1, jnp.int32).at[slot_index].set(labels)
    got_rows, got_labels = (
        lax.all_to_all(send_rows, ("grp", "mem"), split_axis=0, concat_axis=0, tiled=True),
        lax.all_to_all(send_labels, ("grp", "mem"), split_axis=0, concat_axis=0, tiled=True),
    )
    offsets = got_labels[:, 0]
    live = offsets >= 0
    ids_one = jnp.where(live, offsets * codes_two + got_labels[:, 1], -1)
    ids_two = jnp.where(live, offsets * codes_two + got_labels[:, 2], -1)
    squares = jnp.sum(jnp.square(got_rows.astype(jnp.float32)), axis=1)
    block_rows = pick_block(slot_total)
    block_count = slot_total // block_rows
    row_blocks = got_rows.reshape(block_count, block_rows, feat_width)
    cluster_range = jnp.arange(clusters, dtype=jnp.int32)

    def local_totals(cluster_ids):

        def add_block(carry, pieces):
            totals, counts = carry
            block_x, block_ids = pieces
            hot_table = (block_ids[:, None] == cluster_range[None, :]).astype(jnp.bfloat16)
            totals = totals + lax.dot_general(
                hot_table, block_x, (((0,), (0,)), ((), ())), preferred_element_type=jnp.float32
            )
            counts = counts + jnp.sum(hot_table, axis=0, dtype=jnp.float32)
            return ((totals, counts), None)

        start = (
            jnp.zeros((clusters, feat_width), jnp.float32),
            jnp.zeros((clusters,), jnp.float32),
        )
        result, unused = lax.scan(
            add_block, start, (row_blocks, cluster_ids.reshape(block_count, block_rows))
        )
        return result

    start_table = initial_centroids.reshape(clusters, feat_width).astype(jnp.float32)

    def update(earlier, cluster_ids):
        totals, counts = local_totals(cluster_ids)
        totals, counts = over_members(totals, counts)
        centre = (totals + PRIOR * earlier) / (counts[:, None] + PRIOR)
        return (centre, centre.astype(jnp.bfloat16))

    centre_one, rounded_one = update(start_table, ids_one)
    assigned = jnp.take(rounded_one, jnp.maximum(ids_one, 0), axis=0).astype(jnp.float32)
    first_local = (
        squares
        - 2.0 * jnp.sum(got_rows.astype(jnp.float32) * assigned, axis=1)
        + jnp.sum(assigned * assigned, axis=1)
    ) / feat_width
    centre_two, rounded_two = update(centre_one, ids_two)
    centre_squares = jnp.sum(jnp.square(rounded_two.astype(jnp.float32)), axis=1).reshape(
        group_codes, codes_two
    )
    code_range = jnp.arange(group_codes, dtype=jnp.int32)

    def score_block(pieces):
        block_x, block_offsets, block_sq = pieces
        raw = lax.dot_general(
            rounded_two, block_x, (((1,), (1,)), ((), ())), preferred_element_type=jnp.float32
        )
        raw = raw.reshape(group_codes, codes_two, block_rows)
        select = (block_offsets[None, :] == code_range[:, None]).astype(jnp.float32)
        inner = jnp.sum(raw * select[:, None, :], axis=0)
        norms = jnp.sum(centre_squares[:, :, None] * select[:, None, :], axis=0)
        return (block_sq[None, :] - 2.0 * inner + norms) / feat_width

    scored = lax.map(
        score_block,
        (
            row_blocks,
            offsets.reshape(block_count, block_rows),
            squares.reshape(block_count, block_rows),
        ),
    )
    all_local = jnp.transpose(scored, (1, 0, 2)).reshape(codes_two, slot_total)
    one_local = first_local[None, :]
    back_all, back_one = (
        lax.all_to_all(all_local, ("grp", "mem"), split_axis=1, concat_axis=1, tiled=True),
        lax.all_to_all(one_local, ("grp", "mem"), split_axis=1, concat_axis=1, tiled=True),
    )
    distances = jnp.take(back_all, slot_index, axis=1)
    first_distance = jnp.take(back_one[0], slot_index, axis=0)
    return (distances, first_distance)


def quick(embeddings, initial_centroids, row_owner, prefix_offset, first_assign, second_assign):
    rows, feat = embeddings.shape
    group_codes, codes_two = initial_centroids.shape[:2]
    groups = lax.axis_size("grp")
    members = lax.axis_size("mem")
    chips = groups // CORES * members
    total = chips * BLOCK
    shape = jax.ShapeDtypeStruct
    vmem = pl.BlockSpec(memory_space=pltpu.VMEM)
    same_core = [
        [group * members + member for group in range(core, groups, CORES) for member in range(members)]
        for core in range(CORES)
    ]

    def swap(array):
        blocks = array.reshape(chips, array.shape[0] // chips, array.shape[1])
        blocks = lax.all_to_all(
            blocks, ("grp", "mem"), split_axis=0, concat_axis=0, axis_index_groups=same_core, tiled=True
        )
        return blocks.reshape(array.shape)

    def other_core(array):
        return lax.ppermute(array, "grp", [(group, group ^ 1) for group in range(groups)])

    move, info = call(
        lambda *refs: split_kernel(members, group_codes, *refs),
        [shape((MOVED, feat), jnp.bfloat16), shape((8, rows), jnp.int32)],
        [
            row_owner.reshape(1, rows),
            prefix_offset.reshape(1, rows),
            first_assign.reshape(1, rows),
            second_assign.reshape(1, rows),
            embeddings,
        ],
    )
    came = other_core(move)
    (own_labels,) = call(label_kernel, [shape((8, total), jnp.float32)], [info])
    any_memory = pl.BlockSpec(memory_space=pl.ANY)
    send, slot, came_slot, own_start = call(
        lambda *refs: pack_kernel(members, *refs),
        [
            shape((total, feat), jnp.bfloat16),
            shape((1, rows), jnp.int32),
            shape((8, LANES), jnp.int32),
            shape((SECTION, feat), jnp.bfloat16),
        ],
        [embeddings, info, own_labels, came, initial_centroids],
        in_memory=[any_memory, vmem, vmem, vmem, any_memory],
        scratch=[
            pltpu.VMEM((rows, feat), jnp.bfloat16),
            pltpu.VMEM((codes_two, feat), jnp.bfloat16),
            pltpu.SemaphoreType.DMA((2,)),
        ],
    )
    other_start = other_core(own_start)
    got = swap(send)
    part, label = call(
        sums_kernel,
        [shape((2 * CORES * SECTION, feat), jnp.bfloat16), shape((8, total), jnp.float32)],
        [got],
    )
    other_part = other_core(part)
    key, squares = call(
        prepare_kernel,
        [shape((total, LANES), jnp.float32)] * 2,
        [got, label],
    )
    (record,) = call(
        lambda *refs: score_kernel(codes_two, *refs),
        [shape((total, LANES), jnp.bfloat16)],
        [got, part, other_part, own_start, other_start, key, squares],
    )
    back = swap(record)
    (came_back,) = call(return_kernel, [shape((MOVED, LANES), jnp.bfloat16)], [back, came_slot])
    other_back = other_core(came_back)
    (gathered,) = call(gather_kernel, [shape((LANES, rows), jnp.float32)], [back, slot])
    return call(
        unpack_kernel,
        [shape((codes_two, rows), jnp.float32), shape((1, rows), jnp.float32), shape((1, 1), jnp.float32)],
        [gathered, came_back, other_back, info],
        out_memory=[vmem, vmem, pl.BlockSpec(memory_space=pltpu.SMEM)],
    )


def body(*inputs):
    distances, first_distance, full = quick(*inputs)
    return lax.cond(
        full[0, 0] > 0.5,
        lambda kept, given: general(*given),
        lambda kept, given: kept,
        (distances, first_distance[0]),
        inputs,
    )


def solution(mesh):
    placed = (
        P(("grp", "mem"), None),
        P("grp", None, None),
        P(("grp", "mem"), None),
        P(("grp", "mem")),
        P(("grp", "mem")),
        P(("grp", "mem")),
    )
    return jax.shard_map(
        body,
        mesh=mesh,
        in_specs=placed,
        out_specs=(P(None, ("grp", "mem")), P(("grp", "mem"))),
        check_vma=False,
    )
```

```python
import jax
import jax.numpy as jnp
from jax import lax
from jax.experimental import pallas as pl
from jax.experimental.pallas import tpu as pltpu
from jax.sharding import PartitionSpec as P

PRIOR = 16
BLOCK = 24
KEEP = 22
MOVED = 16
LANES = 128
CORES = 2
SECTION = 112
SECOND, CHIP = 256, 256 * 128
FULL = 128
STEP_SCORE = 384
ROUNDING_BLOCK = 4.5e-4
ROUNDING_ALL = 2.5e-4
NT = (((1,), (1,)), ((), ()))
VMEM_LIMIT = 48 * 1024 * 1024


def iota(shape, dim):
    return lax.broadcasted_iota(jnp.int32, shape, dim)


def hot(condition):
    return jnp.where(condition, 1.0, 0.0).astype(jnp.bfloat16)


def dot(a, b):
    return jnp.dot(a, b, preferred_element_type=jnp.float32)


def dot_nt(a, b):
    return lax.dot_general(a, b, NT, preferred_element_type=jnp.float32)


def three_terms(values):
    high = values.astype(jnp.bfloat16)
    rest = values - high.astype(jnp.float32)
    middle = rest.astype(jnp.bfloat16)
    low = (rest - middle.astype(jnp.float32)).astype(jnp.bfloat16)
    return high, middle, low


def call(kernel, out_shape, args, out_memory=None, in_memory=None, scratch=()):
    vmem = pl.BlockSpec(memory_space=pltpu.VMEM)
    return pl.pallas_call(
        kernel,
        out_shape=out_shape,
        in_specs=in_memory or [vmem] * len(args),
        out_specs=out_memory or [vmem] * len(out_shape),
        scratch_shapes=scratch,
        compiler_params=pltpu.CompilerParams(vmem_limit_bytes=VMEM_LIMIT),
    )(*args)


def rank_in_bin(member):
    bins = hot(member)
    before = hot(iota((LANES, LANES), 0) < iota((LANES, LANES), 1))
    base = jnp.zeros((member.shape[0], 1), jnp.float32)
    ranks = []
    for begin in range(0, member.shape[1], LANES):
        piece = bins[:, begin : begin + LANES]
        ranks.append(dot(piece, before) + base)
        base = base + jnp.sum(piece.astype(jnp.float32), axis=1, keepdims=True)
    rank = jnp.concatenate(ranks, axis=1)
    return jnp.sum(jnp.where(member, rank, 0.0), axis=0, keepdims=True)


def column_of(row):
    diagonal = iota((LANES, LANES), 0) == iota((LANES, LANES), 1)
    pieces = []
    for begin in range(0, row.shape[1], LANES):
        piece = jnp.where(diagonal, row[:, begin : begin + LANES], 0.0)
        pieces.append(jnp.sum(piece, axis=1, keepdims=True))
    return jnp.concatenate(pieces, axis=0)


def highest(values):
    return jnp.max(values, axis=(0, 1), keepdims=True)


def split_kernel(
    members, group_codes, owner_ref, offset_ref, first_ref, second_ref, x_ref, move_ref, info_ref
):
    rows, feat = x_ref.shape
    chips = lax.axis_size("grp") // CORES * members
    group = owner_ref[...] // members
    code = group * group_codes + offset_ref[...]
    chip = (group // CORES) * members + code % members
    rank = rank_in_bin(iota((chips, rows), 0) == chip).astype(jnp.int32)
    moves = rank >= KEEP
    place = rank_in_bin((iota((16, rows), 0) == 0) & moves).astype(jnp.int32)
    fits = place < MOVED - 1
    full = highest(jnp.where(moves & ~fits, 1.0, 0.0))
    place = jnp.where(moves & fits, place, -1)
    labels = first_ref[...] + 1 + LANES * (group % CORES) + SECOND * second_ref[...] + CHIP * chip
    info = [chip, rank, place, labels, jnp.broadcast_to(full.astype(jnp.int32), (1, rows))]
    info_ref[...] = jnp.concatenate(info + [jnp.zeros((3, rows), jnp.int32)], axis=0)
    column = column_of(labels.astype(jnp.float32))
    packed = jnp.where(column_of(place.astype(jnp.float32)) == iota((1, LANES), 1).astype(jnp.float32), column, 0.0)
    packed = jnp.sum(packed, axis=0, keepdims=True).astype(jnp.int32)
    last = [packed % SECOND, (packed // SECOND) % LANES, packed // CHIP]
    last = [part.astype(jnp.float32) for part in last] + [jnp.broadcast_to(full, (1, feat - 3 * LANES))]
    last = jnp.concatenate(last, axis=1)
    moved = dot(hot(iota((MOVED, rows), 0) == place), x_ref[...])
    move_ref[...] = jnp.where(iota((MOVED, feat), 0) == MOVED - 1, last, moved).astype(jnp.bfloat16)


def pack_kernel(
    members, x_ref, info_ref, came_ref, start_ref, send_ref, slot_ref, came_slot_ref, own_start_ref, x, mine, sem
):
    rows, feat = x_ref.shape
    group_codes, codes_two = start_ref.shape[:2]
    offset = (lax.axis_index("mem") + members * group_codes - group_codes * lax.axis_index("grp")) % members
    fetch_start = pltpu.make_async_copy(start_ref.at[jnp.minimum(offset, group_codes - 1)], mine, sem.at[1])
    fetch = pltpu.make_async_copy(x_ref, x, sem.at[0])
    fetch.start()
    fetch_start.start()
    chips = send_ref.shape[0] // BLOCK
    run = feat // 2
    in_run = run // BLOCK
    chip, rank, labels = info_ref[0:1, :], info_ref[1:2, :], info_ref[3:4, :]
    full = info_ref[4:5, 0:1].astype(jnp.float32)
    kept = rank < KEEP
    slot = jnp.where(kept, chip * BLOCK + rank, -1)
    slot_ref[...] = slot
    kept_of = jnp.sum(hot((iota((chips, rows), 0) == chip) & kept).astype(jnp.float32), axis=1, keepdims=True)
    came = came_ref[...]
    came_last = came.astype(jnp.float32)[MOVED - 1 : MOVED]
    came_first = came_last[:, 0:LANES]
    came_chip = came_last[:, 2 * LANES : 3 * LANES]
    member = (iota((chips, LANES), 0).astype(jnp.float32) == came_chip) & (came_first > 0.5)
    after = jnp.sum(jnp.where(member, kept_of, 0.0), axis=0, keepdims=True) + rank_in_bin(member)
    fits = after < BLOCK - 1
    is_live = came_first > 0.5
    full = jnp.maximum(full, came_last[:, 3 * LANES : 3 * LANES + 1])
    full = jnp.maximum(full, highest(jnp.where(is_live & ~fits, 1.0, 0.0)))
    came_slot = jnp.where(is_live & fits, came_chip * BLOCK + after, -1.0)
    came_slot_ref[...] = jnp.broadcast_to(came_slot, (8, LANES)).astype(jnp.int32)
    came_labels = came_first + SECOND * came_last[:, LANES : 2 * LANES]
    label_column = jnp.concatenate(
        [column_of((labels % CHIP).astype(jnp.float32)), column_of(came_labels)[:MOVED]], axis=0
    )
    slot_column = jnp.concatenate([column_of(slot.astype(jnp.float32)), column_of(came_slot)[:MOVED]], axis=0)
    came_slot = came_slot.astype(jnp.int32)
    source, target = iota((run, run), 0).astype(jnp.float32), iota((run, run), 1).astype(jnp.float32)
    source = source - jnp.floor((source + 0.5) * (1.0 / BLOCK)) * BLOCK
    begin = ((lax.axis_index("mem") % in_run) * BLOCK).astype(jnp.float32)
    turn = hot(target == begin + source)
    block_of = jnp.floor((iota((in_run, run), 1).astype(jnp.float32) + 0.5) * (1.0 / BLOCK))
    in_block = block_of == iota((in_run, run), 0).astype(jnp.float32)
    lane = iota((1, LANES), 1).astype(jnp.float32)
    packed = []
    for at in range(0, chips * BLOCK, LANES):
        part = jnp.where(slot_column == lane + at, label_column, 0.0)
        packed.append(jnp.sum(part, axis=0, keepdims=True).astype(jnp.int32))
    packed = jnp.concatenate(packed, axis=1)
    labels = [(packed % SECOND).astype(jnp.float32), (packed // SECOND).astype(jnp.float32) + FULL * full]
    last = [
        jnp.where(in_block, part[:, at : at + run], 0.0)
        for part in labels
        for at in range(0, chips * BLOCK, run)
    ]
    last = dot(jnp.concatenate(last, axis=0).astype(jnp.bfloat16), turn)
    last = jnp.concatenate([last[:chips], last[chips:]], axis=1).astype(jnp.bfloat16)
    extra = jnp.concatenate([last, came], axis=0)
    lane_id = iota((1, LANES), 1)
    position = jnp.concatenate([came_slot[:, :MOVED], jnp.full((1, LANES - MOVED), -1, jnp.int32)], axis=1)
    position = jnp.where(lane_id < chips, lane_id * BLOCK + BLOCK - 1, pltpu.roll(position, chips, 1))
    position = position[:, : chips + MOVED]
    fetch_start.wait()
    own_start_ref[...] = jnp.zeros((SECTION, feat), jnp.bfloat16)
    own_start_ref[0:codes_two, :] = mine[...]
    fetch.wait()
    step = chips * BLOCK
    for begin in range(0, chips * BLOCK, step):
        moved = dot(hot(iota((step, rows), 0) + begin == slot), x[...])
        moved = moved + dot(hot(iota((step, chips + MOVED), 0) + begin == position), extra)
        send_ref[begin : begin + step, :] = moved.astype(jnp.bfloat16)


def row_of(column):
    diagonal = iota((LANES, LANES), 0) == iota((LANES, LANES), 1)
    return jnp.sum(jnp.where(diagonal, column, 0.0), axis=0, keepdims=True)


def sums_kernel(got_ref, part_ref, label_ref):
    total, feat = got_ref.shape
    run = feat // 2
    runs = []
    for begin in range(0, total, run):
        row = jnp.zeros((1, feat), jnp.float32)
        for at in range(begin, begin + run, BLOCK):
            row = row + got_ref[at + BLOCK - 8 : at + BLOCK, :].astype(jnp.float32)[7:8, :]
        runs.append(row)
    first = jnp.concatenate([row[:, :run] for row in runs], axis=1) - 1.0
    second = jnp.concatenate([row[:, run:] for row in runs], axis=1)
    full = jnp.where(jnp.max(second) >= FULL, 1.0, 0.0)
    second = jnp.where(second >= FULL, second - FULL, second)
    second = jnp.where(first >= LANES, second + LANES, second)
    second = jnp.where(first >= 0.0, second, -1.0)
    label_ref[...] = jnp.broadcast_to(first, (8, total))
    x = got_ref[...]
    cluster = iota((CORES * LANES, total), 0).astype(jnp.float32)
    is_count = iota((SECTION, feat), 0) == SECTION - 1
    member = hot(jnp.concatenate([cluster == first, cluster == second], axis=0))
    totals = dot(member, x)
    counts = jnp.sum(member.astype(jnp.float32), axis=1, keepdims=True)
    for section in range(2 * CORES):
        begin, at = section * LANES, section * SECTION
        count = row_of(counts[begin : begin + LANES])
        large = jnp.floor(count * (1.0 / LANES))
        count = [large, count - large * LANES, jnp.full((1, feat - 2 * LANES), full, jnp.float32)]
        count = jnp.concatenate(count, axis=1)
        sums = jnp.where(is_count, count, totals[begin : begin + SECTION])
        part_ref[at : at + SECTION, :] = sums.astype(jnp.bfloat16)


def prepare_kernel(got_ref, label_ref, key_ref, squares_ref):
    total, feat = got_ref.shape
    diagonal = iota((LANES, LANES), 0) == iota((LANES, LANES), 1)
    ones = jnp.ones((LANES, LANES), jnp.bfloat16)
    for begin in range(0, total, STEP_SCORE):
        key = [
            jnp.where(diagonal, label_ref[0:1, at : at + LANES], 0.0)
            for at in range(begin, begin + STEP_SCORE, LANES)
        ]
        key = jnp.concatenate(key, axis=0).astype(jnp.bfloat16)
        key_ref[begin : begin + STEP_SCORE, :] = dot(key, ones)
        wide = got_ref[begin : begin + STEP_SCORE, :].astype(jnp.float32)
        squares = jnp.sum(wide * wide, axis=1, keepdims=True) * (1.0 / feat)
        squares_ref[begin : begin + STEP_SCORE, :] = jnp.broadcast_to(squares, (STEP_SCORE, LANES))


def score_kernel(
    codes_two, got_ref, own_ref, other_ref, own_start_ref, other_start_ref, key_ref, squares_ref, out_ref
):
    total, feat = got_ref.shape
    my_core = lax.axis_index("grp") % CORES
    count_row = SECTION - 1

    def both(at):
        own = own_ref[at : at + SECTION, :].astype(jnp.float32)
        return own + other_ref[at : at + SECTION, :].astype(jnp.float32)

    full = jnp.zeros((1, 1), jnp.float32)
    rounded, squares_of = [], []
    starts = [ref[...].astype(jnp.float32) for ref in (own_start_ref, other_start_ref)]
    for core in range(CORES):
        centre = jnp.where(my_core == core, starts[0], starts[1])
        for update in range(2):
            sums = both((update * CORES + core) * SECTION)
            counts = sums[count_row : count_row + 1]
            full = jnp.maximum(full, counts[:, 2 * LANES : 2 * LANES + 1])
            counts = column_of(counts[:, :LANES] * LANES + counts[:, LANES : 2 * LANES])
            centre = (sums + PRIOR * centre) * (1.0 / (counts[:SECTION] + PRIOR))
            narrow = jnp.concatenate(
                [centre.astype(jnp.bfloat16), jnp.zeros((LANES - SECTION, feat), jnp.bfloat16)], axis=0
            )
            wide = narrow.astype(jnp.float32)
            rounded.append(narrow)
            squares_of.append(row_of(jnp.sum(wide * wide, axis=1, keepdims=True)) * (1.0 / feat))
    full = jnp.max(full)
    table = jnp.concatenate(rounded, axis=0)
    lane = iota((STEP_SCORE, LANES), 1)
    is_score = lane < codes_two
    lane_value = lane.astype(jnp.float32)
    ones = jnp.ones((LANES, LANES), jnp.bfloat16)
    spread = iota((2 * LANES, LANES), 0) // LANES
    spread = hot(iota((2 * LANES, LANES), 1) == codes_two + 1 + spread)
    excess_all = jnp.zeros((STEP_SCORE, LANES), jnp.float32)
    excess_block = []

    def across(values):
        return dot(values.astype(jnp.bfloat16), ones)

    for begin in range(0, total, STEP_SCORE):
        x = got_ref[begin : begin + STEP_SCORE, :]
        inner = dot_nt(x, table)
        key = key_ref[begin : begin + STEP_SCORE, :]
        is_other = key >= LANES
        first = jnp.where(is_other, key - LANES, key)
        squares = squares_ref[begin : begin + STEP_SCORE, :]

        def distance(update):
            low, high = [
                squares_of[at] - (2.0 / feat) * inner[:, at * LANES : (at + 1) * LANES]
                for at in (update, 2 + update)
            ]
            return squares + jnp.where(is_other, high, low)

        near = jnp.where(lane_value == first, distance(0), 0.0)
        near_high = near.astype(jnp.bfloat16)
        near_low = (near - near_high.astype(jnp.float32)).astype(jnp.bfloat16)
        score = jnp.where(is_score, distance(1), 0.0)
        mean = (across(score) * (1.0 / codes_two)).astype(jnp.bfloat16).astype(jnp.float32)
        rest = jnp.where(is_score, score - mean, 0.0)
        record = rest.astype(jnp.bfloat16).astype(jnp.float32)
        lost = rest - record
        is_live = key >= 0.0
        lost = jnp.where(is_live, lost * lost, 0.0)
        sent = jnp.where(is_live, score * score, 0.0)
        excess_all = excess_all + (lost - (ROUNDING_ALL * ROUNDING_ALL) * sent)
        excess = lost - (ROUNDING_BLOCK * ROUNDING_BLOCK) * sent
        excess = jnp.sum(excess.reshape(STEP_SCORE // BLOCK, BLOCK // 8, 8, LANES), axis=1)
        excess_block.append(excess.reshape(STEP_SCORE // BLOCK * 8, LANES))
        near = dot(jnp.concatenate([near_high, near_low], axis=1), spread)
        record = jnp.where(lane == codes_two, mean, record + near)
        out_ref[begin : begin + STEP_SCORE, :] = record.astype(jnp.bfloat16)
    excess = across(jnp.concatenate(excess_block, axis=0))
    excess = jnp.sum(excess.reshape(total // BLOCK, 8, LANES), axis=1)
    full = jnp.maximum(full, jnp.where(jnp.max(excess) > 0.0, 1.0, 0.0))
    full = jnp.maximum(full, jnp.where(jnp.sum(excess_all) > 0.0, 1.0, 0.0))
    for begin in range(0, total, STEP_SCORE):
        record = out_ref[begin : begin + STEP_SCORE, :].astype(jnp.float32)
        record = jnp.where(lane == LANES - 1, full, record)
        out_ref[begin : begin + STEP_SCORE, :] = record.astype(jnp.bfloat16)


def return_kernel(got_ref, came_slot_ref, out_ref):
    total = got_ref.shape[0]
    got = got_ref[...]
    full = highest(jnp.where(iota((total, LANES), 1) == LANES - 1, got.astype(jnp.float32), 0.0))
    slot = column_of(came_slot_ref[0:1, :].astype(jnp.float32))[:MOVED]
    moved = dot(hot(iota((MOVED, total), 1).astype(jnp.float32) == slot), got)
    out_ref[...] = jnp.where(iota((MOVED, LANES), 1) == LANES - 1, full, moved).astype(jnp.bfloat16)


def gather_kernel(got_ref, slot_ref, out_ref):
    total = got_ref.shape[0]
    rows = slot_ref.shape[1]
    out_ref[...] = dot(got_ref[...].T, hot(iota((total, rows), 0) == slot_ref[...]))


def unpack_kernel(gathered_ref, own_ref, back_ref, info_ref, all_ref, one_ref, full_ref):
    rows = info_ref.shape[1]
    codes_two = all_ref.shape[0]
    back = back_ref[...].astype(jnp.float32)
    full = jnp.maximum(own_ref[...].astype(jnp.float32), back)
    full_ref[0, 0] = jnp.max(full[:, LANES - 1 :])
    moved = dot(back.T.astype(jnp.bfloat16), hot(iota((MOVED, rows), 0) == info_ref[2:3, :]))
    moved = gathered_ref[...] + moved
    mean = moved[codes_two : codes_two + 1]
    near = moved[codes_two + 1 : codes_two + 2] + moved[codes_two + 2 : codes_two + 3]
    all_ref[...] = moved[:codes_two] + mean
    one_ref[...] = near


def over_members(totals, counts):
    members = lax.axis_size("mem")
    clusters, feat = totals.shape
    share = -(-clusters // members)

    def swap(blocks):
        return lax.all_to_all(blocks, "mem", split_axis=0, concat_axis=0, tiled=True)

    padded = jnp.pad(totals.astype(jnp.bfloat16), ((0, members * share - clusters), (0, 0)))
    own = jnp.sum(swap(padded.reshape(members, share, feat)).astype(jnp.float32), axis=0)
    own = jnp.broadcast_to(own.astype(jnp.bfloat16)[None], (members, share, feat))
    summed = swap(own).reshape(members * share, feat)[:clusters].astype(jnp.float32)
    counted = jnp.sum(swap(jnp.broadcast_to(counts[None], (members, clusters))), axis=0)
    return summed, counted


def pick_block(total):
    for candidate in range(1024, 0, -1):
        if total % candidate == 0:
            return candidate
    return total


def general(embeddings, initial_centroids, row_owner, prefix_offset, first_assign, second_assign):
    row_count, feat_width = embeddings.shape
    group_codes = initial_centroids.shape[0]
    codes_two = initial_centroids.shape[1]
    clusters = group_codes * codes_two
    group_count = lax.axis_size("grp")
    member_count = lax.axis_size("mem")
    devices_all = group_count * member_count
    capacity = 2 * row_count // devices_all + 4
    slot_total = devices_all * capacity
    target = row_owner[:, 0]
    dest_table = (target[:, None] == jnp.arange(devices_all, dtype=jnp.int32)[None, :]).astype(
        jnp.int32
    )
    slot_rank = jnp.sum(jnp.cumsum(dest_table, axis=0) * dest_table, axis=1) - 1
    slot_index = target * capacity + slot_rank
    send_rows = jnp.zeros((slot_total, feat_width), jnp.bfloat16).at[slot_index].set(embeddings)
    labels = jnp.stack([prefix_offset, first_assign, second_assign], axis=1)
    send_labels = jnp.full((slot_total, 3), -1, jnp.int32).at[slot_index].set(labels)
    got_rows, got_labels = (
        lax.all_to_all(send_rows, ("grp", "mem"), split_axis=0, concat_axis=0, tiled=True),
        lax.all_to_all(send_labels, ("grp", "mem"), split_axis=0, concat_axis=0, tiled=True),
    )
    offsets = got_labels[:, 0]
    live = offsets >= 0
    ids_one = jnp.where(live, offsets * codes_two + got_labels[:, 1], -1)
    ids_two = jnp.where(live, offsets * codes_two + got_labels[:, 2], -1)
    squares = jnp.sum(jnp.square(got_rows.astype(jnp.float32)), axis=1)
    block_rows = pick_block(slot_total)
    block_count = slot_total // block_rows
    row_blocks = got_rows.reshape(block_count, block_rows, feat_width)
    cluster_range = jnp.arange(clusters, dtype=jnp.int32)

    def local_totals(cluster_ids):

        def add_block(carry, pieces):
            totals, counts = carry
            block_x, block_ids = pieces
            hot_table = (block_ids[:, None] == cluster_range[None, :]).astype(jnp.bfloat16)
            totals = totals + lax.dot_general(
                hot_table, block_x, (((0,), (0,)), ((), ())), preferred_element_type=jnp.float32
            )
            counts = counts + jnp.sum(hot_table, axis=0, dtype=jnp.float32)
            return ((totals, counts), None)

        start = (
            jnp.zeros((clusters, feat_width), jnp.float32),
            jnp.zeros((clusters,), jnp.float32),
        )
        result, unused = lax.scan(
            add_block, start, (row_blocks, cluster_ids.reshape(block_count, block_rows))
        )
        return result

    start_table = initial_centroids.reshape(clusters, feat_width).astype(jnp.float32)

    def update(earlier, cluster_ids):
        totals, counts = local_totals(cluster_ids)
        totals, counts = over_members(totals, counts)
        centre = (totals + PRIOR * earlier) / (counts[:, None] + PRIOR)
        return (centre, centre.astype(jnp.bfloat16))

    centre_one, rounded_one = update(start_table, ids_one)
    assigned = jnp.take(rounded_one, jnp.maximum(ids_one, 0), axis=0).astype(jnp.float32)
    first_local = (
        squares
        - 2.0 * jnp.sum(got_rows.astype(jnp.float32) * assigned, axis=1)
        + jnp.sum(assigned * assigned, axis=1)
    ) / feat_width
    centre_two, rounded_two = update(centre_one, ids_two)
    centre_squares = jnp.sum(jnp.square(rounded_two.astype(jnp.float32)), axis=1).reshape(
        group_codes, codes_two
    )
    code_range = jnp.arange(group_codes, dtype=jnp.int32)

    def score_block(pieces):
        block_x, block_offsets, block_sq = pieces
        raw = lax.dot_general(
            rounded_two, block_x, (((1,), (1,)), ((), ())), preferred_element_type=jnp.float32
        )
        raw = raw.reshape(group_codes, codes_two, block_rows)
        select = (block_offsets[None, :] == code_range[:, None]).astype(jnp.float32)
        inner = jnp.sum(raw * select[:, None, :], axis=0)
        norms = jnp.sum(centre_squares[:, :, None] * select[:, None, :], axis=0)
        return (block_sq[None, :] - 2.0 * inner + norms) / feat_width

    scored = lax.map(
        score_block,
        (
            row_blocks,
            offsets.reshape(block_count, block_rows),
            squares.reshape(block_count, block_rows),
        ),
    )
    all_local = jnp.transpose(scored, (1, 0, 2)).reshape(codes_two, slot_total)
    one_local = first_local[None, :]
    back_all, back_one = (
        lax.all_to_all(all_local, ("grp", "mem"), split_axis=1, concat_axis=1, tiled=True),
        lax.all_to_all(one_local, ("grp", "mem"), split_axis=1, concat_axis=1, tiled=True),
    )
    distances = jnp.take(back_all, slot_index, axis=1)
    first_distance = jnp.take(back_one[0], slot_index, axis=0)
    return (distances, first_distance)


def quick(embeddings, initial_centroids, row_owner, prefix_offset, first_assign, second_assign):
    rows, feat = embeddings.shape
    group_codes, codes_two = initial_centroids.shape[:2]
    groups = lax.axis_size("grp")
    members = lax.axis_size("mem")
    chips = groups // CORES * members
    total = chips * BLOCK
    shape = jax.ShapeDtypeStruct
    vmem = pl.BlockSpec(memory_space=pltpu.VMEM)
    same_core = [
        [group * members + member for group in range(core, groups, CORES) for member in range(members)]
        for core in range(CORES)
    ]

    def swap(array):
        blocks = array.reshape(chips, array.shape[0] // chips, array.shape[1])
        blocks = lax.all_to_all(
            blocks, ("grp", "mem"), split_axis=0, concat_axis=0, axis_index_groups=same_core, tiled=True
        )
        return blocks.reshape(array.shape)

    def other_core(array):
        return lax.ppermute(array, "grp", [(group, group ^ 1) for group in range(groups)])

    move, info = call(
        lambda *refs: split_kernel(members, group_codes, *refs),
        [shape((MOVED, feat), jnp.bfloat16), shape((8, rows), jnp.int32)],
        [
            row_owner.reshape(1, rows),
            prefix_offset.reshape(1, rows),
            first_assign.reshape(1, rows),
            second_assign.reshape(1, rows),
            embeddings,
        ],
    )
    any_memory = pl.BlockSpec(memory_space=pl.ANY)
    send, slot, came_slot, own_start = call(
        lambda *refs: pack_kernel(members, *refs),
        [
            shape((total, feat), jnp.bfloat16),
            shape((1, rows), jnp.int32),
            shape((8, LANES), jnp.int32),
            shape((SECTION, feat), jnp.bfloat16),
        ],
        [embeddings, info, other_core(move), initial_centroids],
        in_memory=[any_memory, vmem, vmem, any_memory],
        scratch=[
            pltpu.VMEM((rows, feat), jnp.bfloat16),
            pltpu.VMEM((codes_two, feat), jnp.bfloat16),
            pltpu.SemaphoreType.DMA((2,)),
        ],
    )
    other_start = other_core(own_start)
    got = swap(send)
    part, label = call(
        sums_kernel,
        [shape((2 * CORES * SECTION, feat), jnp.bfloat16), shape((8, total), jnp.float32)],
        [got],
    )
    other_part = other_core(part)
    key, squares = call(
        prepare_kernel,
        [shape((total, LANES), jnp.float32)] * 2,
        [got, label],
    )
    (record,) = call(
        lambda *refs: score_kernel(codes_two, *refs),
        [shape((total, LANES), jnp.bfloat16)],
        [got, part, other_part, own_start, other_start, key, squares],
    )
    back = swap(record)
    (came_back,) = call(return_kernel, [shape((MOVED, LANES), jnp.bfloat16)], [back, came_slot])
    other_back = other_core(came_back)
    (gathered,) = call(gather_kernel, [shape((LANES, rows), jnp.float32)], [back, slot])
    return call(
        unpack_kernel,
        [shape((codes_two, rows), jnp.float32), shape((1, rows), jnp.float32), shape((1, 1), jnp.float32)],
        [gathered, came_back, other_back, info],
        out_memory=[vmem, vmem, pl.BlockSpec(memory_space=pltpu.SMEM)],
    )


def body(*inputs):
    distances, first_distance, full = quick(*inputs)
    return lax.cond(
        full[0, 0] > 0.5,
        lambda kept, given: general(*given),
        lambda kept, given: kept,
        (distances, first_distance[0]),
        inputs,
    )


def solution(mesh):
    placed = (
        P(("grp", "mem"), None),
        P("grp", None, None),
        P(("grp", "mem"), None),
        P(("grp", "mem")),
        P(("grp", "mem")),
        P(("grp", "mem")),
    )
    return jax.shard_map(
        body,
        mesh=mesh,
        in_specs=placed,
        out_specs=(P(None, ("grp", "mem")), P(("grp", "mem"))),
        check_vma=False,
    )
```
